256 devices in a mesh: dp: 4 (over x), seq: 64 (over y, z, core).
Axes of the slice: x: 4, y: 4, z: 8, core: 2. Of those that a mesh axis runs over, the one named last changes fastest.
Arguments:
- queries: bfloat16 [4, 64, 192, 1536], P('dp', 'seq'), may hold values from -100 to 100
- key_field: bfloat16 [4, 64, 192, 1536], P('dp', 'seq'), may hold values from -7 to 7
- value_field: bfloat16 [4, 64, 192, 1536], P('dp', 'seq'), may hold values from -6 to 6
- out_grad: bfloat16 [4, 64, 192, 1536], P('dp', 'seq'), may hold values from -6 to 6
- out_weight: bfloat16 [1536, 1536], P('seq'), may hold values from -0.15625 to 0.15625
- frame_video: int32 [4, 64], P('dp'), may hold values from 0 to 15, never falling along the last dimension, each value on 1 to 32 neighbouring positions
Outputs:
- mixed_out: bfloat16 [4, 64, 192, 1536], P('dp', 'seq')
- query_grad: bfloat16 [4, 64, 192, 1536], P('dp', 'seq')
- key_grad: bfloat16 [4, 64, 192, 1536], P('dp', 'seq')
- value_grad: bfloat16 [4, 64, 192, 1536], P('dp', 'seq')
- weight_grad: float32 [1536, 1536], P('seq')
The draws below stay inside these ranges and needn't reach their ends.
Inputs may be any that keep to these rules, and one draw needn't show every extreme that they name: `frame_video`: each replica's frames are grouped into whole videos in order: ids never fall, each video has 1 to min(32, 32) frames and one has exactly that many.
All inputs are finite; a program needn't handle non-finite values.
Results may differ from the reference program's by a relative error of at most 0.04.
Values may be sent and summed in bfloat16 or wider, within the bound.
No kernel may reach another device: no remote copies, remote signals or barrier semaphores. Data moves between devices by JAX's collectives and lax.ppermute only.
A program may use at most 128 MiB of HBM per device.

```python
import math
import jax
import jax.numpy as jnp
import numpy as np
from jax import lax

HEAD = 128
HEADS = 12
DW = 1536
HD = 1536
FRAMES = 64
SPAN = 192
N_DP = 4


def pair_fields(key):
    shape = (N_DP, FRAMES, SPAN, HEADS, HEAD)
    query_base = jnp.clip(jax.random.normal(jax.random.fold_in(key, 11), shape, jnp.float32), -6.0, 6.0)
    key_base = jnp.clip(jax.random.normal(jax.random.fold_in(key, 12), shape, jnp.float32), -6.0, 6.0)
    return (query_base, key_base)


def draw_queries(key, part):
    query_base, key_base = pair_fields(key)
    query_new = query_base.reshape(N_DP, FRAMES, SPAN, HEADS * HEAD)
    return query_new.astype(jnp.bfloat16)


def draw_key_field(key, part):
    query_base, key_base = pair_fields(key)
    key_new = key_base.reshape(N_DP, FRAMES, SPAN, HEADS * HEAD)
    return key_new.astype(jnp.bfloat16)


def shard_levels(stream_key, dims, shards, low, top_value):
    def one(axis_at, blocks):
        steps = jax.random.uniform(jax.random.fold_in(jax.random.fold_in(stream_key, 6), axis_at), (blocks,), jnp.float32, low / len(shards), top_value / len(shards))
        return jnp.repeat(jnp.exp(steps), dims[axis_at] // blocks).reshape((-1,) + (1,) * (len(dims) - axis_at - 1))

    gain = one(*shards[0])
    for cut in shards[1:]:
        gain = gain * one(*cut)
    return gain


def split_up(amount, total, reach, slope):
    weights = [(1 << 20) // math.isqrt(standing ** slope) + 1 for standing in range(2, amount + 1)]
    surplus, holding = total - reach - (amount - 1), [1] * (amount - 1)
    while surplus > 0:
        movable = [i for i in range(amount - 1) if holding[i] < reach]
        whole, left = sum([weights[i] for i in movable]), surplus
        for i in movable:
            extra = min(reach - holding[i], max(1, left * weights[i] // whole), surplus)
            holding[i] = holding[i] + extra
            surplus = surplus - extra
    return np.array([reach] + holding)


def ragged_sizes(key, count, total, limit, slope):
    if count == 2:
        one = jax.random.randint(key, (), max(1, total - limit), min(limit, total - 1) + 1)
        return jnp.stack([one, total - one])
    tallies = jnp.asarray(split_up(count, total, limit, slope), jnp.int32)
    twos = (count - 1) // 2
    source_of, sink = tallies[1:1 + 2 * twos:2], tallies[2:2 + 2 * twos:2]
    room = jnp.minimum(source_of - 1, limit - sink)
    moved = jax.random.randint(jax.random.fold_in(key, 1), (twos,), 0, 1 << 20) % (room + 1)
    tallies = tallies.at[1:1 + 2 * twos:2].set(source_of - moved).at[2:2 + 2 * twos:2].set(sink + moved)
    return tallies[jax.random.permutation(jax.random.fold_in(key, 2), count)]


def bell_draw(own_key, extent, spread, bound, pieces=(), held_as=jnp.bfloat16):
    values = jax.random.normal(own_key, extent, jnp.float32) * spread
    if len(pieces) > 0:
        values = shard_levels(own_key, extent, pieces, -0.22, 0.18) * values
    return jnp.clip(values, min=-bound, max=bound).astype(held_as)


def setup_inputs(seed: int = 0) -> dict:
    seeds = jax.random.split(jax.random.key(seed), 7)
    return {
        "queries": draw_queries(jax.random.fold_in(seeds[6], 71), 0),
        "key_field": draw_key_field(jax.random.fold_in(seeds[6], 71), 0),
        "value_field": bell_draw(seeds[2], (N_DP, FRAMES, SPAN, HD), 1.0, 6.0, ((0, 4), (1, 64))),
        "out_grad": bell_draw(seeds[3], (N_DP, FRAMES, SPAN, DW), 1.0, 6.0, ((0, 4), (1, 64))),
        "out_weight": bell_draw(seeds[4], (HD, DW), HD ** -0.5, 0.15625, ((0, 64),)),
        "frame_video": jax.vmap(lambda own: jnp.searchsorted(jnp.cumsum(ragged_sizes(own, FRAMES // 4, FRAMES, min(32, FRAMES // 2), 2)), jnp.arange(FRAMES), side="right"))(jax.random.split(seeds[5], N_DP)).reshape((N_DP, FRAMES)).astype(jnp.int32),
    }


def reference(queries, key_field, value_field, out_grad, out_weight, frame_video):
    factor = HEAD ** -0.5
    mixed_list = []
    qgrad_list = []
    kgrad_list = []
    vgrad_list = []
    weight_grad = jnp.zeros((HEADS * HEAD, DW), jnp.float32)
    for replica in range(N_DP):
        query4 = queries[replica].reshape(FRAMES, SPAN, HEADS, HEAD).astype(jnp.float32)
        key4 = key_field[replica].reshape(FRAMES, SPAN, HEADS, HEAD).astype(jnp.float32)
        value4 = value_field[replica].reshape(FRAMES, SPAN, HEADS, HEAD).astype(jnp.float32)
        videos = frame_video[replica]
        allowed = (videos[:, None] == videos[None, :])[None, None]
        logits = jnp.einsum('fphe,gphe->phfg', query4, key4) * factor
        logits = jnp.where(allowed, logits, jnp.float32(-1e30))
        shifted = jnp.exp(logits - jnp.max(logits, axis=-1, keepdims=True))
        probs = shifted / jnp.sum(shifted, axis=-1, keepdims=True)
        probs_low = probs.astype(jnp.bfloat16).astype(jnp.float32)
        mixed = jnp.einsum('phfg,gphe->fphe', probs_low, value4).astype(jnp.bfloat16)
        mixed_flat = mixed.reshape(FRAMES * SPAN, HEADS * HEAD)
        out_flat = jnp.dot(mixed_flat, out_weight, preferred_element_type=jnp.float32).astype(jnp.bfloat16)
        grad_flat = out_grad[replica].reshape(FRAMES * SPAN, DW)
        mixed_grad = lax.dot_general(grad_flat, out_weight, (((1,), (1,)), ((), ())), preferred_element_type=jnp.float32).astype(jnp.bfloat16)
        grad4 = mixed_grad.reshape(FRAMES, SPAN, HEADS, HEAD).astype(jnp.float32)
        value_grad = jnp.einsum('phfg,fphe->gphe', probs_low, grad4).astype(jnp.bfloat16)
        through = jnp.einsum('fphe,gphe->phfg', grad4, value4)
        inner = jnp.einsum('fphe,fphe->phf', grad4, mixed.astype(jnp.float32))[..., None]
        score_grad = (probs * (through - inner)).astype(jnp.bfloat16).astype(jnp.float32)
        query_grad = (jnp.einsum('phfg,gphe->fphe', score_grad, key4) * factor).astype(jnp.bfloat16)
        key_grad = (jnp.einsum('phfg,fphe->gphe', score_grad, query4) * factor).astype(jnp.bfloat16)
        weight_grad = weight_grad + lax.dot_general(mixed_flat, grad_flat, (((0,), (0,)), ((), ())), preferred_element_type=jnp.float32)
        mixed_list.append(out_flat.reshape(FRAMES, SPAN, DW))
        qgrad_list.append(query_grad.reshape(FRAMES, SPAN, HEADS * HEAD))
        kgrad_list.append(key_grad.reshape(FRAMES, SPAN, HEADS * HEAD))
        vgrad_list.append(value_grad.reshape(FRAMES, SPAN, HEADS * HEAD))
    return (jnp.stack(mixed_list), jnp.stack(qgrad_list), jnp.stack(kgrad_list), jnp.stack(vgrad_list), weight_grad)
```

```python
import functools

import jax
import jax.numpy as jnp
import numpy as np
from jax import lax
from jax.experimental import pallas as pl
from jax.experimental.pallas import tpu as pltpu
from jax.sharding import PartitionSpec as P

HEAD = 128
HEADS = 12
WIDTH = HEAD * HEADS
HALF = WIDTH // 2
FRAMES = 64
PLACES = 3
ROWS = FRAMES * PLACES
NX, NY, NZ = 4, 4, 8
SEQ = NY * NZ * 2
STRIP = WIDTH // SEQ
QUARTER = WIDTH // NX
BF = jnp.bfloat16
F32 = jnp.float32
FACTOR = HEAD ** (-0.5)
MIB = 1 << 20


def params(mib):
    return pltpu.CompilerParams(vmem_limit_bytes=mib * MIB)


def dot(a, b, dims=((1,), (0,))):
    return lax.dot_general(a, b, (dims, ((), ())), preferred_element_type=F32)


def swap_matrix(to_blocks):
    a = lax.broadcasted_iota(jnp.int32, (256, 256), 0 if to_blocks else 1)
    b = lax.broadcasted_iota(jnp.int32, (256, 256), 1 if to_blocks else 0)
    return jnp.where(8 * (a % 32) + a // 32 == b, F32(1), F32(0)).astype(BF)


def pack(sources, out_ref):
    swap = swap_matrix(False)
    for half in range(2):
        for tile in range(HALF // 256):
            parts = [
                src[32 * half : 32 * half + 32, HALF * e + 256 * tile : HALF * e + 256 * tile + 256]
                for src in sources
                for e in range(2)
            ]
            mixed = dot(swap, jnp.concatenate(parts, axis=0))
            out_ref[256 * half : 256 * half + 256, 256 * tile : 256 * tile + 256] = mixed.astype(BF)


def unpack(in_ref, sinks):
    swap = swap_matrix(True)
    for half in range(2):
        for tile in range(HALF // 256):
            piece = in_ref[256 * half : 256 * half + 256, 256 * tile : 256 * tile + 256]
            rows = dot(swap, piece).astype(BF)
            for n in range(8):
                col = HALF * (n % 2) + 256 * tile
                sinks[n // 2][32 * half : 32 * half + 32, col : col + 256] = rows[32 * n : 32 * n + 32]


def pack_kernel(a, b, c, d, out_ref):
    pack((a, b, c, d), out_ref)


def unpack_kernel(in_ref, a, b, c, d):
    unpack(in_ref, (a, b, c, d))


place_block = pl.BlockSpec((FRAMES, WIDTH), lambda j: (j, 0))
message_block = pl.BlockSpec((8 * SEQ, HALF), lambda j: (0, j))
rows_shape = jax.ShapeDtypeStruct((ROWS, WIDTH), BF)
message_shape = jax.ShapeDtypeStruct((8 * SEQ, PLACES * HALF), BF)


def pack_call(*arrays):
    return pl.pallas_call(
        pack_kernel,
        grid=(PLACES,),
        in_specs=[place_block] * 4,
        out_specs=message_block,
        out_shape=message_shape,
        compiler_params=params(24),
        name="pack",
    )(*arrays)


def unpack_call(message):
    return pl.pallas_call(
        unpack_kernel,
        grid=(PLACES,),
        in_specs=[message_block],
        out_specs=[place_block] * 4,
        out_shape=[rows_shape] * 4,
        compiler_params=params(24),
        name="unpack",
    )(message)


def pair(ref, n):
    at = 2 * HEAD * n
    return jnp.concatenate([ref[:, at : at + HEAD], ref[:, at + HEAD : at + 2 * HEAD]], axis=0)


def put_pair(ref, n, value):
    at = 2 * HEAD * n
    ref[:, at : at + HEAD] = value[:FRAMES]
    ref[:, at + HEAD : at + 2 * HEAD] = value[FRAMES:]


def forward_kernel(mask_ref, in_ref, q, k, v, g, mixed, probs_ref):
    unpack(in_ref, (q, k, v, g))
    allowed = mask_ref[...] > 0.5
    for n in range(HEADS // 2):
        logits = dot(pair(q, n), pair(k, n), ((1,), (1,))) * FACTOR
        logits = jnp.where(allowed, logits, F32(-1e30))
        shifted = jnp.exp(logits - jnp.max(logits, axis=-1, keepdims=True))
        probs = shifted / jnp.sum(shifted, axis=-1, keepdims=True)
        probs_ref[n] = probs
        put_pair(mixed, n, dot(probs.astype(BF), pair(v, n)).astype(BF))


probs_block = pl.BlockSpec((HEADS // 2, 2 * FRAMES, 2 * FRAMES), lambda j: (j, 0, 0))


def forward_call(mask, message):
    return pl.pallas_call(
        forward_kernel,
        grid=(PLACES,),
        in_specs=[pl.BlockSpec((128, 128), lambda j: (0, 0)), message_block],
        out_specs=[place_block] * 5 + [probs_block],
        out_shape=[rows_shape] * 5 + [jax.ShapeDtypeStruct((HEADS // 2 * PLACES, 128, 128), F32)],
        compiler_params=params(32),
        name="forward",
    )(mask, message)


def weight_kernel(at, mixed, grad, keep, send, turned, strips):
    @pl.when(pl.program_id(0) == 0)
    def _():
        turned[...] = mixed[...].astype(F32).T
        for side in range(2):
            core = at[0] if side == 0 else 1 - at[0]
            for dy in range(NY):
                for dz in range(NZ):
                    y, z = (at[2] + dy) % NY, (at[3] + dz) % NZ
                    src = pl.multiple_of((y * NZ + z) * 2 * STRIP + core * STRIP, 8)
                    dst = (dy * NZ + dz) * STRIP
                    strips[side, dst : dst + STRIP, :] = turned[pl.ds(src, STRIP), :]

    for side, out in ((0, keep), (1, send)):
        out[0] = dot(strips[side].astype(BF), grad[...]).astype(BF)


def weight_call(at, mixed, grad):
    return pl.pallas_call(
        weight_kernel,
        grid_spec=pltpu.PrefetchScalarGridSpec(
            num_scalar_prefetch=1,
            grid=(NX,),
            in_specs=[
                pl.BlockSpec((ROWS, WIDTH), lambda d, at: (0, 0)),
                pl.BlockSpec((ROWS, QUARTER), lambda d, at: (0, (at[1] + d) % NX)),
            ],
            out_specs=[pl.BlockSpec((1, HALF, QUARTER), lambda d, at: (d, 0, 0))] * 2,
            scratch_shapes=[pltpu.VMEM((WIDTH, ROWS), F32), pltpu.VMEM((2, HALF, ROWS), F32)],
        ),
        out_shape=[jax.ShapeDtypeStruct((NX, HALF, QUARTER), BF)] * 2,
        compiler_params=params(32),
        name="weight",
    )(at, mixed, grad)


def project_kernel(mixed, grad, weight, out, mixed_grad, total):
    step = pl.program_id(0)
    w = weight[...]
    part = dot(mixed[...], w)

    @pl.when(step == 0)
    def _():
        total[...] = part

    @pl.when(step > 0)
    def _():
        total[...] += part

    mixed_grad[...] = dot(grad[...], w, ((1,), (1,))).astype(BF)

    @pl.when(step == pl.num_programs(0) - 1)
    def _():
        out[...] = total[...].astype(BF)


def project_call(mixed, grad, weight):
    depth = 256
    return pl.pallas_call(
        project_kernel,
        grid=(WIDTH // depth,),
        in_specs=[
            pl.BlockSpec((ROWS, depth), lambda i: (0, i)),
            pl.BlockSpec((ROWS, WIDTH), lambda i: (0, 0)),
            pl.BlockSpec((depth, WIDTH), lambda i: (i, 0)),
        ],
        out_specs=[
            pl.BlockSpec((ROWS, WIDTH), lambda i: (0, 0)),
            pl.BlockSpec((ROWS, depth), lambda i: (0, i)),
        ],
        out_shape=[rows_shape] * 2,
        scratch_shapes=[pltpu.VMEM((ROWS, WIDTH), F32)],
        compiler_params=params(32),
        name="project",
    )(mixed, grad, weight)


def backward_kernel(q, k, v, mixed, mixed_grad, out, probs_ref, message, q_grad, k_grad, v_grad):
    for n in range(HEADS // 2):
        probs = probs_ref[n]
        grad = pair(mixed_grad, n)
        put_pair(v_grad, n, dot(probs.astype(BF), grad, ((0,), (0,))).astype(BF))
        through = dot(grad, pair(v, n), ((1,), (1,)))
        inner = jnp.sum(grad.astype(F32) * pair(mixed, n).astype(F32), axis=-1, keepdims=True)
        score = (probs * (through - inner)).astype(BF)
        put_pair(q_grad, n, (dot(score, pair(k, n)) * FACTOR).astype(BF))
        put_pair(k_grad, n, (dot(score, pair(q, n), ((0,), (0,))) * FACTOR).astype(BF))
    pack((out, q_grad, k_grad, v_grad), message)


def backward_call(*arrays):
    return pl.pallas_call(
        backward_kernel,
        grid=(PLACES,),
        in_specs=[place_block] * 6 + [probs_block],
        out_specs=message_block,
        out_shape=message_shape,
        scratch_shapes=[pltpu.VMEM((FRAMES, WIDTH), BF)] * 3,
        compiler_params=params(32),
        name="backward",
    )(*arrays)


def seq_shift(dy, dz, dc):
    seq = np.arange(SEQ).reshape(NY, NZ, 2)
    return [
        (int(seq[y, z, c]), int(seq[(y + dy) % NY, (z + dz) % NZ, c ^ dc]))
        for y in range(NY)
        for z in range(NZ)
        for c in range(2)
    ]


def add_up(parts):
    total = parts[0].astype(F32)
    for part in parts[1:]:
        total = total + part.astype(F32)
    return total


def reduce_weight(keep, send):
    came = lax.ppermute(send, "seq", seq_shift(0, 0, 1))
    parts = [add_up([keep[d], came[d]]).astype(BF) for d in range(NX)]
    came = [lax.ppermute(parts[d], "dp", [(i, (i + d) % NX) for i in range(NX)]) for d in (1, 3, 2)]
    chip = add_up([parts[0]] + came).astype(BF).reshape(NY, NZ * STRIP, QUARTER)
    came = [lax.ppermute(chip[d], "seq", seq_shift(d, 0, 0)) for d in (1, 3, 2)]
    column = add_up([chip[0]] + came).astype(BF).reshape(NZ, STRIP, QUARTER)
    came = [lax.ppermute(column[d], "seq", seq_shift(0, d, 0)) for d in (1, 7, 2, 6, 3, 5, 4)]
    strip = add_up([column[0]] + came)
    return lax.all_gather(strip, "dp", axis=1, tiled=True)


def gather_weight(out_weight):
    seq = np.arange(SEQ).reshape(NY, NZ * 2)
    rows = [list(map(int, seq[y])) for y in range(NY)]
    columns = [list(map(int, seq[:, n])) for n in range(NZ * 2)]
    part = lax.all_gather(out_weight, "seq", axis=0, tiled=True, axis_index_groups=rows)
    return lax.all_gather(part, "seq", axis=0, tiled=True, axis_index_groups=columns)


def exchange(message):
    return lax.all_to_all(message, "seq", split_axis=0, concat_axis=0, tiled=True)


def local(queries, key_field, value_field, out_grad, out_weight, frame_video):
    weight = gather_weight(out_weight)
    videos = frame_video[0]
    same = jnp.tile((videos[:, None] == videos[None, :]), (2, 2))
    head = jnp.arange(2 * FRAMES) // FRAMES
    mask = (same & (head[:, None] == head[None, :])).astype(F32)
    rank = lax.axis_index("seq")
    at = jnp.stack([rank % 2, lax.axis_index("dp"), rank // (2 * NZ), rank // 2 % NZ]).astype(jnp.int32)

    flat = [x.reshape(ROWS, WIDTH) for x in (queries, key_field, value_field, out_grad)]
    arrived = exchange(pack_call(*flat))
    q, k, v, g, mixed, probs = forward_call(mask, arrived)
    keep, send = weight_call(at, mixed, g)
    out, mixed_grad = project_call(mixed, g, weight)
    message = backward_call(q, k, v, mixed, mixed_grad, out, probs)
    results = unpack_call(exchange(message))
    weight_grad = reduce_weight(keep, send)
    return tuple(x.reshape(queries.shape) for x in results) + (weight_grad,)


def solution(mesh):
    placed = P("dp", "seq", None, None)
    return jax.shard_map(
        local,
        mesh=mesh,
        in_specs=(placed, placed, placed, placed, P("seq", None), P("dp", None)),
        out_specs=(placed, placed, placed, placed, P("seq", None)),
        check_vma=False,
    )
```

```python
import functools

import jax
import jax.numpy as jnp
import numpy as np
from jax import lax
from jax.experimental import pallas as pl
from jax.experimental.pallas import tpu as pltpu
from jax.sharding import PartitionSpec as P

HEAD = 128
HEADS = 12
WIDTH = HEAD * HEADS
HALF = WIDTH // 2
FRAMES = 64
PLACES = 3
ROWS = FRAMES * PLACES
NX, NY, NZ = 4, 4, 8
SEQ = NY * NZ * 2
STRIP = WIDTH // SEQ
QUARTER = WIDTH // NX
BF = jnp.bfloat16
F32 = jnp.float32
FACTOR = HEAD ** (-0.5)
MIB = 1 << 20


def params(mib):
    return pltpu.CompilerParams(vmem_limit_bytes=mib * MIB)


def dot(a, b, dims=((1,), (0,))):
    return lax.dot_general(a, b, (dims, ((), ())), preferred_element_type=F32)


def swap_matrix(to_blocks):
    a = lax.broadcasted_iota(jnp.int32, (256, 256), 0 if to_blocks else 1)
    b = lax.broadcasted_iota(jnp.int32, (256, 256), 1 if to_blocks else 0)
    return jnp.where(8 * (a % 32) + a // 32 == b, F32(1), F32(0)).astype(BF)


def pack(sources, out_ref):
    swap = swap_matrix(False)
    for half in range(2):
        for tile in range(HALF // 256):
            parts = [
                src[32 * half : 32 * half + 32, HALF * e + 256 * tile : HALF * e + 256 * tile + 256]
                for src in sources
                for e in range(2)
            ]
            mixed = dot(swap, jnp.concatenate(parts, axis=0))
            out_ref[256 * half : 256 * half + 256, 256 * tile : 256 * tile + 256] = mixed.astype(BF)


def unpack(in_ref, sinks):
    swap = swap_matrix(True)
    for half in range(2):
        for tile in range(HALF // 256):
            piece = in_ref[256 * half : 256 * half + 256, 256 * tile : 256 * tile + 256]
            rows = dot(swap, piece).astype(BF)
            for n in range(8):
                col = HALF * (n % 2) + 256 * tile
                sinks[n // 2][32 * half : 32 * half + 32, col : col + 256] = rows[32 * n : 32 * n + 32]


def pack_kernel(a, b, c, d, out_ref):
    pack((a, b, c, d), out_ref)


def unpack_kernel(in_ref, a, b, c, d):
    unpack(in_ref, (a, b, c, d))


place_block = pl.BlockSpec((FRAMES, WIDTH), lambda j: (j, 0))
message_block = pl.BlockSpec((8 * SEQ, HALF), lambda j: (0, j))
rows_shape = jax.ShapeDtypeStruct((ROWS, WIDTH), BF)
message_shape = jax.ShapeDtypeStruct((8 * SEQ, PLACES * HALF), BF)


def pack_call(*arrays):
    return pl.pallas_call(
        pack_kernel,
        grid=(PLACES,),
        in_specs=[place_block] * 4,
        out_specs=message_block,
        out_shape=message_shape,
        compiler_params=params(60),
        name="pack",
    )(*arrays)


def unpack_call(message):
    return pl.pallas_call(
        unpack_kernel,
        grid=(PLACES,),
        in_specs=[message_block],
        out_specs=[place_block] * 4,
        out_shape=[rows_shape] * 4,
        compiler_params=params(60),
        name="unpack",
    )(message)


def pair(ref, n):
    at = 2 * HEAD * n
    return jnp.concatenate([ref[:, at : at + HEAD], ref[:, at + HEAD : at + 2 * HEAD]], axis=0)


def put_pair(ref, n, value):
    at = 2 * HEAD * n
    ref[:, at : at + HEAD] = value[:FRAMES]
    ref[:, at + HEAD : at + 2 * HEAD] = value[FRAMES:]


def forward_kernel(mask_ref, in_ref, q, k, v, g, mixed, probs_ref):
    unpack(in_ref, (q, k, v, g))
    allowed = mask_ref[...] > 0.5
    for n in range(HEADS // 2):
        logits = dot(pair(q, n), pair(k, n), ((1,), (1,))) * FACTOR
        logits = jnp.where(allowed, logits, F32(-1e30))
        shifted = jnp.exp(logits - jnp.max(logits, axis=-1, keepdims=True))
        probs = shifted / jnp.sum(shifted, axis=-1, keepdims=True)
        probs_ref[n] = probs
        put_pair(mixed, n, dot(probs.astype(BF), pair(v, n)).astype(BF))


probs_block = pl.BlockSpec((HEADS // 2, 2 * FRAMES, 2 * FRAMES), lambda j: (j, 0, 0))


def forward_call(mask, message):
    return pl.pallas_call(
        forward_kernel,
        grid=(PLACES,),
        in_specs=[pl.BlockSpec((128, 128), lambda j: (0, 0)), message_block],
        out_specs=[place_block] * 5 + [probs_block],
        out_shape=[rows_shape] * 5 + [jax.ShapeDtypeStruct((HEADS // 2 * PLACES, 128, 128), F32)],
        compiler_params=params(60),
        name="forward",
    )(mask, message)


def weight_kernel(at, mixed, grad, keep, send, turned, strips):
    @pl.when(pl.program_id(0) == 0)
    def _():
        turned[...] = mixed[...].astype(F32).T
        for side in range(2):
            core = at[0] if side == 0 else 1 - at[0]
            for dy in range(NY):
                for dz in range(NZ):
                    y, z = (at[2] + dy) % NY, at[3] ^ dz
                    src = pl.multiple_of((y * NZ + z) * 2 * STRIP + core * STRIP, 8)
                    dst = (dy * NZ + dz) * STRIP
                    strips[side, dst : dst + STRIP, :] = turned[pl.ds(src, STRIP), :]

    for side, out in ((0, keep), (1, send)):
        out[0] = dot(strips[side].astype(BF), grad[...]).astype(BF)


def weight_call(at, mixed, grad):
    return pl.pallas_call(
        weight_kernel,
        grid_spec=pltpu.PrefetchScalarGridSpec(
            num_scalar_prefetch=1,
            grid=(NX,),
            in_specs=[
                pl.BlockSpec((ROWS, WIDTH), lambda d, at: (0, 0)),
                pl.BlockSpec((ROWS, QUARTER), lambda d, at: (0, (at[1] + d) % NX)),
            ],
            out_specs=[pl.BlockSpec((1, HALF, QUARTER), lambda d, at: (d, 0, 0))] * 2,
            scratch_shapes=[pltpu.VMEM((WIDTH, ROWS), F32), pltpu.VMEM((2, HALF, ROWS), F32)],
        ),
        out_shape=[jax.ShapeDtypeStruct((NX, HALF, QUARTER), BF)] * 2,
        compiler_params=params(60),
        name="weight",
    )(at, mixed, grad)


def project_kernel(mixed, grad, weight, out, mixed_grad, total):
    step = pl.program_id(0)
    w = weight[...]
    part = dot(mixed[...], w)

    @pl.when(step == 0)
    def _():
        total[...] = part

    @pl.when(step > 0)
    def _():
        total[...] += part

    mixed_grad[...] = dot(grad[...], w, ((1,), (1,))).astype(BF)

    @pl.when(step == pl.num_programs(0) - 1)
    def _():
        out[...] = total[...].astype(BF)


def project_call(mixed, grad, weight):
    depth = 256
    return pl.pallas_call(
        project_kernel,
        grid=(WIDTH // depth,),
        in_specs=[
            pl.BlockSpec((ROWS, depth), lambda i: (0, i)),
            pl.BlockSpec((ROWS, WIDTH), lambda i: (0, 0)),
            pl.BlockSpec((depth, WIDTH), lambda i: (i, 0)),
        ],
        out_specs=[
            pl.BlockSpec((ROWS, WIDTH), lambda i: (0, 0)),
            pl.BlockSpec((ROWS, depth), lambda i: (0, i)),
        ],
        out_shape=[rows_shape] * 2,
        scratch_shapes=[pltpu.VMEM((ROWS, WIDTH), F32)],
        compiler_params=params(60),
        name="project",
    )(mixed, grad, weight)


def backward_kernel(q, k, v, mixed, mixed_grad, out, probs_ref, message, q_grad, k_grad, v_grad):
    for n in range(HEADS // 2):
        probs = probs_ref[n]
        grad = pair(mixed_grad, n)
        put_pair(v_grad, n, dot(probs.astype(BF), grad, ((0,), (0,))).astype(BF))
        through = dot(grad, pair(v, n), ((1,), (1,)))
        inner = jnp.sum(grad.astype(F32) * pair(mixed, n).astype(F32), axis=-1, keepdims=True)
        score = (probs * (through - inner)).astype(BF)
        put_pair(q_grad, n, (dot(score, pair(k, n)) * FACTOR).astype(BF))
        put_pair(k_grad, n, (dot(score, pair(q, n), ((0,), (0,))) * FACTOR).astype(BF))
    pack((out, q_grad, k_grad, v_grad), message)


def backward_call(*arrays):
    return pl.pallas_call(
        backward_kernel,
        grid=(PLACES,),
        in_specs=[place_block] * 6 + [probs_block],
        out_specs=message_block,
        out_shape=message_shape,
        scratch_shapes=[pltpu.VMEM((FRAMES, WIDTH), BF)] * 3,
        compiler_params=params(60),
        name="backward",
    )(*arrays)


def seq_shift(dy, dz, dc):
    seq = np.arange(SEQ).reshape(NY, NZ, 2)
    return [
        (int(seq[y, z, c]), int(seq[(y + dy) % NY, (z + dz) % NZ, c ^ dc]))
        for y in range(NY)
        for z in range(NZ)
        for c in range(2)
    ]


def seq_flip(bit):
    seq = np.arange(SEQ).reshape(NY, NZ, 2)
    return [
        (int(seq[y, z, c]), int(seq[y, z ^ bit, c])) for y in range(NY) for z in range(NZ) for c in range(2)
    ]


def add_up(parts):
    total = parts[0].astype(F32)
    for part in parts[1:]:
        total = total + part.astype(F32)
    return total


def reduce_chip(keep, came):
    return [add_up([keep[d], came[d]]).astype(BF) for d in range(NX)]


def reduce_rest(parts):
    came = [lax.ppermute(parts[d], "dp", [(i, (i + d) % NX) for i in range(NX)]) for d in (1, 3, 2)]
    chip = add_up([parts[0]] + came).astype(BF).reshape(NY, NZ * STRIP, QUARTER)
    came = [lax.ppermute(chip[d], "seq", seq_shift(d, 0, 0)) for d in (1, 3, 2)]
    strips = add_up([chip[0]] + came).astype(BF).reshape(NZ, STRIP, QUARTER)
    for bit in (4, 2, 1):
        came = lax.ppermute(strips[bit:], "seq", seq_flip(bit))
        strips = add_up([strips[:bit], came])
        if bit > 1:
            strips = strips.astype(BF)
    own = strips[0]
    came = {d: lax.ppermute(own, "dp", [(i, (i + d) % NX) for i in range(NX)]) for d in (1, 3, 2)}
    place = lax.axis_index("dp")
    quarters = [lax.select_n((place - n) % NX, own, came[1], came[2], came[3]) for n in range(NX)]
    return jnp.concatenate(quarters, axis=1)


def gather_weight(out_weight):
    cores = [list(range(core, SEQ, 2)) for core in range(2)]
    own = lax.all_gather(out_weight, "seq", axis=0, axis_index_groups=cores)
    other = lax.ppermute(own, "seq", seq_shift(0, 0, 1))
    first = lax.axis_index("seq") % 2 == 0
    both = [jnp.where(first, own, other), jnp.where(first, other, own)]
    return jnp.stack(both, axis=1).reshape(WIDTH, WIDTH)


def exchange(message):
    return lax.all_to_all(message, "seq", split_axis=0, concat_axis=0, tiled=True)


def local(queries, key_field, value_field, out_grad, out_weight, frame_video):
    weight = gather_weight(out_weight)
    videos = frame_video[0]
    same = jnp.tile((videos[:, None] == videos[None, :]), (2, 2))
    head = jnp.arange(2 * FRAMES) // FRAMES
    mask = (same & (head[:, None] == head[None, :])).astype(F32)
    rank = lax.axis_index("seq")
    at = jnp.stack([rank % 2, lax.axis_index("dp"), rank // (2 * NZ), rank // 2 % NZ]).astype(jnp.int32)

    flat = [x.reshape(ROWS, WIDTH) for x in (queries, key_field, value_field, out_grad)]
    arrived = exchange(pack_call(*flat))
    q, k, v, g, mixed, probs = forward_call(mask, arrived)
    keep, send = weight_call(at, mixed, g)
    came = lax.ppermute(send, "seq", seq_shift(0, 0, 1))
    out, mixed_grad = project_call(mixed, g, weight)
    parts, mixed_grad = lax.optimization_barrier((reduce_chip(keep, came), mixed_grad))
    message = backward_call(q, k, v, mixed, mixed_grad, out, probs)
    results = unpack_call(exchange(message))
    weight_grad = reduce_rest(parts)
    return tuple(x.reshape(queries.shape) for x in results) + (weight_grad,)


def solution(mesh):
    placed = P("dp", "seq", None, None)
    return jax.shard_map(
        local,
        mesh=mesh,
        in_specs=(placed, placed, placed, placed, P("seq", None), P("dp", None)),
        out_specs=(placed, placed, placed, placed, P("seq", None)),
        check_vma=False,
    )
```

```python
import functools

import jax
import jax.numpy as jnp
import numpy as np
from jax import lax
from jax.experimental import pallas as pl
from jax.experimental.pallas import tpu as pltpu
from jax.sharding import PartitionSpec as P

HEAD = 128
HEADS = 12
WIDTH = HEAD * HEADS
HALF = WIDTH // 2
FRAMES = 64
PLACES = 3
ROWS = FRAMES * PLACES
NX, NY, NZ = 4, 4, 8
SEQ = NY * NZ * 2
STRIP = WIDTH // SEQ
QUARTER = WIDTH // NX
BF = jnp.bfloat16
F32 = jnp.float32
FACTOR = HEAD ** (-0.5)
MIB = 1 << 20


def params(mib):
    return pltpu.CompilerParams(vmem_limit_bytes=mib * MIB)


def cost(us):
    return pl.CostEstimate(flops=0, bytes_accessed=int(us * 3.5e6), transcendentals=0)


def dot(a, b, dims=((1,), (0,))):
    return lax.dot_general(a, b, (dims, ((), ())), preferred_element_type=F32)


def swap_matrix(to_blocks):
    a = lax.broadcasted_iota(jnp.int32, (256, 256), 0 if to_blocks else 1)
    b = lax.broadcasted_iota(jnp.int32, (256, 256), 1 if to_blocks else 0)
    return jnp.where(8 * (a % 32) + a // 32 == b, F32(1), F32(0)).astype(BF)


def pack(sources, out_ref):
    swap = swap_matrix(False)
    for half in range(2):
        for tile in range(HALF // 256):
            parts = [
                src[32 * half : 32 * half + 32, HALF * e + 256 * tile : HALF * e + 256 * tile + 256]
                for src in sources
                for e in range(2)
            ]
            mixed = dot(swap, jnp.concatenate(parts, axis=0))
            out_ref[256 * half : 256 * half + 256, 256 * tile : 256 * tile + 256] = mixed.astype(BF)


def unpack(in_ref, sinks):
    swap = swap_matrix(True)
    for half in range(2):
        for tile in range(HALF // 256):
            piece = in_ref[256 * half : 256 * half + 256, 256 * tile : 256 * tile + 256]
            rows = dot(swap, piece).astype(BF)
            for n in range(8):
                col = HALF * (n % 2) + 256 * tile
                sinks[n // 2][32 * half : 32 * half + 32, col : col + 256] = rows[32 * n : 32 * n + 32]


def pack_kernel(a, b, c, d, out_ref):
    pack((a, b, c, d), out_ref)


def unpack_kernel(in_ref, a, b, c, d):
    unpack(in_ref, (a, b, c, d))


place_block = pl.BlockSpec((FRAMES, WIDTH), lambda j: (j, 0))
message_block = pl.BlockSpec((8 * SEQ, HALF), lambda j: (0, j))
rows_shape = jax.ShapeDtypeStruct((ROWS, WIDTH), BF)
message_shape = jax.ShapeDtypeStruct((8 * SEQ, PLACES * HALF), BF)


def pack_call(*arrays):
    return pl.pallas_call(
        pack_kernel,
        grid=(PLACES,),
        in_specs=[place_block] * 4,
        out_specs=message_block,
        out_shape=message_shape,
        compiler_params=params(60),
        cost_estimate=cost(4),
        name="pack",
    )(*arrays)


def unpack_call(message):
    return pl.pallas_call(
        unpack_kernel,
        grid=(PLACES,),
        in_specs=[message_block],
        out_specs=[place_block] * 4,
        out_shape=[rows_shape] * 4,
        compiler_params=params(60),
        cost_estimate=cost(4),
        name="unpack",
    )(message)


def pair(ref, n):
    at = 2 * HEAD * n
    return jnp.concatenate([ref[:, at : at + HEAD], ref[:, at + HEAD : at + 2 * HEAD]], axis=0)


def put_pair(ref, n, value):
    at = 2 * HEAD * n
    ref[:, at : at + HEAD] = value[:FRAMES]
    ref[:, at + HEAD : at + 2 * HEAD] = value[FRAMES:]


def forward_kernel(mask_ref, in_ref, q, k, v, g, mixed, probs_ref):
    unpack(in_ref, (q, k, v, g))
    allowed = mask_ref[...] > 0.5
    for n in range(HEADS // 2):
        logits = dot(pair(k, n), pair(q, n), ((1,), (1,))) * FACTOR
        logits = jnp.where(allowed, logits, F32(-1e30))
        shifted = jnp.exp(logits - jnp.max(logits, axis=0, keepdims=True))
        probs = shifted * (1 / jnp.sum(shifted, axis=0, keepdims=True))
        probs_ref[n] = probs
        put_pair(mixed, n, dot(probs.astype(BF), pair(v, n), ((0,), (0,))).astype(BF))


probs_block = pl.BlockSpec((HEADS // 2, 2 * FRAMES, 2 * FRAMES), lambda j: (j, 0, 0))


def forward_call(mask, message):
    return pl.pallas_call(
        forward_kernel,
        grid=(PLACES,),
        in_specs=[pl.BlockSpec((128, 128), lambda j: (0, 0)), message_block],
        out_specs=[place_block] * 5 + [probs_block],
        out_shape=[rows_shape] * 5 + [jax.ShapeDtypeStruct((HEADS // 2 * PLACES, 128, 128), F32)],
        compiler_params=params(14),
        cost_estimate=cost(6),
        name="forward",
    )(mask, message)


def strip_copies(at, copy):
    for side in range(2):
        core = at[0] if side == 0 else 1 - at[0]
        for dy in range(NY):
            for dz in range(NZ):
                y, z = (at[2] + dy) % NY, at[3] ^ dz
                there = pl.multiple_of((y * NZ + z) * 2 * STRIP + core * STRIP, 8)
                copy(side, (dy * NZ + dz) * STRIP, there)


def weight_kernel(at, mixed, grad, keep, send, ordered, turned, strips):
    @pl.when(pl.program_id(0) == 0)
    def _():
        turned[...] = mixed[...].astype(F32).T

        def copy(side, here, there):
            strips[side, here : here + STRIP, :] = turned[pl.ds(there, STRIP), :]

        strip_copies(at, copy)
        for side in range(2):
            ordered[:, HALF * side : HALF * side + HALF] = strips[side].T.astype(BF)

    for side, out in ((0, keep), (1, send)):
        out[0] = dot(strips[side].astype(BF), grad[...]).astype(BF)


def weight_call(at, mixed, grad):
    return pl.pallas_call(
        weight_kernel,
        grid_spec=pltpu.PrefetchScalarGridSpec(
            num_scalar_prefetch=1,
            grid=(NX,),
            in_specs=[
                pl.BlockSpec((ROWS, WIDTH), lambda d, at: (0, 0)),
                pl.BlockSpec((ROWS, QUARTER), lambda d, at: (0, (at[1] + d) % NX)),
            ],
            out_specs=[pl.BlockSpec((1, HALF, QUARTER), lambda d, at: (d, 0, 0))] * 2
            + [pl.BlockSpec((ROWS, WIDTH), lambda d, at: (0, 0))],
            scratch_shapes=[pltpu.VMEM((WIDTH, ROWS), F32), pltpu.VMEM((2, HALF, ROWS), F32)],
        ),
        out_shape=[jax.ShapeDtypeStruct((NX, HALF, QUARTER), BF)] * 2 + [rows_shape],
        compiler_params=params(16),
        cost_estimate=cost(4),
        name="weight",
    )(at, mixed, grad)


PIECES = ((0, 0, HALF), (-1, 0, HALF), (1, 0, HALF), (2, 0, HALF // 2), (2, HALF // 2, HALF // 2))


def project_kernel(at, ordered, grad, *refs):
    weights, (out, mixed_grad, strips, turned) = refs[: 2 * len(PIECES)], refs[2 * len(PIECES) :]
    totals = {}
    for n, (shift, start, size) in enumerate(PIECES):
        cols = pl.ds(pl.multiple_of((at[1] + shift + NX) % NX * QUARTER, QUARTER), QUARTER)
        part = None
        for side in range(2):
            w = weights[side * len(PIECES) + n][...]
            term = dot(ordered[:, HALF * side + start : HALF * side + start + size], w)
            part = term if part is None else part + term
            turn = dot(w, grad[:, cols], ((1,), (1,)))
            rows = slice(start, start + size)
            if n == 0:
                strips[side, rows, :] = turn
            else:
                strips[side, rows, :] += turn
        totals[shift] = totals[shift] + part if shift in totals else part
        if start + size == HALF:
            out[:, cols] = totals[shift].astype(BF)

    def copy(side, here, there):
        turned[pl.ds(there, STRIP), :] = strips[side, here : here + STRIP, :]

    strip_copies(at, copy)
    mixed_grad[...] = turned[...].T.astype(BF)


def project_call(at, ordered, grad, weights):
    vmem = pl.BlockSpec(memory_space=pltpu.VMEM)
    return pl.pallas_call(
        project_kernel,
        in_specs=[pl.BlockSpec(memory_space=pltpu.SMEM)] + [vmem] * (2 + 2 * len(PIECES)),
        out_specs=[vmem] * 2,
        out_shape=[rows_shape] * 2,
        scratch_shapes=[pltpu.VMEM((2, HALF, ROWS), F32), pltpu.VMEM((WIDTH, ROWS), F32)],
        compiler_params=params(24),
        cost_estimate=cost(6),
        name="project",
    )(at, ordered, grad, *weights)


def backward_kernel(q, k, v, mixed_grad, out, probs_ref, message, q_grad, k_grad, v_grad):
    for n in range(HEADS // 2):
        probs = probs_ref[n]
        probs_low = probs.astype(BF)
        grad = pair(mixed_grad, n)
        put_pair(v_grad, n, dot(probs_low, grad).astype(BF))
        through = dot(pair(v, n), grad, ((1,), (1,)))
        inner = jnp.sum(probs_low.astype(F32) * through, axis=0, keepdims=True)
        score = (probs * (through - inner)).astype(BF)
        put_pair(q_grad, n, (dot(score, pair(k, n), ((0,), (0,))) * FACTOR).astype(BF))
        put_pair(k_grad, n, (dot(score, pair(q, n)) * FACTOR).astype(BF))
    pack((out, q_grad, k_grad, v_grad), message)


def backward_call(*arrays):
    return pl.pallas_call(
        backward_kernel,
        grid=(PLACES,),
        in_specs=[place_block] * 5 + [probs_block],
        out_specs=message_block,
        out_shape=message_shape,
        scratch_shapes=[pltpu.VMEM((FRAMES, WIDTH), BF)] * 3,
        compiler_params=params(14),
        cost_estimate=cost(6),
        name="backward",
    )(*arrays)


def seq_shift(dy, dz, dc):
    seq = np.arange(SEQ).reshape(NY, NZ, 2)
    return [
        (int(seq[y, z, c]), int(seq[(y + dy) % NY, (z + dz) % NZ, c ^ dc]))
        for y in range(NY)
        for z in range(NZ)
        for c in range(2)
    ]


def seq_flip(bit):
    seq = np.arange(SEQ).reshape(NY, NZ, 2)
    return [
        (int(seq[y, z, c]), int(seq[y, z ^ bit, c])) for y in range(NY) for z in range(NZ) for c in range(2)
    ]


def add_up(parts):
    total = parts[0].astype(F32)
    for part in parts[1:]:
        total = total + part.astype(F32)
    return total


def reduce_chip(keep, came):
    return [add_up([keep[d], came[d]]).astype(BF) for d in range(NX)]


def along_x(x, shift):
    return lax.ppermute(x, "dp", [(i, (i + shift) % NX) for i in range(NX)])


def reduce_x(parts):
    mid = HALF // 2
    right = along_x(parts[2][:mid], 1)
    left = along_x(parts[2][mid:], -1)
    ahead = jnp.concatenate([add_up([parts[1][:mid], right]).astype(BF), parts[1][mid:]], axis=0)
    back = jnp.concatenate([parts[3][:mid], add_up([parts[3][mid:], left]).astype(BF)], axis=0)
    return add_up([parts[0], along_x(ahead, 1), along_x(back, -1)]).astype(BF)


def reduce_rest(chip):
    chip = chip.reshape(NY, NZ * STRIP, QUARTER)
    came = [lax.ppermute(chip[d], "seq", seq_shift(d, 0, 0)) for d in (1, 3, 2)]
    strips = add_up([chip[0]] + came).astype(BF).reshape(NZ, STRIP, QUARTER)
    for bit in (4, 2, 1):
        came = lax.ppermute(strips[bit:], "seq", seq_flip(bit))
        strips = add_up([strips[:bit], came])
        if bit > 1:
            strips = strips.astype(BF)
    own = strips[0]
    came = {d: along_x(own, d) for d in (1, 3, 2)}
    place = lax.axis_index("dp")
    quarters = [lax.select_n((place - n) % NX, own, came[1], came[2], came[3]) for n in range(NX)]
    return jnp.concatenate(quarters, axis=1)


def gather_weight(out_weight):
    place = lax.axis_index("dp")
    own = lax.select_n(place, *[out_weight[:, QUARTER * n : QUARTER * n + QUARTER] for n in range(NX)])
    own = own[None]
    for bit in (1, 2, 4):
        own = jnp.concatenate([own, lax.ppermute(own, "seq", seq_flip(bit))], axis=0)
    own = own.reshape(NZ * STRIP, QUARTER)
    came = {d: lax.ppermute(own, "seq", seq_shift(NY - d, 0, 0)) for d in (1, 3, 2)}
    own = jnp.concatenate([own, came[1], came[2], came[3]], axis=0)
    mid = HALF // 2
    left, right = along_x(own, 1), along_x(own, -1)
    pieces = [own, left, right, along_x(left[:mid], 1), along_x(right[mid:], -1)]
    return pieces + [lax.ppermute(piece, "seq", seq_shift(0, 0, 1)) for piece in pieces]


def exchange(message):
    return lax.all_to_all(message, "seq", split_axis=0, concat_axis=0, tiled=True)


def local(queries, key_field, value_field, out_grad, out_weight, frame_video):
    weights = gather_weight(out_weight)
    videos = frame_video[0]
    same = jnp.tile((videos[:, None] == videos[None, :]), (2, 2))
    head = jnp.arange(2 * FRAMES) // FRAMES
    mask = (same & (head[:, None] == head[None, :])).astype(F32)
    rank = lax.axis_index("seq")
    at = jnp.stack([rank % 2, lax.axis_index("dp"), rank // (2 * NZ), rank // 2 % NZ]).astype(jnp.int32)

    flat = [x.reshape(ROWS, WIDTH) for x in (queries, key_field, value_field, out_grad)]
    arrived = exchange(pack_call(*flat))
    q, k, v, g, mixed, probs = forward_call(mask, arrived)
    keep, send, ordered = weight_call(at, mixed, g)
    parts = reduce_chip(keep, lax.ppermute(send, "seq", seq_shift(0, 0, 1)))
    out, mixed_grad = project_call(at, ordered, g, weights)
    parts, mixed_grad = lax.optimization_barrier((parts, mixed_grad))
    chip = reduce_x(parts)
    message = backward_call(q, k, v, mixed_grad, out, probs)
    results = unpack_call(exchange(message))
    weight_grad = reduce_rest(chip)
    return tuple(x.reshape(queries.shape) for x in results) + (weight_grad,)


def solution(mesh):
    placed = P("dp", "seq", None, None)
    return jax.shard_map(
        local,
        mesh=mesh,
        in_specs=(placed, placed, placed, placed, P("seq", None), P("dp", None)),
        out_specs=(placed, placed, placed, placed, P("seq", None)),
        check_vma=False,
    )
```

```python
import functools

import jax
import jax.numpy as jnp
import numpy as np
from jax import lax
from jax.experimental import pallas as pl
from jax.experimental.pallas import tpu as pltpu
from jax.sharding import PartitionSpec as P

HEAD = 128
HEADS = 12
WIDTH = HEAD * HEADS
HALF = WIDTH // 2
FRAMES = 64
PLACES = 3
ROWS = FRAMES * PLACES
NX, NY, NZ = 4, 4, 8
SEQ = NY * NZ * 2
STRIP = WIDTH // SEQ
QUARTER = WIDTH // NX
BF = jnp.bfloat16
F32 = jnp.float32
FACTOR = HEAD ** (-0.5)
MIB = 1 << 20


def params(mib):
    return pltpu.CompilerParams(vmem_limit_bytes=mib * MIB)


def cost(us):
    return pl.CostEstimate(flops=0, bytes_accessed=int(us * 3.5e6), transcendentals=0)


def dot(a, b, dims=((1,), (0,))):
    return lax.dot_general(a, b, (dims, ((), ())), preferred_element_type=F32)


def swap_matrix(to_blocks):
    a = lax.broadcasted_iota(jnp.int32, (256, 256), 0 if to_blocks else 1)
    b = lax.broadcasted_iota(jnp.int32, (256, 256), 1 if to_blocks else 0)
    return jnp.where(8 * (a % 32) + a // 32 == b, F32(1), F32(0)).astype(BF)


def pack(sources, out_ref):
    swap = swap_matrix(False)
    for half in range(2):
        for tile in range(HALF // 256):
            parts = [
                src[32 * half : 32 * half + 32, HALF * e + 256 * tile : HALF * e + 256 * tile + 256]
                for src in sources
                for e in range(2)
            ]
            mixed = dot(swap, jnp.concatenate(parts, axis=0))
            out_ref[256 * half : 256 * half + 256, 256 * tile : 256 * tile + 256] = mixed.astype(BF)


def unpack(in_ref, sinks):
    swap = swap_matrix(True)
    for half in range(2):
        for tile in range(HALF // 256):
            piece = in_ref[256 * half : 256 * half + 256, 256 * tile : 256 * tile + 256]
            rows = dot(swap, piece).astype(BF)
            for n in range(8):
                col = HALF * (n % 2) + 256 * tile
                sinks[n // 2][32 * half : 32 * half + 32, col : col + 256] = rows[32 * n : 32 * n + 32]


def pack_kernel(a, b, c, d, out_ref):
    pack((a, b, c, d), out_ref)


def unpack_kernel(in_ref, a, b, c, d):
    unpack(in_ref, (a, b, c, d))


place_block = pl.BlockSpec((FRAMES, WIDTH), lambda j: (j, 0))
message_block = pl.BlockSpec((8 * SEQ, HALF), lambda j: (0, j))
rows_shape = jax.ShapeDtypeStruct((ROWS, WIDTH), BF)
message_shape = jax.ShapeDtypeStruct((8 * SEQ, PLACES * HALF), BF)


def pack_call(*arrays):
    return pl.pallas_call(
        pack_kernel,
        grid=(PLACES,),
        in_specs=[place_block] * 4,
        out_specs=message_block,
        out_shape=message_shape,
        compiler_params=params(60),
        cost_estimate=cost(4),
        name="pack",
    )(*arrays)


def unpack_call(message):
    return pl.pallas_call(
        unpack_kernel,
        grid=(PLACES,),
        in_specs=[message_block],
        out_specs=[place_block] * 4,
        out_shape=[rows_shape] * 4,
        compiler_params=params(60),
        cost_estimate=cost(4),
        name="unpack",
    )(message)


def pair(ref, n):
    at = 2 * HEAD * n
    return jnp.concatenate([ref[:, at : at + HEAD], ref[:, at + HEAD : at + 2 * HEAD]], axis=0)


def put_pair(ref, n, value):
    at = 2 * HEAD * n
    ref[:, at : at + HEAD] = value[:FRAMES]
    ref[:, at + HEAD : at + 2 * HEAD] = value[FRAMES:]


def forward_kernel(mask_ref, in_ref, q, k, v, g, mixed, probs_ref):
    unpack(in_ref, (q, k, v, g))
    allowed = mask_ref[...] > 0.5
    for n in range(HEADS // 2):
        logits = dot(pair(k, n), pair(q, n), ((1,), (1,))) * FACTOR
        logits = jnp.where(allowed, logits, F32(-1e30))
        shifted = jnp.exp(logits - jnp.max(logits, axis=0, keepdims=True))
        probs = shifted * (1 / jnp.sum(shifted, axis=0, keepdims=True))
        probs_ref[n] = probs
        put_pair(mixed, n, dot(probs.astype(BF), pair(v, n), ((0,), (0,))).astype(BF))


probs_block = pl.BlockSpec((HEADS // 2, 2 * FRAMES, 2 * FRAMES), lambda j: (j, 0, 0))


def forward_call(mask, message):
    return pl.pallas_call(
        forward_kernel,
        grid=(PLACES,),
        in_specs=[pl.BlockSpec((128, 128), lambda j: (0, 0)), message_block],
        out_specs=[place_block] * 5 + [probs_block],
        out_shape=[rows_shape] * 5 + [jax.ShapeDtypeStruct((HEADS // 2 * PLACES, 128, 128), F32)],
        compiler_params=params(14),
        cost_estimate=cost(6),
        name="forward",
    )(mask, message)


def strip_copies(at, copy):
    for side in range(2):
        core = at[0] if side == 0 else 1 - at[0]
        for dy in range(NY):
            for dz in range(NZ):
                y, z = (at[2] + dy) % NY, at[3] ^ dz
                there = pl.multiple_of((y * NZ + z) * 2 * STRIP + core * STRIP, 8)
                copy(side, (dy * NZ + dz) * STRIP, there)


def weight_kernel(at, mixed, grad, keep, send, ordered, turned, strips):
    @pl.when(pl.program_id(0) == 0)
    def _():
        turned[...] = mixed[...].astype(F32).T

        def copy(side, here, there):
            strips[side, here : here + STRIP, :] = turned[pl.ds(there, STRIP), :]

        strip_copies(at, copy)
        for side in range(2):
            ordered[:, HALF * side : HALF * side + HALF] = strips[side].T.astype(BF)

    for side, out in ((0, keep), (1, send)):
        out[0] = dot(strips[side].astype(BF), grad[...]).astype(BF)


def weight_call(at, mixed, grad):
    return pl.pallas_call(
        weight_kernel,
        grid_spec=pltpu.PrefetchScalarGridSpec(
            num_scalar_prefetch=1,
            grid=(NX,),
            in_specs=[
                pl.BlockSpec((ROWS, WIDTH), lambda d, at: (0, 0)),
                pl.BlockSpec((ROWS, QUARTER), lambda d, at: (0, (at[1] + d) % NX)),
            ],
            out_specs=[pl.BlockSpec((1, HALF, QUARTER), lambda d, at: (d, 0, 0))] * 2
            + [pl.BlockSpec((ROWS, WIDTH), lambda d, at: (0, 0))],
            scratch_shapes=[pltpu.VMEM((WIDTH, ROWS), F32), pltpu.VMEM((2, HALF, ROWS), F32)],
        ),
        out_shape=[jax.ShapeDtypeStruct((NX, HALF, QUARTER), BF)] * 2 + [rows_shape],
        compiler_params=params(16),
        cost_estimate=cost(4),
        name="weight",
    )(at, mixed, grad)


PIECES = ((0, 0, HALF), (-1, 0, HALF), (1, 0, HALF), (2, 0, HALF // 2), (2, HALF // 2, HALF // 2))


def project_kernel(at, ordered, grad, *refs):
    weights, (out, mixed_grad, strips, turned) = refs[: 2 * len(PIECES)], refs[2 * len(PIECES) :]
    totals = {}
    for n, (shift, start, size) in enumerate(PIECES):
        cols = pl.ds(pl.multiple_of((at[1] + shift + NX) % NX * QUARTER, QUARTER), QUARTER)
        part = None
        for side in range(2):
            w = weights[side * len(PIECES) + n][...]
            term = dot(ordered[:, HALF * side + start : HALF * side + start + size], w)
            part = term if part is None else part + term
            turn = dot(w, grad[:, cols], ((1,), (1,)))
            rows = slice(start, start + size)
            if n == 0:
                strips[side, rows, :] = turn
            else:
                strips[side, rows, :] += turn
        totals[shift] = totals[shift] + part if shift in totals else part
        if start + size == HALF:
            out[:, cols] = totals[shift].astype(BF)

    def copy(side, here, there):
        turned[pl.ds(there, STRIP), :] = strips[side, here : here + STRIP, :]

    strip_copies(at, copy)
    mixed_grad[...] = turned[...].T.astype(BF)


def project_call(at, ordered, grad, weights):
    vmem = pl.BlockSpec(memory_space=pltpu.VMEM)
    return pl.pallas_call(
        project_kernel,
        in_specs=[pl.BlockSpec(memory_space=pltpu.SMEM)] + [vmem] * (2 + 2 * len(PIECES)),
        out_specs=[vmem] * 2,
        out_shape=[rows_shape] * 2,
        scratch_shapes=[pltpu.VMEM((2, HALF, ROWS), F32), pltpu.VMEM((WIDTH, ROWS), F32)],
        compiler_params=params(24),
        cost_estimate=cost(6),
        name="project",
    )(at, ordered, grad, *weights)


def backward_kernel(q, k, v, mixed_grad, out, probs_ref, message, q_grad, k_grad, v_grad):
    for n in range(HEADS // 2):
        probs = probs_ref[n]
        probs_low = probs.astype(BF)
        grad = pair(mixed_grad, n)
        put_pair(v_grad, n, dot(probs_low, grad).astype(BF))
        through = dot(pair(v, n), grad, ((1,), (1,)))
        inner = jnp.sum(probs_low.astype(F32) * through, axis=0, keepdims=True)
        score = (probs * (through - inner)).astype(BF)
        put_pair(q_grad, n, (dot(score, pair(k, n), ((0,), (0,))) * FACTOR).astype(BF))
        put_pair(k_grad, n, (dot(score, pair(q, n)) * FACTOR).astype(BF))
    pack((out, q_grad, k_grad, v_grad), message)


def backward_call(*arrays):
    return pl.pallas_call(
        backward_kernel,
        grid=(PLACES,),
        in_specs=[place_block] * 5 + [probs_block],
        out_specs=message_block,
        out_shape=message_shape,
        scratch_shapes=[pltpu.VMEM((FRAMES, WIDTH), BF)] * 3,
        compiler_params=params(14),
        cost_estimate=cost(6),
        name="backward",
    )(*arrays)


def seq_shift(dy, dz, dc):
    seq = np.arange(SEQ).reshape(NY, NZ, 2)
    return [
        (int(seq[y, z, c]), int(seq[(y + dy) % NY, (z + dz) % NZ, c ^ dc]))
        for y in range(NY)
        for z in range(NZ)
        for c in range(2)
    ]


def seq_flip(bit):
    seq = np.arange(SEQ).reshape(NY, NZ, 2)
    return [
        (int(seq[y, z, c]), int(seq[y, z ^ bit, c])) for y in range(NY) for z in range(NZ) for c in range(2)
    ]


def add_up(parts):
    total = parts[0].astype(F32)
    for part in parts[1:]:
        total = total + part.astype(F32)
    return total


def reduce_chip(keep, came):
    return [add_up([keep[d], came[d]]).astype(BF) for d in range(NX)]


def along_x(x, shift):
    return lax.ppermute(x, "dp", [(i, (i + shift) % NX) for i in range(NX)])


def reduce_x_first(parts):
    mid = HALF // 2
    return along_x(parts[2][:mid], 1), along_x(parts[2][mid:], -1)


def reduce_x_second(parts, right, left):
    mid = HALF // 2
    ahead = jnp.concatenate([add_up([parts[1][:mid], right]).astype(BF), parts[1][mid:]], axis=0)
    back = jnp.concatenate([parts[3][:mid], add_up([parts[3][mid:], left]).astype(BF)], axis=0)
    return add_up([parts[0], along_x(ahead, 1), along_x(back, -1)]).astype(BF)


def reduce_rest(chip):
    chip = chip.reshape(NY, NZ * STRIP, QUARTER)
    came = [lax.ppermute(chip[d], "seq", seq_shift(d, 0, 0)) for d in (1, 3, 2)]
    strips = add_up([chip[0]] + came).astype(BF).reshape(NZ, STRIP, QUARTER)
    for bit in (4, 2, 1):
        came = lax.ppermute(strips[bit:], "seq", seq_flip(bit))
        strips = add_up([strips[:bit], came])
        if bit > 1:
            strips = strips.astype(BF)
    own = strips[0]
    came = {d: along_x(own, d) for d in (1, 3, 2)}
    place = lax.axis_index("dp")
    quarters = [lax.select_n((place - n) % NX, own, came[1], came[2], came[3]) for n in range(NX)]
    return jnp.concatenate(quarters, axis=1)


def gather_weight(out_weight):
    place = lax.axis_index("dp")
    own = lax.select_n(place, *[out_weight[:, QUARTER * n : QUARTER * n + QUARTER] for n in range(NX)])
    own = own[None]
    for bit in (1, 2, 4):
        own = jnp.concatenate([own, lax.ppermute(own, "seq", seq_flip(bit))], axis=0)
    own = own.reshape(NZ * STRIP, QUARTER)
    came = {d: lax.ppermute(own, "seq", seq_shift(NY - d, 0, 0)) for d in (1, 3, 2)}
    own = jnp.concatenate([own, came[1], came[2], came[3]], axis=0)
    mid = HALF // 2
    left, right = along_x(own, 1), along_x(own, -1)
    pieces = [own, left, right, along_x(left[:mid], 1), along_x(right[mid:], -1)]
    return pieces + [lax.ppermute(piece, "seq", seq_shift(0, 0, 1)) for piece in pieces]


def exchange(message):
    return lax.all_to_all(message, "seq", split_axis=0, concat_axis=0, tiled=True)


def local(queries, key_field, value_field, out_grad, out_weight, frame_video):
    videos = frame_video[0]
    same = jnp.tile((videos[:, None] == videos[None, :]), (2, 2))
    head = jnp.arange(2 * FRAMES) // FRAMES
    mask = (same & (head[:, None] == head[None, :])).astype(F32)
    rank = lax.axis_index("seq")
    at = jnp.stack([rank % 2, lax.axis_index("dp"), rank // (2 * NZ), rank // 2 % NZ]).astype(jnp.int32)

    flat = [x.reshape(ROWS, WIDTH) for x in (queries, key_field, value_field, out_grad)]
    message, out_weight = lax.optimization_barrier((pack_call(*flat), out_weight))
    weights = gather_weight(out_weight)
    arrived, weights = lax.optimization_barrier((exchange(message), weights))
    q, k, v, g, mixed, probs = forward_call(mask, arrived)
    keep, send, ordered = weight_call(at, mixed, g)
    parts = reduce_chip(keep, lax.ppermute(send, "seq", seq_shift(0, 0, 1)))
    out, mixed_grad = project_call(at, ordered, g, weights)
    parts, mixed_grad = lax.optimization_barrier((parts, mixed_grad))
    right, left = reduce_x_first(parts)
    message = backward_call(q, k, v, mixed_grad, out, probs)
    message, right, left = lax.optimization_barrier((message, right, left))
    chip = reduce_x_second(parts, right, left)
    results = unpack_call(exchange(message))
    weight_grad = reduce_rest(chip)
    return tuple(x.reshape(queries.shape) for x in results) + (weight_grad,)


def solution(mesh):
    placed = P("dp", "seq", None, None)
    return jax.shard_map(
        local,
        mesh=mesh,
        in_specs=(placed, placed, placed, placed, P("seq", None), P("dp", None)),
        out_specs=(placed, placed, placed, placed, P("seq", None)),
        check_vma=False,
    )
```

```python
import functools

import jax
import jax.numpy as jnp
import numpy as np
from jax import lax
from jax.experimental import pallas as pl
from jax.experimental.pallas import tpu as pltpu
from jax.sharding import PartitionSpec as P

HEAD = 128
HEADS = 12
WIDTH = HEAD * HEADS
HALF = WIDTH // 2
FRAMES = 64
PLACES = 3
ROWS = FRAMES * PLACES
NX, NY, NZ = 4, 4, 8
SEQ = NY * NZ * 2
STRIP = WIDTH // SEQ
QUARTER = WIDTH // NX
BF = jnp.bfloat16
F32 = jnp.float32
FACTOR = HEAD ** (-0.5)
MIB = 1 << 20


def params(mib):
    return pltpu.CompilerParams(vmem_limit_bytes=mib * MIB)


def cost(us):
    return pl.CostEstimate(flops=0, bytes_accessed=int(us * 3.5e6), transcendentals=0)


def dot(a, b, dims=((1,), (0,))):
    return lax.dot_general(a, b, (dims, ((), ())), preferred_element_type=F32)


def swap_matrix(to_blocks):
    a = lax.broadcasted_iota(jnp.int32, (256, 256), 0 if to_blocks else 1)
    b = lax.broadcasted_iota(jnp.int32, (256, 256), 1 if to_blocks else 0)
    return jnp.where(8 * (a % 32) + a // 32 == b, F32(1), F32(0)).astype(BF)


def pack(sources, out_ref):
    swap = swap_matrix(False)
    for half in range(2):
        for tile in range(HALF // 256):
            parts = [
                src[32 * half : 32 * half + 32, HALF * e + 256 * tile : HALF * e + 256 * tile + 256]
                for src in sources
                for e in range(2)
            ]
            mixed = dot(swap, jnp.concatenate(parts, axis=0))
            out_ref[256 * half : 256 * half + 256, 256 * tile : 256 * tile + 256] = mixed.astype(BF)


def unpack(in_ref, sinks):
    swap = swap_matrix(True)
    for half in range(2):
        for tile in range(HALF // 256):
            piece = in_ref[256 * half : 256 * half + 256, 256 * tile : 256 * tile + 256]
            rows = dot(swap, piece).astype(BF)
            for n in range(8):
                col = HALF * (n % 2) + 256 * tile
                sinks[n // 2][32 * half : 32 * half + 32, col : col + 256] = rows[32 * n : 32 * n + 32]


def pack_kernel(a, b, c, d, out_ref):
    pack((a, b, c, d), out_ref)


def unpack_kernel(in_ref, a, b, c, d):
    unpack(in_ref, (a, b, c, d))


place_block = pl.BlockSpec((FRAMES, WIDTH), lambda j: (j, 0))
message_block = pl.BlockSpec((8 * SEQ, HALF), lambda j: (0, j))
rows_shape = jax.ShapeDtypeStruct((ROWS, WIDTH), BF)
message_shape = jax.ShapeDtypeStruct((8 * SEQ, PLACES * HALF), BF)


def pack_call(*arrays):
    return pl.pallas_call(
        pack_kernel,
        grid=(PLACES,),
        in_specs=[place_block] * 4,
        out_specs=message_block,
        out_shape=message_shape,
        compiler_params=params(60),
        cost_estimate=cost(4),
        name="pack",
    )(*arrays)


def unpack_call(message):
    return pl.pallas_call(
        unpack_kernel,
        grid=(PLACES,),
        in_specs=[message_block],
        out_specs=[place_block] * 4,
        out_shape=[rows_shape] * 4,
        compiler_params=params(10),
        cost_estimate=cost(4),
        name="unpack",
    )(message)


def pair(ref, n):
    at = 2 * HEAD * n
    return jnp.concatenate([ref[:, at : at + HEAD], ref[:, at + HEAD : at + 2 * HEAD]], axis=0)


def put_pair(ref, n, value):
    at = 2 * HEAD * n
    ref[:, at : at + HEAD] = value[:FRAMES]
    ref[:, at + HEAD : at + 2 * HEAD] = value[FRAMES:]


def forward_kernel(mask_ref, in_ref, q, k, v, g, mixed, probs_ref):
    unpack(in_ref, (q, k, v, g))
    allowed = mask_ref[...] > 0.5
    for n in range(HEADS // 2):
        logits = dot(pair(k, n), pair(q, n), ((1,), (1,))) * FACTOR
        logits = jnp.where(allowed, logits, F32(-1e30))
        shifted = jnp.exp(logits - jnp.max(logits, axis=0, keepdims=True))
        probs = shifted * (1 / jnp.sum(shifted, axis=0, keepdims=True))
        probs_ref[n] = probs
        put_pair(mixed, n, dot(probs.astype(BF), pair(v, n), ((0,), (0,))).astype(BF))


probs_block = pl.BlockSpec((HEADS // 2, 2 * FRAMES, 2 * FRAMES), lambda j: (j, 0, 0))


def forward_call(mask, message):
    return pl.pallas_call(
        forward_kernel,
        grid=(PLACES,),
        in_specs=[pl.BlockSpec((128, 128), lambda j: (0, 0)), message_block],
        out_specs=[place_block] * 5 + [probs_block],
        out_shape=[rows_shape] * 5 + [jax.ShapeDtypeStruct((HEADS // 2 * PLACES, 128, 128), F32)],
        compiler_params=params(14),
        cost_estimate=cost(6),
        name="forward",
    )(mask, message)


def strip_copies(at, copy):
    for side in range(2):
        core = at[0] if side == 0 else 1 - at[0]
        for dy in range(NY):
            for z in range(NZ):
                y = (at[2] + dy) % NY
                there = pl.multiple_of((y * NZ + z) * 2 * STRIP + core * STRIP, 8)
                copy(side, (dy * NZ + z) * STRIP, there)


def weight_kernel(at, mixed, grad, keep, send, ordered, turned, strips):
    @pl.when(pl.program_id(0) == 0)
    def _():
        turned[...] = mixed[...].astype(F32).T

        def copy(side, here, there):
            strips[side, here : here + STRIP, :] = turned[pl.ds(there, STRIP), :]

        strip_copies(at, copy)
        for side in range(2):
            ordered[:, HALF * side : HALF * side + HALF] = strips[side].T.astype(BF)

    for side, out in ((0, keep), (1, send)):
        out[0] = dot(strips[side].astype(BF), grad[...]).astype(BF)


def weight_call(at, mixed, grad):
    return pl.pallas_call(
        weight_kernel,
        grid_spec=pltpu.PrefetchScalarGridSpec(
            num_scalar_prefetch=1,
            grid=(NX,),
            in_specs=[
                pl.BlockSpec((ROWS, WIDTH), lambda d, at: (0, 0)),
                pl.BlockSpec((ROWS, QUARTER), lambda d, at: (0, (at[1] + d) % NX)),
            ],
            out_specs=[pl.BlockSpec((1, HALF, QUARTER), lambda d, at: (d, 0, 0))] * 2
            + [pl.BlockSpec((ROWS, WIDTH), lambda d, at: (0, 0))],
            scratch_shapes=[pltpu.VMEM((WIDTH, ROWS), F32), pltpu.VMEM((2, HALF, ROWS), F32)],
        ),
        out_shape=[jax.ShapeDtypeStruct((NX, HALF, QUARTER), BF)] * 2 + [rows_shape],
        compiler_params=params(16),
        cost_estimate=cost(4),
        name="weight",
    )(at, mixed, grad)


PIECES = ((0, 0, HALF), (-1, 0, HALF), (1, 0, HALF), (2, 0, HALF // 2), (2, HALF // 2, HALF // 2))


def project_kernel(at, ordered, grad, *refs):
    weights, (out, mixed_grad, strips, turned) = refs[: 2 * len(PIECES)], refs[2 * len(PIECES) :]
    totals = {}
    for n, (shift, start, size) in enumerate(PIECES):
        cols = pl.ds(pl.multiple_of((at[1] + shift + NX) % NX * QUARTER, QUARTER), QUARTER)
        part = None
        for side in range(2):
            w = weights[side * len(PIECES) + n][...]
            term = dot(ordered[:, HALF * side + start : HALF * side + start + size], w)
            part = term if part is None else part + term
            turn = dot(w, grad[:, cols], ((1,), (1,)))
            rows = slice(start, start + size)
            if n == 0:
                strips[side, rows, :] = turn
            else:
                strips[side, rows, :] += turn
        totals[shift] = totals[shift] + part if shift in totals else part
        if start + size == HALF:
            out[:, cols] = totals[shift].astype(BF)

    def copy(side, here, there):
        turned[pl.ds(there, STRIP), :] = strips[side, here : here + STRIP, :]

    strip_copies(at, copy)
    mixed_grad[...] = turned[...].T.astype(BF)


def project_call(at, ordered, grad, weights):
    vmem = pl.BlockSpec(memory_space=pltpu.VMEM)
    return pl.pallas_call(
        project_kernel,
        in_specs=[pl.BlockSpec(memory_space=pltpu.SMEM)] + [vmem] * (2 + 2 * len(PIECES)),
        out_specs=[vmem] * 2,
        out_shape=[rows_shape] * 2,
        scratch_shapes=[pltpu.VMEM((2, HALF, ROWS), F32), pltpu.VMEM((WIDTH, ROWS), F32)],
        compiler_params=params(24),
        cost_estimate=cost(6),
        name="project",
    )(at, ordered, grad, *weights)


def backward_kernel(q, k, v, mixed_grad, out, probs_ref, message, q_grad, k_grad, v_grad):
    for n in range(HEADS // 2):
        probs = probs_ref[n]
        probs_low = probs.astype(BF)
        grad = pair(mixed_grad, n)
        put_pair(v_grad, n, dot(probs_low, grad).astype(BF))
        through = dot(pair(v, n), grad, ((1,), (1,)))
        inner = jnp.sum(probs_low.astype(F32) * through, axis=0, keepdims=True)
        score = (probs * (through - inner)).astype(BF)
        put_pair(q_grad, n, (dot(score, pair(k, n), ((0,), (0,))) * FACTOR).astype(BF))
        put_pair(k_grad, n, (dot(score, pair(q, n)) * FACTOR).astype(BF))
    pack((out, q_grad, k_grad, v_grad), message)


def backward_call(*arrays):
    return pl.pallas_call(
        backward_kernel,
        grid=(PLACES,),
        in_specs=[place_block] * 5 + [probs_block],
        out_specs=message_block,
        out_shape=message_shape,
        scratch_shapes=[pltpu.VMEM((FRAMES, WIDTH), BF)] * 3,
        compiler_params=params(14),
        cost_estimate=cost(6),
        name="backward",
    )(*arrays)


def seq_shift(dy, dz, dc):
    seq = np.arange(SEQ).reshape(NY, NZ, 2)
    return [
        (int(seq[y, z, c]), int(seq[(y + dy) % NY, (z + dz) % NZ, c ^ dc]))
        for y in range(NY)
        for z in range(NZ)
        for c in range(2)
    ]


def seq_flip(bit):
    seq = np.arange(SEQ).reshape(NY, NZ, 2)
    return [
        (int(seq[y, z, c]), int(seq[y, z ^ bit, c])) for y in range(NY) for z in range(NZ) for c in range(2)
    ]


def add_up(parts):
    total = parts[0].astype(F32)
    for part in parts[1:]:
        total = total + part.astype(F32)
    return total


def reduce_chip(keep, came):
    return [add_up([keep[d], came[d]]).astype(BF) for d in range(NX)]


def along_x(x, shift):
    return lax.ppermute(x, "dp", [(i, (i + shift) % NX) for i in range(NX)])


def reduce_x_first(parts):
    mid = HALF // 2
    return along_x(parts[2][:mid], 1), along_x(parts[2][mid:], -1)


def reduce_x_second(parts, right, left):
    mid = HALF // 2
    ahead = jnp.concatenate([add_up([parts[1][:mid], right]).astype(BF), parts[1][mid:]], axis=0)
    back = jnp.concatenate([parts[3][:mid], add_up([parts[3][mid:], left]).astype(BF)], axis=0)
    return add_up([parts[0], along_x(ahead, 1), along_x(back, -1)]).astype(BF)


def reduce_y(chip):
    chip = chip.reshape(NY, NZ * STRIP, QUARTER)
    came = [lax.ppermute(chip[d], "seq", seq_shift(d, 0, 0)) for d in (1, 3, 2)]
    return add_up([chip[0]] + came).astype(BF).reshape(NZ // 2, 2, STRIP, QUARTER)


def reduce_z_pairs(pairs):
    at = lax.axis_index("seq") // 4 % (NZ // 2)
    pick = lambda n: lax.dynamic_index_in_dim(pairs, at ^ n, 0, keepdims=False)
    came = [lax.ppermute(pick(n), "seq", seq_flip(2 * n)) for n in (2, 1, 3)]
    return add_up([pick(0)] + came).astype(BF)


def reduce_z_last(pair):
    odd = lax.axis_index("seq") // 2 % 2 == 1
    came = lax.ppermute(jnp.where(odd, pair[0], pair[1]), "seq", seq_flip(1))
    return add_up([jnp.where(odd, pair[1], pair[0]), came])


def gather_x(own):
    flip = lambda x, n: lax.ppermute(x, "dp", [(i, i ^ n) for i in range(NX)])
    near = flip(own, 1)
    far = flip(jnp.stack([own, near]), 2)
    place = lax.axis_index("dp")
    quarters = [lax.select_n(place ^ n, own, near, far[0], far[1]) for n in range(NX)]
    return jnp.concatenate(quarters, axis=1)


def gather_weight_y(out_weight):
    place = lax.axis_index("dp")
    own = lax.select_n(place, *[out_weight[:, QUARTER * n : QUARTER * n + QUARTER] for n in range(NX)])
    came = {d: lax.ppermute(own, "seq", seq_shift(NY - d, 0, 0)) for d in (1, 3, 2)}
    return jnp.concatenate([own, came[1], came[2], came[3]], axis=0)


def gather_weight_z(part):
    seq = np.arange(SEQ).reshape(NY, NZ * 2)
    part = lax.all_gather(part, "seq", axis=0, axis_index_groups=[list(map(int, row)) for row in seq])
    part = part.reshape(NZ, 2, NY, STRIP, QUARTER).transpose(1, 2, 0, 3, 4).reshape(2, HALF, QUARTER)
    first = lax.axis_index("seq") % 2 == 0
    return jnp.where(first, part[0], part[1]), jnp.where(first, part[1], part[0])


def swap_cores(x):
    return lax.ppermute(x, "seq", seq_shift(0, 0, 1))


def exchange(message):
    return lax.all_to_all(message, "seq", split_axis=0, concat_axis=0, tiled=True)


def local(queries, key_field, value_field, out_grad, out_weight, frame_video):
    videos = frame_video[0]
    same = jnp.tile((videos[:, None] == videos[None, :]), (2, 2))
    head = jnp.arange(2 * FRAMES) // FRAMES
    mask = (same & (head[:, None] == head[None, :])).astype(F32)
    rank = lax.axis_index("seq")
    at = jnp.stack([rank % 2, lax.axis_index("dp"), rank // (2 * NZ), rank // 2 % NZ]).astype(jnp.int32)

    flat = [x.reshape(ROWS, WIDTH) for x in (queries, key_field, value_field, out_grad)]
    message, part = lax.optimization_barrier((pack_call(*flat), gather_weight_y(out_weight)))
    own, other = gather_weight_z(part)
    left, right = along_x(own, 1), along_x(own, -1)
    arrived, mask, own, other, left, right = lax.optimization_barrier(
        (exchange(message), mask, own, other, left, right)
    )
    mid = HALF // 2
    pieces = [left, right, along_x(left[:mid], 1), along_x(right[mid:], -1)]
    q, k, v, g, mixed, probs = forward_call(mask, arrived)
    mixed, pieces = lax.optimization_barrier((mixed, pieces))
    keep, send, ordered = weight_call(at, mixed, g)
    weights = [own] + pieces + [other] + [swap_cores(piece) for piece in pieces]
    parts = reduce_chip(keep, swap_cores(send))
    out, mixed_grad = project_call(at, ordered, g, weights)
    parts, mixed_grad = lax.optimization_barrier((parts, mixed_grad))
    right, left = reduce_x_first(parts)
    message = backward_call(q, k, v, mixed_grad, out, probs)
    message, right, left = lax.optimization_barrier((message, right, left))
    pair = reduce_z_pairs(reduce_y(reduce_x_second(parts, right, left)))
    came, pair = lax.optimization_barrier((exchange(message), pair))
    results = unpack_call(came)
    weight_grad = gather_x(reduce_z_last(pair))
    return tuple(x.reshape(queries.shape) for x in results) + (weight_grad,)


def solution(mesh):
    placed = P("dp", "seq", None, None)
    return jax.shard_map(
        local,
        mesh=mesh,
        in_specs=(placed, placed, placed, placed, P("seq", None), P("dp", None)),
        out_specs=(placed, placed, placed, placed, P("seq", None)),
        check_vma=False,
    )
```

```python
import functools

import jax
import jax.numpy as jnp
import numpy as np
from jax import lax
from jax.experimental import pallas as pl
from jax.experimental.pallas import tpu as pltpu
from jax.sharding import PartitionSpec as P

HEAD = 128
HEADS = 12
WIDTH = HEAD * HEADS
HALF = WIDTH // 2
FRAMES = 64
PLACES = 3
ROWS = FRAMES * PLACES
NX, NY, NZ = 4, 4, 8
SEQ = NY * NZ * 2
STRIP = WIDTH // SEQ
QUARTER = WIDTH // NX
BF = jnp.bfloat16
F32 = jnp.float32
FACTOR = HEAD ** (-0.5)
MIB = 1 << 20


def params(mib):
    return pltpu.CompilerParams(vmem_limit_bytes=mib * MIB)


def cost(us):
    return pl.CostEstimate(flops=0, bytes_accessed=int(us * 3.5e6), transcendentals=0)


def dot(a, b, dims=((1,), (0,))):
    return lax.dot_general(a, b, (dims, ((), ())), preferred_element_type=F32)


def swap_matrix(to_blocks):
    a = lax.broadcasted_iota(jnp.int32, (256, 256), 0 if to_blocks else 1)
    b = lax.broadcasted_iota(jnp.int32, (256, 256), 1 if to_blocks else 0)
    return jnp.where(8 * (a % 32) + a // 32 == b, F32(1), F32(0)).astype(BF)


def pack(sources, place, out_ref):
    swap = swap_matrix(False)
    for half in range(2):
        rows = slice(FRAMES * place + 32 * half, FRAMES * place + 32 * half + 32)
        for tile in range(HALF // 256):
            parts = [
                src[rows, HALF * e + 256 * tile : HALF * e + 256 * tile + 256]
                for src in sources
                for e in range(2)
            ]
            mixed = dot(swap, jnp.concatenate(parts, axis=0))
            out_ref[256 * half : 256 * half + 256, 256 * tile : 256 * tile + 256] = mixed.astype(BF)


def unpack(in_ref, place, sinks):
    swap = swap_matrix(True)
    for half in range(2):
        rows = slice(FRAMES * place + 32 * half, FRAMES * place + 32 * half + 32)
        for tile in range(HALF // 256):
            at = HALF * place + 256 * tile
            piece = dot(swap, in_ref[256 * half : 256 * half + 256, at : at + 256]).astype(BF)
            for n in range(8):
                col = HALF * (n % 2) + 256 * tile
                sinks[n // 2][rows, col : col + 256] = piece[32 * n : 32 * n + 32]


def place_rows(place):
    return pl.ds(FRAMES * place, FRAMES)


def message_copy(staged, message, sems, place):
    return pltpu.make_async_copy(
        staged.at[place], message.at[:, pl.ds(HALF * place, HALF)], sems.at[place]
    )


def pack_kernel(a, b, c, d, message, *scratch):
    held, staged, in_sems, out_sems = scratch[:4], scratch[4], scratch[5], scratch[6]
    arrays = (a, b, c, d)
    came = [
        [
            pltpu.make_async_copy(
                src.at[place_rows(j)], dst.at[place_rows(j)], in_sems.at[4 * j + n]
            )
            for n, (src, dst) in enumerate(zip(arrays, held))
        ]
        for j in range(PLACES)
    ]
    for copies in came:
        for copy in copies:
            copy.start()
    for j in range(PLACES):
        for copy in came[j]:
            copy.wait()
        pack(held, j, staged.at[j])
        message_copy(staged, message, out_sems, j).start()
    for j in range(PLACES):
        message_copy(staged, message, out_sems, j).wait()


def unpack_kernel(in_ref, a, b, c, d, *scratch):
    held, sems = scratch[:4], scratch[4]
    arrays = (a, b, c, d)
    gone = [
        [
            pltpu.make_async_copy(src.at[place_rows(j)], dst.at[place_rows(j)], sems.at[4 * j + n])
            for n, (dst, src) in enumerate(zip(arrays, held))
        ]
        for j in range(PLACES)
    ]
    for j in range(PLACES):
        unpack(in_ref, j, held)
        for copy in gone[j]:
            copy.start()
    for copies in gone:
        for copy in copies:
            copy.wait()


VMEM = pl.BlockSpec(memory_space=pltpu.VMEM)
ANY = pl.BlockSpec(memory_space=pl.ANY)
rows_shape = jax.ShapeDtypeStruct((ROWS, WIDTH), BF)
message_shape = jax.ShapeDtypeStruct((8 * SEQ, PLACES * HALF), BF)
rows_held = pltpu.VMEM((ROWS, WIDTH), BF)
message_held = pltpu.VMEM((PLACES, 8 * SEQ, HALF), BF)
probs_shape = jax.ShapeDtypeStruct((HEADS // 2 * PLACES, 2 * FRAMES, 2 * FRAMES), F32)


def pack_call(*arrays):
    return pl.pallas_call(
        pack_kernel,
        in_specs=[ANY] * 4,
        out_specs=ANY,
        out_shape=message_shape,
        scratch_shapes=[rows_held] * 4
        + [message_held, pltpu.SemaphoreType.DMA((4 * PLACES,)), pltpu.SemaphoreType.DMA((PLACES,))],
        compiler_params=params(58),
        cost_estimate=cost(3),
        name="pack",
    )(*arrays)


def unpack_call(message):
    return pl.pallas_call(
        unpack_kernel,
        in_specs=[VMEM],
        out_specs=[ANY] * 4,
        out_shape=[rows_shape] * 4,
        scratch_shapes=[rows_held] * 4 + [pltpu.SemaphoreType.DMA((4 * PLACES,))],
        compiler_params=params(12),
        cost_estimate=cost(3),
        name="unpack",
    )(message)


def pair(ref, place, n):
    at, rows = 2 * HEAD * n, slice(FRAMES * place, FRAMES * place + FRAMES)
    return jnp.concatenate([ref[rows, at : at + HEAD], ref[rows, at + HEAD : at + 2 * HEAD]], axis=0)


def put_pair(ref, place, n, value):
    at, rows = 2 * HEAD * n, slice(FRAMES * place, FRAMES * place + FRAMES)
    ref[rows, at : at + HEAD] = value[:FRAMES]
    ref[rows, at + HEAD : at + 2 * HEAD] = value[FRAMES:]


def forward_kernel(mask_ref, in_ref, q, k, v, g, mixed, probs_ref):
    allowed = mask_ref[...] > 0.5
    for j in range(PLACES):
        unpack(in_ref, j, (q, k, v, g))
        for n in range(HEADS // 2):
            logits = dot(pair(k, j, n), pair(q, j, n), ((1,), (1,))) * FACTOR
            logits = jnp.where(allowed, logits, F32(-1e30))
            shifted = jnp.exp(logits - jnp.max(logits, axis=0, keepdims=True))
            probs = shifted * (1 / jnp.sum(shifted, axis=0, keepdims=True))
            probs_ref[HEADS // 2 * j + n] = probs
            put_pair(mixed, j, n, dot(probs.astype(BF), pair(v, j, n), ((0,), (0,))).astype(BF))


def forward_call(mask, message):
    return pl.pallas_call(
        forward_kernel,
        in_specs=[VMEM] * 2,
        out_specs=[VMEM] * 6,
        out_shape=[rows_shape] * 5 + [probs_shape],
        compiler_params=params(8),
        cost_estimate=cost(5),
        name="forward",
    )(mask, message)


def strip_copies(at, copy):
    for side in range(2):
        core = at[0] if side == 0 else 1 - at[0]
        for dy in range(NY):
            for z in range(NZ):
                y = (at[2] + dy) % NY
                there = pl.multiple_of((y * NZ + z) * 2 * STRIP + core * STRIP, 8)
                copy(side, (dy * NZ + z) * STRIP, there)


def weight_kernel(at, mixed, grad, keep, send, ordered, turned, strips):
    turned[...] = mixed[...].astype(F32).T

    def copy(side, here, there):
        strips[side, here : here + STRIP, :] = turned[pl.ds(there, STRIP), :]

    strip_copies(at, copy)
    for side, out in ((1, send), (0, keep)):
        rows = strips[side]
        ordered[:, HALF * side : HALF * side + HALF] = rows.T.astype(BF)
        rows = rows.astype(BF)
        for d in range(NX):
            cols = pl.ds(pl.multiple_of((at[1] + d) % NX * QUARTER, QUARTER), QUARTER)
            out[d] = dot(rows, grad[:, cols]).astype(BF)


def weight_call(at, mixed, grad):
    return pl.pallas_call(
        weight_kernel,
        in_specs=[pl.BlockSpec(memory_space=pltpu.SMEM), VMEM, VMEM],
        out_specs=[VMEM] * 3,
        scratch_shapes=[pltpu.VMEM((WIDTH, ROWS), F32), pltpu.VMEM((2, HALF, ROWS), F32)],
        out_shape=[jax.ShapeDtypeStruct((NX, HALF, QUARTER), BF)] * 2 + [rows_shape],
        compiler_params=params(12),
        cost_estimate=cost(4),
        name="weight",
    )(at, mixed, grad)


PIECES = ((0, 0, HALF), (-1, 0, HALF), (1, 0, HALF), (2, 0, HALF // 2), (2, HALF // 2, HALF // 2))


def project_kernel(at, ordered, grad, *refs):
    weights, (out, mixed_grad, strips, turned) = refs[: 2 * len(PIECES)], refs[2 * len(PIECES) :]
    totals = {}
    for n, (shift, start, size) in enumerate(PIECES):
        cols = pl.ds(pl.multiple_of((at[1] + shift + NX) % NX * QUARTER, QUARTER), QUARTER)
        part = None
        for side in range(2):
            w = weights[side * len(PIECES) + n][...]
            term = dot(ordered[:, HALF * side + start : HALF * side + start + size], w)
            part = term if part is None else part + term
            turn = dot(w, grad[:, cols], ((1,), (1,)))
            rows = slice(start, start + size)
            if n == 0:
                strips[side, rows, :] = turn
            else:
                strips[side, rows, :] += turn
        totals[shift] = totals[shift] + part if shift in totals else part
        if start + size == HALF:
            out[:, cols] = totals[shift].astype(BF)

    def copy(side, here, there):
        turned[pl.ds(there, STRIP), :] = strips[side, here : here + STRIP, :]

    strip_copies(at, copy)
    mixed_grad[...] = turned[...].T.astype(BF)


def project_call(at, ordered, grad, weights):
    return pl.pallas_call(
        project_kernel,
        in_specs=[pl.BlockSpec(memory_space=pltpu.SMEM)] + [VMEM] * (2 + 2 * len(PIECES)),
        out_specs=[VMEM] * 2,
        out_shape=[rows_shape] * 2,
        scratch_shapes=[pltpu.VMEM((2, HALF, ROWS), F32), pltpu.VMEM((WIDTH, ROWS), F32)],
        compiler_params=params(14),
        cost_estimate=cost(5),
        name="project",
    )(at, ordered, grad, *weights)


def backward_kernel(q, k, v, mixed_grad, out, probs_ref, message, *scratch):
    q_grad, k_grad, v_grad, staged, sems = scratch
    for j in range(PLACES):
        for n in range(HEADS // 2):
            probs = probs_ref[HEADS // 2 * j + n]
            probs_low = probs.astype(BF)
            grad = pair(mixed_grad, j, n)
            put_pair(v_grad, j, n, dot(probs_low, grad).astype(BF))
            through = dot(pair(v, j, n), grad, ((1,), (1,)))
            inner = jnp.sum(probs_low.astype(F32) * through, axis=0, keepdims=True)
            score = (probs * (through - inner)).astype(BF)
            put_pair(q_grad, j, n, (dot(score, pair(k, j, n), ((0,), (0,))) * FACTOR).astype(BF))
            put_pair(k_grad, j, n, (dot(score, pair(q, j, n)) * FACTOR).astype(BF))
        pack((out, q_grad, k_grad, v_grad), j, staged.at[j])
        message_copy(staged, message, sems, j).start()
    for j in range(PLACES):
        message_copy(staged, message, sems, j).wait()


def backward_call(*arrays):
    return pl.pallas_call(
        backward_kernel,
        in_specs=[VMEM] * 6,
        out_specs=ANY,
        out_shape=message_shape,
        scratch_shapes=[rows_held] * 3 + [message_held, pltpu.SemaphoreType.DMA((PLACES,))],
        compiler_params=params(14),
        cost_estimate=cost(5),
        name="backward",
    )(*arrays)


def seq_shift(dy, dz, dc):
    seq = np.arange(SEQ).reshape(NY, NZ, 2)
    return [
        (int(seq[y, z, c]), int(seq[(y + dy) % NY, (z + dz) % NZ, c ^ dc]))
        for y in range(NY)
        for z in range(NZ)
        for c in range(2)
    ]


def seq_flip(bit):
    seq = np.arange(SEQ).reshape(NY, NZ, 2)
    return [
        (int(seq[y, z, c]), int(seq[y, z ^ bit, c])) for y in range(NY) for z in range(NZ) for c in range(2)
    ]


def add_up(parts):
    total = parts[0].astype(F32)
    for part in parts[1:]:
        total = total + part.astype(F32)
    return total


def reduce_chip(keep, came):
    return [add_up([keep[d], came[d]]).astype(BF) for d in range(NX)]


def along_x(x, shift):
    return lax.ppermute(x, "dp", [(i, (i + shift) % NX) for i in range(NX)])


def reduce_x_first(parts):
    mid = HALF // 2
    return along_x(parts[2][:mid], 1), along_x(parts[2][mid:], -1)


def reduce_x_second(parts, right, left):
    mid = HALF // 2
    ahead = jnp.concatenate([add_up([parts[1][:mid], right]).astype(BF), parts[1][mid:]], axis=0)
    back = jnp.concatenate([parts[3][:mid], add_up([parts[3][mid:], left]).astype(BF)], axis=0)
    return add_up([parts[0], along_x(ahead, 1), along_x(back, -1)]).astype(BF)


def reduce_y(chip):
    chip = chip.reshape(NY, NZ * STRIP, QUARTER)
    came = [lax.ppermute(chip[d], "seq", seq_shift(d, 0, 0)) for d in (1, 3, 2)]
    return add_up([chip[0]] + came).astype(BF).reshape(NZ, STRIP, QUARTER)


def reduce_z(strips):
    at = lax.axis_index("seq") // 2 % NZ
    pick = lambda n: lax.dynamic_index_in_dim(strips, at ^ n, 0, keepdims=False)
    came = [lax.ppermute(pick(n), "seq", seq_flip(n)) for n in (4, 5, 3, 2, 6, 1, 7)]
    return add_up([pick(0)] + came)


def gather_x(own):
    came = {d: along_x(own, d) for d in (2, 1, 3)}
    place = lax.axis_index("dp")
    quarters = [lax.select_n((place - n) % NX, own, came[1], came[2], came[3]) for n in range(NX)]
    return jnp.concatenate(quarters, axis=1)


def gather_weight_z(out_weight):
    place = lax.axis_index("dp")
    own = lax.select_n(place, *[out_weight[:, QUARTER * n : QUARTER * n + QUARTER] for n in range(NX)])
    came = [lax.ppermute(own, "seq", seq_flip(n)) for n in (4, 2, 6)]
    even = jnp.stack([own, came[1], came[0], came[2]])
    odd = lax.ppermute(even, "seq", seq_flip(1))
    at = lax.axis_index("seq") // 2 % NZ
    both = jnp.stack([even, odd], axis=1).reshape(NZ, STRIP, QUARTER)
    for bit in (1, 2, 4):
        halves = both.reshape(NZ // (2 * bit), 2, bit, STRIP, QUARTER)
        both = jnp.where(at & bit != 0, halves[:, ::-1], halves).reshape(NZ, STRIP, QUARTER)
    return both.reshape(NZ * STRIP, QUARTER)


def gather_weight_y(own):
    came = {d: lax.ppermute(own, "seq", seq_shift(NY - d, 0, 0)) for d in (1, 3, 2)}
    return jnp.concatenate([own, came[1], came[2], came[3]], axis=0)


def swap_cores(x):
    return lax.ppermute(x, "seq", seq_shift(0, 0, 1))


def exchange(message):
    return lax.all_to_all(message, "seq", split_axis=0, concat_axis=0, tiled=True)


def local(queries, key_field, value_field, out_grad, out_weight, frame_video):
    videos = frame_video[0]
    same = jnp.tile((videos[:, None] == videos[None, :]), (2, 2))
    head = jnp.arange(2 * FRAMES) // FRAMES
    mask = (same & (head[:, None] == head[None, :])).astype(F32)
    rank = lax.axis_index("seq")
    at = jnp.stack([rank % 2, lax.axis_index("dp"), rank // (2 * NZ), rank // 2 % NZ]).astype(jnp.int32)

    flat = [x.reshape(ROWS, WIDTH) for x in (queries, key_field, value_field, out_grad)]
    message, part = lax.optimization_barrier((pack_call(*flat), gather_weight_z(out_weight)))
    own = gather_weight_y(part)
    mid = HALF // 2
    left, right = along_x(own, 1), along_x(own, -1)
    pieces = [own, left, right, along_x(left[:mid], 1), along_x(right[mid:], -1)]
    weights = pieces + [swap_cores(piece) for piece in pieces]
    arrived, mask, weights = lax.optimization_barrier((exchange(message), mask, weights))
    q, k, v, g, mixed, probs = forward_call(mask, arrived)
    keep, send, ordered = weight_call(at, mixed, g)
    parts = reduce_chip(keep, swap_cores(send))
    out, mixed_grad = project_call(at, ordered, g, weights)
    parts, mixed_grad = lax.optimization_barrier((parts, mixed_grad))
    right, left = reduce_x_first(parts)
    message = backward_call(q, k, v, mixed_grad, out, probs)
    message, right, left = lax.optimization_barrier((message, right, left))
    strips = reduce_y(reduce_x_second(parts, right, left))
    came = exchange(message)
    strip = reduce_z(strips)
    came, strip = lax.optimization_barrier((came, strip))
    results = unpack_call(came)
    weight_grad = gather_x(strip)
    return tuple(x.reshape(queries.shape) for x in results) + (weight_grad,)


def solution(mesh):
    placed = P("dp", "seq", None, None)
    return jax.shard_map(
        local,
        mesh=mesh,
        in_specs=(placed, placed, placed, placed, P("seq", None), P("dp", None)),
        out_specs=(placed, placed, placed, placed, P("seq", None)),
        check_vma=False,
    )
```

```python
import functools

import jax
import jax.numpy as jnp
import numpy as np
from jax import lax
from jax.experimental import pallas as pl
from jax.experimental.pallas import tpu as pltpu
from jax.sharding import PartitionSpec as P

HEAD = 128
HEADS = 12
WIDTH = HEAD * HEADS
HALF = WIDTH // 2
FRAMES = 64
PLACES = 3
ROWS = FRAMES * PLACES
NX, NY, NZ = 4, 4, 8
SEQ = NY * NZ * 2
STRIP = WIDTH // SEQ
QUARTER = WIDTH // NX
BF = jnp.bfloat16
F32 = jnp.float32
FACTOR = HEAD ** (-0.5)
MIB = 1 << 20


def params(mib):
    return pltpu.CompilerParams(vmem_limit_bytes=mib * MIB)


def cost(us):
    return pl.CostEstimate(flops=0, bytes_accessed=int(us * 3.5e6), transcendentals=0)


def dot(a, b, dims=((1,), (0,))):
    return lax.dot_general(a, b, (dims, ((), ())), preferred_element_type=F32)


def swap_matrix(to_blocks):
    a = lax.broadcasted_iota(jnp.int32, (256, 256), 0 if to_blocks else 1)
    b = lax.broadcasted_iota(jnp.int32, (256, 256), 1 if to_blocks else 0)
    return jnp.where(8 * (a % 32) + a // 32 == b, F32(1), F32(0)).astype(BF)


def pack(sources, place, out_ref):
    swap = swap_matrix(False)
    for half in range(2):
        rows = slice(FRAMES * place + 32 * half, FRAMES * place + 32 * half + 32)
        for tile in range(1):
            parts = [
                src[rows, HALF * e + 256 * tile : HALF * e + 256 * tile + HALF]
                for src in sources
                for e in range(2)
            ]
            mixed = dot(swap, jnp.concatenate(parts, axis=0))
            out_ref[256 * half : 256 * half + 256, 256 * tile : 256 * tile + HALF] = mixed.astype(BF)


def unpack(in_ref, place, sinks):
    swap = swap_matrix(True)
    for half in range(2):
        rows = slice(FRAMES * place + 32 * half, FRAMES * place + 32 * half + 32)
        for tile in range(1):
            at = HALF * place + 256 * tile
            piece = dot(swap, in_ref[256 * half : 256 * half + 256, at : at + HALF]).astype(BF)
            for n in range(8):
                col = HALF * (n % 2) + 256 * tile
                sinks[n // 2][rows, col : col + HALF] = piece[32 * n : 32 * n + 32]


def place_rows(place):
    return pl.ds(FRAMES * place, FRAMES)


def message_copy(staged, message, sems, place):
    return pltpu.make_async_copy(
        staged.at[place], message.at[:, pl.ds(HALF * place, HALF)], sems.at[place]
    )


def pack_kernel(places, a, b, c, d, *refs):
    message, *held, staged, in_sems, out_sems = refs[-8:]
    arrays = (a, b, c, d)
    came = {
        j: [
            pltpu.make_async_copy(
                src.at[place_rows(j)], dst.at[place_rows(j)], in_sems.at[4 * j + n]
            )
            for n, (src, dst) in enumerate(zip(arrays, held))
        ]
        for j in places
    }
    for j in places:
        for copy in came[j]:
            copy.start()
    for j in places:
        for copy in came[j]:
            copy.wait()
        pack(held, j, staged.at[j])
        message_copy(staged, message, out_sems, j).start()
    for j in places:
        message_copy(staged, message, out_sems, j).wait()


def unpack_kernel(in_ref, a, b, c, d, *scratch):
    held, sems = scratch[:4], scratch[4]
    arrays = (a, b, c, d)
    gone = [
        [
            pltpu.make_async_copy(src.at[place_rows(j)], dst.at[place_rows(j)], sems.at[4 * j + n])
            for n, (dst, src) in enumerate(zip(arrays, held))
        ]
        for j in range(PLACES)
    ]
    for j in range(PLACES):
        unpack(in_ref, j, held)
        for copy in gone[j]:
            copy.start()
    for copies in gone:
        for copy in copies:
            copy.wait()


VMEM = pl.BlockSpec(memory_space=pltpu.VMEM)
ANY = pl.BlockSpec(memory_space=pl.ANY)
rows_shape = jax.ShapeDtypeStruct((ROWS, WIDTH), BF)
message_shape = jax.ShapeDtypeStruct((8 * SEQ, PLACES * HALF), BF)
rows_held = pltpu.VMEM((ROWS, WIDTH), BF)
message_held = pltpu.VMEM((PLACES, 8 * SEQ, HALF), BF)
probs_shape = jax.ShapeDtypeStruct((HEADS // 2 * PLACES, 2 * FRAMES, 2 * FRAMES), F32)


def pack_call(places, arrays, message=None):
    rest = [] if message is None else [message]
    return pl.pallas_call(
        functools.partial(pack_kernel, places),
        in_specs=[ANY] * (4 + len(rest)),
        out_specs=ANY,
        out_shape=message_shape,
        input_output_aliases={4: 0} if rest else {},
        scratch_shapes=[rows_held] * 4
        + [message_held, pltpu.SemaphoreType.DMA((4 * PLACES,)), pltpu.SemaphoreType.DMA((PLACES,))],
        compiler_params=params(56),
        cost_estimate=cost(3),
        name="pack",
    )(*arrays, *rest)


def unpack_call(message):
    return pl.pallas_call(
        unpack_kernel,
        in_specs=[VMEM],
        out_specs=[ANY] * 4,
        out_shape=[rows_shape] * 4,
        scratch_shapes=[rows_held] * 4 + [pltpu.SemaphoreType.DMA((4 * PLACES,))],
        compiler_params=params(12),
        cost_estimate=cost(3),
        name="unpack",
    )(message)


def pair(ref, place, n):
    at, rows = 2 * HEAD * n, slice(FRAMES * place, FRAMES * place + FRAMES)
    return jnp.concatenate([ref[rows, at : at + HEAD], ref[rows, at + HEAD : at + 2 * HEAD]], axis=0)


def put_pair(ref, place, n, value):
    at, rows = 2 * HEAD * n, slice(FRAMES * place, FRAMES * place + FRAMES)
    ref[rows, at : at + HEAD] = value[:FRAMES]
    ref[rows, at + HEAD : at + 2 * HEAD] = value[FRAMES:]


def forward_kernel(videos, in_ref, q, k, v, g, mixed, probs_ref):
    square = (2 * FRAMES, 2 * FRAMES)
    video = jnp.broadcast_to(videos[...], square)
    head = [lax.broadcasted_iota(jnp.int32, square, axis) // FRAMES for axis in range(2)]
    allowed = (video == video.T) & (head[0] == head[1])
    for j in range(PLACES):
        unpack(in_ref, j, (q, k, v, g))
        pairs = range(HEADS // 2)
        logits = [dot(pair(k, j, n), pair(q, j, n), ((1,), (1,))) for n in pairs]
        lows = []
        for n in pairs:
            raw = jnp.where(allowed, logits[n] * FACTOR, F32(-1e30))
            shifted = jnp.exp(raw - jnp.max(raw, axis=0, keepdims=True))
            probs = shifted * (1 / jnp.sum(shifted, axis=0, keepdims=True))
            probs_ref[HEADS // 2 * j + n] = probs
            lows.append(probs.astype(BF))
        for n in pairs:
            put_pair(mixed, j, n, dot(lows[n], pair(v, j, n), ((0,), (0,))).astype(BF))


def forward_call(videos, message):
    return pl.pallas_call(
        forward_kernel,
        in_specs=[VMEM] * 2,
        out_specs=[VMEM] * 6,
        out_shape=[rows_shape] * 5 + [probs_shape],
        compiler_params=params(8),
        cost_estimate=cost(5),
        name="forward",
    )(videos, message)


def strip_copies(at, copy):
    for side in range(2):
        core = at[0] if side == 0 else 1 - at[0]
        for dy in range(NY):
            for z in range(NZ):
                y = (at[2] + dy) % NY
                there = pl.multiple_of((y * NZ + z) * 2 * STRIP + core * STRIP, 8)
                copy(side, (dy * NZ + z) * STRIP, there)


def weight_kernel(at, mixed, grad, keep, send, ordered, turned, strips):
    turned[...] = mixed[...].astype(F32).T

    def copy(side, here, there):
        strips[side, here : here + STRIP, :] = turned[pl.ds(there, STRIP), :]

    strip_copies(at, copy)
    for side, out in ((1, send), (0, keep)):
        rows = strips[side]
        ordered[:, HALF * side : HALF * side + HALF] = rows.T.astype(BF)
        rows = rows.astype(BF)
        for d in range(0, NX, 2):
            g = [
                grad[:, pl.ds(pl.multiple_of((at[1] + d + i) % NX * QUARTER, QUARTER), QUARTER)]
                for i in range(2)
            ]
            both = dot(rows, jnp.concatenate(g, axis=1)).astype(BF)
            out[d] = both[:, :QUARTER]
            out[d + 1] = both[:, QUARTER:]


def weight_call(at, mixed, grad):
    return pl.pallas_call(
        weight_kernel,
        in_specs=[pl.BlockSpec(memory_space=pltpu.SMEM), VMEM, VMEM],
        out_specs=[VMEM] * 3,
        scratch_shapes=[pltpu.VMEM((WIDTH, ROWS), F32), pltpu.VMEM((2, HALF, ROWS), F32)],
        out_shape=[jax.ShapeDtypeStruct((NX, HALF, QUARTER), BF)] * 2 + [rows_shape],
        compiler_params=params(12),
        cost_estimate=cost(4),
        name="weight",
    )(at, mixed, grad)


PIECES = ((0, 0, HALF), (-1, 0, HALF), (1, 0, HALF), (2, 0, HALF // 2), (2, HALF // 2, HALF // 2))


def project_kernel(at, ordered, grad, *refs):
    weights, (out, mixed_grad, strips, turned) = refs[: 2 * len(PIECES)], refs[2 * len(PIECES) :]

    def cols(shift):
        return pl.ds(pl.multiple_of((at[1] + shift + NX) % NX * QUARTER, QUARTER), QUARTER)

    totals = [None, None]
    for side in range(2):
        near, left, right, *far = (ref[...] for ref in weights[len(PIECES) * side : len(PIECES) * side + len(PIECES)])
        pieces = (near, left, right, jnp.concatenate(far, axis=0))
        rows = ordered[:, HALF * side : HALF * side + HALF]
        turn = None
        for n, shifts in enumerate(((0, -1), (1, 2))):
            w = jnp.concatenate(pieces[2 * n : 2 * n + 2], axis=1)
            part = dot(rows, w)
            totals[n] = part if side == 0 else totals[n] + part
            g = jnp.concatenate([grad[:, cols(shift)] for shift in shifts], axis=1)
            term = dot(w, g, ((1,), (1,)))
            turn = term if turn is None else turn + term
            if side == 1:
                total = totals[n].astype(BF)
                out[:, cols(shifts[0])] = total[:, :QUARTER]
                out[:, cols(shifts[1])] = total[:, QUARTER:]
        strips[side] = turn

    def copy(side, here, there):
        turned[pl.ds(there, STRIP), :] = strips[side, here : here + STRIP, :]

    strip_copies(at, copy)
    mixed_grad[...] = turned[...].T.astype(BF)


def project_call(at, ordered, grad, weights):
    return pl.pallas_call(
        project_kernel,
        in_specs=[pl.BlockSpec(memory_space=pltpu.SMEM)] + [VMEM] * (2 + 2 * len(PIECES)),
        out_specs=[VMEM] * 2,
        out_shape=[rows_shape] * 2,
        scratch_shapes=[pltpu.VMEM((2, HALF, ROWS), F32), pltpu.VMEM((WIDTH, ROWS), F32)],
        compiler_params=params(14),
        cost_estimate=cost(5),
        name="project",
    )(at, ordered, grad, *weights)


def backward_kernel(q, k, v, mixed_grad, out, probs_ref, message, *scratch):
    q_grad, k_grad, v_grad, staged, sems = scratch
    for j in range(PLACES):
        pairs = range(HEADS // 2)
        grads = [pair(mixed_grad, j, n) for n in pairs]
        through = [dot(pair(v, j, n), grads[n], ((1,), (1,))) for n in pairs]
        scores = []
        for n in pairs:
            probs = probs_ref[HEADS // 2 * j + n]
            probs_low = probs.astype(BF)
            put_pair(v_grad, j, n, dot(probs_low, grads[n]).astype(BF))
            inner = jnp.sum(probs_low.astype(F32) * through[n], axis=0, keepdims=True)
            scores.append((probs * (through[n] - inner)).astype(BF))
        for n in pairs:
            put_pair(k_grad, j, n, (dot(scores[n], pair(q, j, n)) * FACTOR).astype(BF))
            put_pair(q_grad, j, n, (dot(scores[n], pair(k, j, n), ((0,), (0,))) * FACTOR).astype(BF))
        pack((out, q_grad, k_grad, v_grad), j, staged.at[j])
        message_copy(staged, message, sems, j).start()
    for j in range(PLACES):
        message_copy(staged, message, sems, j).wait()


def backward_call(*arrays):
    return pl.pallas_call(
        backward_kernel,
        in_specs=[VMEM] * 6,
        out_specs=ANY,
        out_shape=message_shape,
        scratch_shapes=[rows_held] * 3 + [message_held, pltpu.SemaphoreType.DMA((PLACES,))],
        compiler_params=params(14),
        cost_estimate=cost(5),
        name="backward",
    )(*arrays)


def seq_shift(dy, dz, dc):
    seq = np.arange(SEQ).reshape(NY, NZ, 2)
    return [
        (int(seq[y, z, c]), int(seq[(y + dy) % NY, (z + dz) % NZ, c ^ dc]))
        for y in range(NY)
        for z in range(NZ)
        for c in range(2)
    ]


def seq_flip(bit):
    seq = np.arange(SEQ).reshape(NY, NZ, 2)
    return [
        (int(seq[y, z, c]), int(seq[y, z ^ bit, c])) for y in range(NY) for z in range(NZ) for c in range(2)
    ]


def add_up(parts):
    total = parts[0].astype(F32)
    for part in parts[1:]:
        total = total + part.astype(F32)
    return total


def reduce_chip(keep, came):
    return [add_up([keep[d], came[d]]).astype(BF) for d in range(NX)]


def along_x(x, shift):
    return lax.ppermute(x, "dp", [(i, (i + shift) % NX) for i in range(NX)])


def reduce_x(parts):
    return add_up([parts[0]] + [along_x(parts[d], d) for d in (2, 1, 3)]).astype(BF)


def reduce_y(chip):
    chip = chip.reshape(NY, NZ * STRIP, QUARTER)
    came = [lax.ppermute(chip[d], "seq", seq_shift(d, 0, 0)) for d in (1, 3, 2)]
    return add_up([chip[0]] + came).astype(BF).reshape(NZ, STRIP, QUARTER)


def reduce_z(strips):
    at = lax.axis_index("seq") // 2 % NZ
    flips = (4, 5, 3, 2, 6, 1, 7)
    picked = [lax.dynamic_index_in_dim(strips, at ^ n, 0, keepdims=False) for n in (0,) + flips]
    own, *away = lax.optimization_barrier(picked)
    return add_up([own] + [lax.ppermute(x, "seq", seq_flip(n)) for x, n in zip(away, flips)])


def gather_x(own):
    came = {d: along_x(own, d) for d in (2, 1, 3)}
    place = lax.axis_index("dp")
    quarters = [lax.select_n((place - n) % NX, own, came[1], came[2], came[3]) for n in range(NX)]
    return jnp.concatenate(quarters, axis=1)


def gather_weight_even(out_weight):
    place = lax.axis_index("dp")
    own = lax.select_n(place, *[out_weight[:, QUARTER * n : QUARTER * n + QUARTER] for n in range(NX)])
    came = [lax.ppermute(own, "seq", seq_flip(n)) for n in (4, 2, 6)]
    return jnp.stack([own, came[1], came[0], came[2]])


def gather_weight_z(even, odd):
    at = lax.axis_index("seq") // 2 % NZ
    both = jnp.stack([even, odd], axis=1).reshape(NZ, STRIP, QUARTER)
    for bit in (1, 2, 4):
        halves = both.reshape(NZ // (2 * bit), 2, bit, STRIP, QUARTER)
        both = jnp.where(at & bit != 0, halves[:, ::-1], halves).reshape(NZ, STRIP, QUARTER)
    return both.reshape(NZ * STRIP, QUARTER)


def gather_weight_y(own):
    came = {d: lax.ppermute(own, "seq", seq_shift(NY - d, 0, 0)) for d in (1, 3, 2)}
    return jnp.concatenate([own, came[1], came[2], came[3]], axis=0)


def swap_cores(x):
    return lax.ppermute(x, "seq", seq_shift(0, 0, 1))


def exchange(message):
    return lax.all_to_all(message, "seq", split_axis=0, concat_axis=0, tiled=True)


def local(queries, key_field, value_field, out_grad, out_weight, frame_video):
    rank = lax.axis_index("seq")
    at = jnp.stack([rank % 2, lax.axis_index("dp"), rank // (2 * NZ), rank // 2 % NZ]).astype(jnp.int32)
    videos = jnp.concatenate([frame_video, frame_video], axis=1)

    flat = [x.reshape(ROWS, WIDTH) for x in (queries, key_field, value_field, out_grad)]
    message, even = lax.optimization_barrier((pack_call((0, 1), flat), gather_weight_even(out_weight)))
    message, even, odd = lax.optimization_barrier(
        (pack_call((2,), flat, message), even, lax.ppermute(even, "seq", seq_flip(1)))
    )
    own = gather_weight_y(gather_weight_z(even, odd))
    mid = HALF // 2
    left, right = along_x(own, 1), along_x(own, -1)
    pieces = [own, left, right, along_x(left[:mid], 1), along_x(right[mid:], -1)]
    weights = pieces + [swap_cores(piece) for piece in pieces]
    arrived, at, videos, weights = lax.optimization_barrier((exchange(message), at, videos, weights))
    q, k, v, g, mixed, probs = forward_call(videos, arrived)
    keep, send, ordered = weight_call(at, mixed, g)
    came = swap_cores(send)
    out, mixed_grad = project_call(at, ordered, g, weights)
    message = backward_call(q, k, v, mixed_grad, out, probs)
    message, came = lax.optimization_barrier((message, came))
    strips = reduce_y(reduce_x(reduce_chip(keep, came)))
    came = exchange(message)
    strip = reduce_z(strips)
    came, strip = lax.optimization_barrier((came, strip))
    results = unpack_call(came)
    weight_grad = gather_x(strip)
    return tuple(x.reshape(queries.shape) for x in results) + (weight_grad,)


def solution(mesh):
    placed = P("dp", "seq", None, None)
    return jax.shard_map(
        local,
        mesh=mesh,
        in_specs=(placed, placed, placed, placed, P("seq", None), P("dp", None)),
        out_specs=(placed, placed, placed, placed, P("seq", None)),
        check_vma=False,
    )
```

```python
import functools

import jax
import jax.numpy as jnp
import numpy as np
from jax import lax
from jax.experimental import pallas as pl
from jax.experimental.pallas import tpu as pltpu
from jax.sharding import PartitionSpec as P

HEAD = 128
HEADS = 12
WIDTH = HEAD * HEADS
HALF = WIDTH // 2
FRAMES = 64
PLACES = 3
ROWS = FRAMES * PLACES
NX, NY, NZ = 4, 4, 8
SEQ = NY * NZ * 2
STRIP = WIDTH // SEQ
QUARTER = WIDTH // NX
BF = jnp.bfloat16
F32 = jnp.float32
FACTOR = HEAD ** (-0.5)
MIB = 1 << 20


def params(mib):
    return pltpu.CompilerParams(vmem_limit_bytes=mib * MIB)


def cost(us):
    return pl.CostEstimate(flops=0, bytes_accessed=int(us * 3.5e6), transcendentals=0)


def dot(a, b, dims=((1,), (0,))):
    return lax.dot_general(a, b, (dims, ((), ())), preferred_element_type=F32)


def swap_matrix(to_blocks):
    a = lax.broadcasted_iota(jnp.int32, (256, 256), 0 if to_blocks else 1)
    b = lax.broadcasted_iota(jnp.int32, (256, 256), 1 if to_blocks else 0)
    return jnp.where(8 * (a % 32) + a // 32 == b, F32(1), F32(0)).astype(BF)


def pack(sources, place, out_ref):
    swap = swap_matrix(False)
    for half in range(2):
        rows = slice(FRAMES * place + 32 * half, FRAMES * place + 32 * half + 32)
        for tile in range(1):
            parts = [
                src[rows, HALF * e + 256 * tile : HALF * e + 256 * tile + HALF]
                for src in sources
                for e in range(2)
            ]
            mixed = dot(swap, jnp.concatenate(parts, axis=0))
            out_ref[256 * half : 256 * half + 256, 256 * tile : 256 * tile + HALF] = mixed.astype(BF)


def unpack(in_ref, place, sinks):
    swap = swap_matrix(True)
    for half in range(2):
        rows = slice(FRAMES * place + 32 * half, FRAMES * place + 32 * half + 32)
        for tile in range(1):
            at = HALF * place + 256 * tile
            piece = dot(swap, in_ref[256 * half : 256 * half + 256, at : at + HALF]).astype(BF)
            for n in range(8):
                col = HALF * (n % 2) + 256 * tile
                sinks[n // 2][rows, col : col + HALF] = piece[32 * n : 32 * n + 32]


def place_rows(place):
    return pl.ds(FRAMES * place, FRAMES)


def message_copy(staged, message, sems, place):
    return pltpu.make_async_copy(
        staged.at[place], message.at[:, pl.ds(HALF * place, HALF)], sems.at[place]
    )


def pack_kernel(places, a, b, c, d, *refs):
    message, *held, staged, in_sems, out_sems = refs[-8:]
    arrays = (a, b, c, d)
    came = {
        j: [
            pltpu.make_async_copy(
                src.at[place_rows(j)], dst.at[place_rows(j)], in_sems.at[4 * j + n]
            )
            for n, (src, dst) in enumerate(zip(arrays, held))
        ]
        for j in places
    }
    for j in places:
        for copy in came[j]:
            copy.start()
    for j in places:
        for copy in came[j]:
            copy.wait()
        pack(held, j, staged.at[j])
        message_copy(staged, message, out_sems, j).start()
    for j in places:
        message_copy(staged, message, out_sems, j).wait()


def unpack_kernel(in_ref, a, b, c, d, *scratch):
    held, sems = scratch[:4], scratch[4]
    arrays = (a, b, c, d)
    gone = [
        [
            pltpu.make_async_copy(src.at[place_rows(j)], dst.at[place_rows(j)], sems.at[4 * j + n])
            for n, (dst, src) in enumerate(zip(arrays, held))
        ]
        for j in range(PLACES)
    ]
    for j in range(PLACES):
        unpack(in_ref, j, held)
        for copy in gone[j]:
            copy.start()
    for copies in gone:
        for copy in copies:
            copy.wait()


VMEM = pl.BlockSpec(memory_space=pltpu.VMEM)
SMEM = pl.BlockSpec(memory_space=pltpu.SMEM)
ANY = pl.BlockSpec(memory_space=pl.ANY)
rows_shape = jax.ShapeDtypeStruct((ROWS, WIDTH), BF)
message_shape = jax.ShapeDtypeStruct((8 * SEQ, PLACES * HALF), BF)
rows_held = pltpu.VMEM((ROWS, WIDTH), BF)
message_held = pltpu.VMEM((PLACES, 8 * SEQ, HALF), BF)
probs_shape = jax.ShapeDtypeStruct((HEADS // 2 * PLACES, 2 * FRAMES, 2 * FRAMES), F32)


def pack_call(places, arrays, message=None):
    rest = [] if message is None else [message]
    return pl.pallas_call(
        functools.partial(pack_kernel, places),
        in_specs=[ANY] * (4 + len(rest)),
        out_specs=ANY,
        out_shape=message_shape,
        input_output_aliases={4: 0} if rest else {},
        scratch_shapes=[rows_held] * 4
        + [message_held, pltpu.SemaphoreType.DMA((4 * PLACES,)), pltpu.SemaphoreType.DMA((PLACES,))],
        compiler_params=params(56),
        cost_estimate=cost(3),
        name="pack",
    )(*arrays, *rest)


def unpack_call(message):
    return pl.pallas_call(
        unpack_kernel,
        in_specs=[VMEM],
        out_specs=[ANY] * 4,
        out_shape=[rows_shape] * 4,
        scratch_shapes=[rows_held] * 4 + [pltpu.SemaphoreType.DMA((4 * PLACES,))],
        compiler_params=params(12),
        cost_estimate=cost(3),
        name="unpack",
    )(message)


def pair(ref, place, n):
    at, rows = 2 * HEAD * n, slice(FRAMES * place, FRAMES * place + FRAMES)
    return jnp.concatenate([ref[rows, at : at + HEAD], ref[rows, at + HEAD : at + 2 * HEAD]], axis=0)


def put_pair(ref, place, n, value):
    at, rows = 2 * HEAD * n, slice(FRAMES * place, FRAMES * place + FRAMES)
    ref[rows, at : at + HEAD] = value[:FRAMES]
    ref[rows, at + HEAD : at + 2 * HEAD] = value[FRAMES:]


def strip_copies(at, copy):
    for side in range(2):
        core = at[0] if side == 0 else 1 - at[0]
        for dy in range(NY):
            for z in range(NZ):
                y = (at[2] + dy) % NY
                there = pl.multiple_of((y * NZ + z) * 2 * STRIP + core * STRIP, 8)
                copy(side, (dy * NZ + z) * STRIP, there)


def forward_kernel(at, videos, in_ref, q, k, v, g, probs_ref, ordered, mine, theirs, *scratch):
    mixed, turned, strips = scratch
    square = (2 * FRAMES, 2 * FRAMES)
    video = jnp.broadcast_to(videos[...], square)
    head = [lax.broadcasted_iota(jnp.int32, square, axis) // FRAMES for axis in range(2)]
    allowed = (video == video.T) & (head[0] == head[1])
    for j in range(PLACES):
        unpack(in_ref, j, (q, k, v, g))
        pairs = range(HEADS // 2)
        logits = [dot(pair(k, j, n), pair(q, j, n), ((1,), (1,))) for n in pairs]
        lows = []
        for n in pairs:
            raw = jnp.where(allowed, logits[n] * FACTOR, F32(-1e30))
            shifted = jnp.exp(raw - jnp.max(raw, axis=0, keepdims=True))
            probs = shifted * (1 / jnp.sum(shifted, axis=0, keepdims=True))
            probs_ref[HEADS // 2 * j + n] = probs
            lows.append(probs.astype(BF))
        for n in pairs:
            put_pair(mixed, j, n, dot(lows[n], pair(v, j, n), ((0,), (0,))).astype(BF))

    turned[...] = mixed[...].astype(F32).T

    def copy(side, here, there):
        strips[side, here : here + STRIP, :] = turned[pl.ds(there, STRIP), :]

    strip_copies(at, copy)
    for side, out in ((1, theirs), (0, mine)):
        rows = strips[side]
        out[...] = rows.astype(BF)
        ordered[:, HALF * side : HALF * side + HALF] = rows.T.astype(BF)


strips_shape = jax.ShapeDtypeStruct((HALF, ROWS), BF)
strips_held = [pltpu.VMEM((WIDTH, ROWS), F32), pltpu.VMEM((2, HALF, ROWS), F32)]


def forward_call(at, videos, message):
    return pl.pallas_call(
        forward_kernel,
        in_specs=[SMEM, VMEM, VMEM],
        out_specs=[VMEM] * 8,
        out_shape=[rows_shape] * 4 + [probs_shape, rows_shape, strips_shape, strips_shape],
        scratch_shapes=[rows_held] + strips_held,
        compiler_params=params(12),
        cost_estimate=cost(4),
        name="forward",
    )(at, videos, message)


def weight_kernel(at, mine, came, grad, came_grad, *outs):
    for d in range(0, NX, 2):
        cols = [
            pl.ds(pl.multiple_of((at[1] + d + i) % NX * QUARTER, QUARTER), QUARTER) for i in range(2)
        ]
        total = None
        for strips, rows in ((mine, grad), (came, came_grad)):
            part = dot(strips[...], jnp.concatenate([rows[:, c] for c in cols], axis=1))
            total = part if total is None else total + part
        total = total.astype(BF)
        size = NZ // 2 * STRIP
        for i in range(2):
            for half in range(2):
                for dy in range(NY):
                    at_row = (2 * dy + half) * size
                    piece = total[at_row : at_row + size, QUARTER * i : QUARTER * i + QUARTER]
                    outs[NX * half + d + i][size * dy : size * dy + size, :] = piece


def weight_call(at, mine, came, grad, came_grad):
    return pl.pallas_call(
        weight_kernel,
        in_specs=[SMEM] + [VMEM] * 4,
        out_specs=[VMEM] * (2 * NX),
        out_shape=[jax.ShapeDtypeStruct((HALF // 2, QUARTER), BF)] * (2 * NX),
        compiler_params=params(10),
        cost_estimate=cost(2),
        name="weight",
    )(at, mine, came, grad, came_grad)


PIECES = ((0, 0, HALF), (-1, 0, HALF), (1, 0, HALF), (2, 0, HALF // 2), (2, HALF // 2, HALF // 2))


def project_kernel(at, ordered, grad, *refs):
    weights, (out, mixed_grad, strips, turned) = refs[: 2 * len(PIECES)], refs[2 * len(PIECES) :]

    def cols(shift):
        return pl.ds(pl.multiple_of((at[1] + shift + NX) % NX * QUARTER, QUARTER), QUARTER)

    totals = [None, None]
    for side in range(2):
        near, left, right, *far = (ref[...] for ref in weights[len(PIECES) * side : len(PIECES) * side + len(PIECES)])
        pieces = (near, left, right, jnp.concatenate(far, axis=0))
        rows = ordered[:, HALF * side : HALF * side + HALF]
        turn = None
        for n, shifts in enumerate(((0, -1), (1, 2))):
            w = jnp.concatenate(pieces[2 * n : 2 * n + 2], axis=1)
            part = dot(rows, w)
            totals[n] = part if side == 0 else totals[n] + part
            g = jnp.concatenate([grad[:, cols(shift)] for shift in shifts], axis=1)
            term = dot(w, g, ((1,), (1,)))
            turn = term if turn is None else turn + term
            if side == 1:
                total = totals[n].astype(BF)
                out[:, cols(shifts[0])] = total[:, :QUARTER]
                out[:, cols(shifts[1])] = total[:, QUARTER:]
        strips[side] = turn

    def copy(side, here, there):
        turned[pl.ds(there, STRIP), :] = strips[side, here : here + STRIP, :]

    strip_copies(at, copy)
    mixed_grad[...] = turned[...].T.astype(BF)


def project_call(at, ordered, grad, weights):
    return pl.pallas_call(
        project_kernel,
        in_specs=[SMEM] + [VMEM] * (2 + 2 * len(PIECES)),
        out_specs=[VMEM] * 2,
        out_shape=[rows_shape] * 2,
        scratch_shapes=[pltpu.VMEM((2, HALF, ROWS), F32), pltpu.VMEM((WIDTH, ROWS), F32)],
        compiler_params=params(14),
        cost_estimate=cost(5),
        name="project",
    )(at, ordered, grad, *weights)


def backward_kernel(q, k, v, mixed_grad, out, probs_ref, message, *scratch):
    q_grad, k_grad, v_grad, staged, sems = scratch
    for j in range(PLACES):
        pairs = range(HEADS // 2)
        grads = [pair(mixed_grad, j, n) for n in pairs]
        through = [dot(pair(v, j, n), grads[n], ((1,), (1,))) for n in pairs]
        scores = []
        for n in pairs:
            probs = probs_ref[HEADS // 2 * j + n]
            probs_low = probs.astype(BF)
            put_pair(v_grad, j, n, dot(probs_low, grads[n]).astype(BF))
            inner = jnp.sum(probs_low.astype(F32) * through[n], axis=0, keepdims=True)
            scores.append((probs * (through[n] - inner)).astype(BF))
        for n in pairs:
            put_pair(k_grad, j, n, (dot(scores[n], pair(q, j, n)) * FACTOR).astype(BF))
            put_pair(q_grad, j, n, (dot(scores[n], pair(k, j, n), ((0,), (0,))) * FACTOR).astype(BF))
        pack((out, q_grad, k_grad, v_grad), j, staged.at[j])
        message_copy(staged, message, sems, j).start()
    for j in range(PLACES):
        message_copy(staged, message, sems, j).wait()


def backward_call(*arrays):
    return pl.pallas_call(
        backward_kernel,
        in_specs=[VMEM] * 6,
        out_specs=ANY,
        out_shape=message_shape,
        scratch_shapes=[rows_held] * 3 + [message_held, pltpu.SemaphoreType.DMA((PLACES,))],
        compiler_params=params(14),
        cost_estimate=cost(5),
        name="backward",
    )(*arrays)


def seq_shift(dy, dz, dc):
    seq = np.arange(SEQ).reshape(NY, NZ, 2)
    return [
        (int(seq[y, z, c]), int(seq[(y + dy) % NY, (z + dz) % NZ, c ^ dc]))
        for y in range(NY)
        for z in range(NZ)
        for c in range(2)
    ]


def seq_flip(bit):
    seq = np.arange(SEQ).reshape(NY, NZ, 2)
    return [
        (int(seq[y, z, c]), int(seq[y, z ^ bit, c])) for y in range(NY) for z in range(NZ) for c in range(2)
    ]


def add_up(parts):
    total = parts[0].astype(F32)
    for part in parts[1:]:
        total = total + part.astype(F32)
    return total


def along_x(x, shift):
    return lax.ppermute(x, "dp", [(i, (i + shift) % NX) for i in range(NX)])


def reduce_x(parts):
    return add_up([parts[0]] + [along_x(parts[d], d) for d in (2, 1, 3)]).astype(BF)


def reduce_y(chip):
    chip = chip.reshape(NY, NZ // 2 * STRIP, QUARTER)
    came = [lax.ppermute(chip[d], "seq", seq_shift(d, 0, 0)) for d in (2, 1, 3)]
    return add_up([chip[0]] + came).astype(BF).reshape(NZ // 2, STRIP, QUARTER)


def reduce_z(strips):
    at = lax.axis_index("seq") // 2 % NZ
    flips = (4, 5, 3, 2, 6, 1, 7)
    picked = [lax.dynamic_index_in_dim(strips, at ^ n, 0, keepdims=False) for n in (0,) + flips]
    own, *away = lax.optimization_barrier(picked)
    return add_up([own] + [lax.ppermute(x, "seq", seq_flip(n)) for x, n in zip(away, flips)])


def gather_x(own):
    came = {d: along_x(own, d) for d in (2, 1, 3)}
    place = lax.axis_index("dp")
    quarters = [lax.select_n((place - n) % NX, own, came[1], came[2], came[3]) for n in range(NX)]
    return jnp.concatenate(quarters, axis=1)


def gather_weight_even(out_weight):
    place = lax.axis_index("dp")
    own = lax.select_n(place, *[out_weight[:, QUARTER * n : QUARTER * n + QUARTER] for n in range(NX)])
    came = [lax.ppermute(own, "seq", seq_flip(n)) for n in (4, 2, 6)]
    return jnp.stack([own, came[1], came[0], came[2]])


def gather_weight_z(even, odd):
    at = lax.axis_index("seq") // 2 % NZ
    both = jnp.stack([even, odd], axis=1).reshape(NZ, STRIP, QUARTER)
    for bit in (1, 2, 4):
        halves = both.reshape(NZ // (2 * bit), 2, bit, STRIP, QUARTER)
        both = jnp.where(at & bit != 0, halves[:, ::-1], halves).reshape(NZ, STRIP, QUARTER)
    return both.reshape(NZ * STRIP, QUARTER)


def gather_weight_y(own):
    came = {d: lax.ppermute(own, "seq", seq_shift(NY - d, 0, 0)) for d in (1, 3, 2)}
    return jnp.concatenate([own, came[1], came[2], came[3]], axis=0)


def swap_cores(x):
    return lax.ppermute(x, "seq", seq_shift(0, 0, 1))


def exchange(message):
    return lax.all_to_all(message, "seq", split_axis=0, concat_axis=0, tiled=True)


def local(queries, key_field, value_field, out_grad, out_weight, frame_video):
    rank = lax.axis_index("seq")
    at = jnp.stack([rank % 2, lax.axis_index("dp"), rank // (2 * NZ), rank // 2 % NZ]).astype(jnp.int32)
    videos = jnp.concatenate([frame_video, frame_video], axis=1)

    flat = [x.reshape(ROWS, WIDTH) for x in (queries, key_field, value_field, out_grad)]
    message, even = lax.optimization_barrier((pack_call((0, 1), flat), gather_weight_even(out_weight)))
    message, even, odd = lax.optimization_barrier(
        (pack_call((2,), flat, message), even, lax.ppermute(even, "seq", seq_flip(1)))
    )
    own = gather_weight_y(gather_weight_z(even, odd))
    mid = HALF // 2
    left, right = along_x(own, 1), along_x(own, -1)
    pieces = [own, left, right, along_x(left[:mid], 1), along_x(right[mid:], -1)]
    weights = pieces + [swap_cores(piece) for piece in pieces]
    arrived, at, videos, weights = lax.optimization_barrier((exchange(message), at, videos, weights))
    q, k, v, g, probs, ordered, mine, theirs = forward_call(at, videos, arrived)
    came, came_g = swap_cores(theirs), swap_cores(g)
    out, mixed_grad = project_call(at, ordered, g, weights)
    parts = weight_call(at, mine, came, g, came_g)
    message = backward_call(q, k, v, mixed_grad, out, probs)
    message, parts = lax.optimization_barrier((message, parts))
    halves = [reduce_x(parts[:NX]), reduce_x(parts[NX:])]
    strips = jnp.concatenate([reduce_y(half) for half in halves], axis=0)
    came = exchange(message)
    strip = reduce_z(strips)
    came, strip = lax.optimization_barrier((came, strip))
    results = unpack_call(came)
    weight_grad = gather_x(strip)
    return tuple(x.reshape(queries.shape) for x in results) + (weight_grad,)


def solution(mesh):
    placed = P("dp", "seq", None, None)
    return jax.shard_map(
        local,
        mesh=mesh,
        in_specs=(placed, placed, placed, placed, P("seq", None), P("dp", None)),
        out_specs=(placed, placed, placed, placed, P("seq", None)),
        check_vma=False,
    )
```

```python
import functools

import jax
import jax.numpy as jnp
import numpy as np
from jax import lax
from jax.experimental import pallas as pl
from jax.experimental.pallas import tpu as pltpu
from jax.sharding import PartitionSpec as P

HEAD = 128
HEADS = 12
WIDTH = HEAD * HEADS
HALF = WIDTH // 2
FRAMES = 64
PLACES = 3
ROWS = FRAMES * PLACES
NX, NY, NZ = 4, 4, 8
SEQ = NY * NZ * 2
STRIP = WIDTH // SEQ
QUARTER = WIDTH // NX
BF = jnp.bfloat16
F32 = jnp.float32
FACTOR = HEAD ** (-0.5)
MIB = 1 << 20


def params(mib):
    return pltpu.CompilerParams(vmem_limit_bytes=mib * MIB)


def cost(us):
    return pl.CostEstimate(flops=0, bytes_accessed=int(us * 3.5e6), transcendentals=0)


def dot(a, b, dims=((1,), (0,))):
    return lax.dot_general(a, b, (dims, ((), ())), preferred_element_type=F32)


def swap_matrix(to_blocks):
    a = lax.broadcasted_iota(jnp.int32, (256, 256), 0 if to_blocks else 1)
    b = lax.broadcasted_iota(jnp.int32, (256, 256), 1 if to_blocks else 0)
    return jnp.where(8 * (a % 32) + a // 32 == b, F32(1), F32(0)).astype(BF)


def pack(sources, place, out_ref):
    swap = swap_matrix(False)
    for half in range(2):
        rows = slice(FRAMES * place + 32 * half, FRAMES * place + 32 * half + 32)
        for tile in range(1):
            parts = [
                src[rows, HALF * e + 256 * tile : HALF * e + 256 * tile + HALF]
                for src in sources
                for e in range(2)
            ]
            mixed = dot(swap, jnp.concatenate(parts, axis=0))
            out_ref[256 * half : 256 * half + 256, 256 * tile : 256 * tile + HALF] = mixed.astype(BF)


def unpack(in_ref, place, sinks):
    swap = swap_matrix(True)
    for half in range(2):
        rows = slice(FRAMES * place + 32 * half, FRAMES * place + 32 * half + 32)
        for tile in range(1):
            at = HALF * place + 256 * tile
            piece = dot(swap, in_ref[256 * half : 256 * half + 256, at : at + HALF]).astype(BF)
            for n in range(8):
                col = HALF * (n % 2) + 256 * tile
                sinks[n // 2][rows, col : col + HALF] = piece[32 * n : 32 * n + 32]


def place_rows(place):
    return pl.ds(FRAMES * place, FRAMES)


def message_copy(staged, message, sems, place):
    return pltpu.make_async_copy(
        staged.at[place], message.at[:, pl.ds(HALF * place, HALF)], sems.at[place]
    )


def pack_kernel(places, a, b, c, d, *refs):
    message, *held, staged, in_sems, out_sems = refs[-8:]
    arrays = (a, b, c, d)
    came = {
        j: [
            pltpu.make_async_copy(
                src.at[place_rows(j)], dst.at[place_rows(j)], in_sems.at[4 * j + n]
            )
            for n, (src, dst) in enumerate(zip(arrays, held))
        ]
        for j in places
    }
    for j in places:
        for copy in came[j]:
            copy.start()
    for j in places:
        for copy in came[j]:
            copy.wait()
        pack(held, j, staged.at[j])
        message_copy(staged, message, out_sems, j).start()
    for j in places:
        message_copy(staged, message, out_sems, j).wait()


def unpack_kernel(in_ref, a, b, c, d, *scratch):
    held, sems = scratch[:4], scratch[4]
    arrays = (a, b, c, d)
    gone = [
        [
            pltpu.make_async_copy(src.at[place_rows(j)], dst.at[place_rows(j)], sems.at[4 * j + n])
            for n, (dst, src) in enumerate(zip(arrays, held))
        ]
        for j in range(PLACES)
    ]
    for j in range(PLACES):
        unpack(in_ref, j, held)
        for copy in gone[j]:
            copy.start()
    for copies in gone:
        for copy in copies:
            copy.wait()


VMEM = pl.BlockSpec(memory_space=pltpu.VMEM)
SMEM = pl.BlockSpec(memory_space=pltpu.SMEM)
ANY = pl.BlockSpec(memory_space=pl.ANY)
rows_shape = jax.ShapeDtypeStruct((ROWS, WIDTH), BF)
message_shape = jax.ShapeDtypeStruct((8 * SEQ, PLACES * HALF), BF)
rows_held = pltpu.VMEM((ROWS, WIDTH), BF)
message_held = pltpu.VMEM((PLACES, 8 * SEQ, HALF), BF)
probs_shape = jax.ShapeDtypeStruct((HEADS // 2 * PLACES, 2 * FRAMES, 2 * FRAMES), F32)


def pack_call(places, arrays, message=None):
    rest = [] if message is None else [message]
    return pl.pallas_call(
        functools.partial(pack_kernel, places),
        in_specs=[ANY] * (4 + len(rest)),
        out_specs=ANY,
        out_shape=message_shape,
        input_output_aliases={4: 0} if rest else {},
        scratch_shapes=[rows_held] * 4
        + [message_held, pltpu.SemaphoreType.DMA((4 * PLACES,)), pltpu.SemaphoreType.DMA((PLACES,))],
        compiler_params=params(56),
        cost_estimate=cost(3),
        name="pack",
    )(*arrays, *rest)


def unpack_call(message):
    return pl.pallas_call(
        unpack_kernel,
        in_specs=[VMEM],
        out_specs=[ANY] * 4,
        out_shape=[rows_shape] * 4,
        scratch_shapes=[rows_held] * 4 + [pltpu.SemaphoreType.DMA((4 * PLACES,))],
        compiler_params=params(12),
        cost_estimate=cost(3),
        name="unpack",
    )(message)


def pair(ref, place, n):
    at, rows = 2 * HEAD * n, slice(FRAMES * place, FRAMES * place + FRAMES)
    return jnp.concatenate([ref[rows, at : at + HEAD], ref[rows, at + HEAD : at + 2 * HEAD]], axis=0)


def put_pair(ref, place, n, value):
    at, rows = 2 * HEAD * n, slice(FRAMES * place, FRAMES * place + FRAMES)
    ref[rows, at : at + HEAD] = value[:FRAMES]
    ref[rows, at + HEAD : at + 2 * HEAD] = value[FRAMES:]


def strip_copies(at, copy):
    for side in range(2):
        core = at[0] if side == 0 else 1 - at[0]
        for dy in range(NY):
            for z in range(NZ):
                y = (at[2] + dy) % NY
                there = pl.multiple_of((y * NZ + z) * 2 * STRIP + core * STRIP, 8)
                copy(side, (dy * NZ + z) * STRIP, there)


def forward_kernel(at, videos, in_ref, q, k, v, g, probs_ref, ordered, mine, theirs, *scratch):
    mixed, turned, strips = scratch
    square = (2 * FRAMES, 2 * FRAMES)
    video = jnp.broadcast_to(videos[...], square)
    head = [lax.broadcasted_iota(jnp.int32, square, axis) // FRAMES for axis in range(2)]
    allowed = (video == video.T) & (head[0] == head[1])
    for j in range(PLACES):
        unpack(in_ref, j, (q, k, v, g))
        pairs = range(HEADS // 2)
        logits = [dot(pair(k, j, n), pair(q, j, n), ((1,), (1,))) for n in pairs]
        lows = []
        for n in pairs:
            raw = jnp.where(allowed, logits[n] * FACTOR, F32(-1e30))
            shifted = jnp.exp(raw - jnp.max(raw, axis=0, keepdims=True))
            probs = shifted * (1 / jnp.sum(shifted, axis=0, keepdims=True))
            probs_ref[HEADS // 2 * j + n] = probs
            lows.append(probs.astype(BF))
        for n in pairs:
            put_pair(mixed, j, n, dot(lows[n], pair(v, j, n), ((0,), (0,))).astype(BF))

    turned[...] = mixed[...].astype(F32).T

    def copy(side, here, there):
        strips[side, here : here + STRIP, :] = turned[pl.ds(there, STRIP), :]

    strip_copies(at, copy)
    for side, out in ((1, theirs), (0, mine)):
        rows = strips[side]
        out[...] = rows.astype(BF)
        ordered[:, HALF * side : HALF * side + HALF] = rows.T.astype(BF)


strips_shape = jax.ShapeDtypeStruct((HALF, ROWS), BF)
strips_held = [pltpu.VMEM((WIDTH, ROWS), F32), pltpu.VMEM((2, HALF, ROWS), F32)]


def forward_call(at, videos, message):
    return pl.pallas_call(
        forward_kernel,
        in_specs=[SMEM, VMEM, VMEM],
        out_specs=[VMEM] * 8,
        out_shape=[rows_shape] * 4 + [probs_shape, rows_shape, strips_shape, strips_shape],
        scratch_shapes=[rows_held] + strips_held,
        compiler_params=params(12),
        cost_estimate=cost(4),
        name="forward",
    )(at, videos, message)


def weight_kernel(at, mine, came, grad, came_grad, *outs):
    for d in range(0, NX, 2):
        cols = [
            pl.ds(pl.multiple_of((at[1] + d + i) % NX * QUARTER, QUARTER), QUARTER) for i in range(2)
        ]
        total = None
        for strips, rows in ((mine, grad), (came, came_grad)):
            part = dot(strips[...], jnp.concatenate([rows[:, c] for c in cols], axis=1))
            total = part if total is None else total + part
        total = total.astype(BF)
        size = NZ // 2 * STRIP
        for i in range(2):
            for half in range(2):
                for dy in range(NY):
                    at_row = (2 * dy + half) * size
                    piece = total[at_row : at_row + size, QUARTER * i : QUARTER * i + QUARTER]
                    outs[NX * half + d + i][size * dy : size * dy + size, :] = piece


def weight_call(at, mine, came, grad, came_grad):
    return pl.pallas_call(
        weight_kernel,
        in_specs=[SMEM] + [VMEM] * 4,
        out_specs=[VMEM] * (2 * NX),
        out_shape=[jax.ShapeDtypeStruct((HALF // 2, QUARTER), BF)] * (2 * NX),
        compiler_params=params(10),
        cost_estimate=cost(2),
        name="weight",
    )(at, mine, came, grad, came_grad)


PIECES = ((0, 0, HALF), (-1, 0, HALF), (1, 0, HALF), (2, 0, HALF // 2), (2, HALF // 2, HALF // 2))


def project_kernel(at, ordered, grad, *refs):
    weights, (out, mixed_grad, strips, turned) = refs[: 2 * len(PIECES)], refs[2 * len(PIECES) :]

    def cols(shift):
        return pl.ds(pl.multiple_of((at[1] + shift + NX) % NX * QUARTER, QUARTER), QUARTER)

    totals = [None, None]
    for side in range(2):
        near, left, right, *far = (ref[...] for ref in weights[len(PIECES) * side : len(PIECES) * side + len(PIECES)])
        pieces = (near, left, right, jnp.concatenate(far, axis=0))
        rows = ordered[:, HALF * side : HALF * side + HALF]
        turn = None
        for n, shifts in enumerate(((0, -1), (1, 2))):
            w = jnp.concatenate(pieces[2 * n : 2 * n + 2], axis=1)
            part = dot(rows, w)
            totals[n] = part if side == 0 else totals[n] + part
            g = jnp.concatenate([grad[:, cols(shift)] for shift in shifts], axis=1)
            term = dot(w, g, ((1,), (1,)))
            turn = term if turn is None else turn + term
            if side == 1:
                total = totals[n].astype(BF)
                out[:, cols(shifts[0])] = total[:, :QUARTER]
                out[:, cols(shifts[1])] = total[:, QUARTER:]
        strips[side] = turn

    def copy(side, here, there):
        turned[pl.ds(there, STRIP), :] = strips[side, here : here + STRIP, :]

    strip_copies(at, copy)
    mixed_grad[...] = turned[...].T.astype(BF)


def project_call(at, ordered, grad, weights):
    return pl.pallas_call(
        project_kernel,
        in_specs=[SMEM] + [VMEM] * (2 + 2 * len(PIECES)),
        out_specs=[VMEM] * 2,
        out_shape=[rows_shape] * 2,
        scratch_shapes=[pltpu.VMEM((2, HALF, ROWS), F32), pltpu.VMEM((WIDTH, ROWS), F32)],
        compiler_params=params(14),
        cost_estimate=cost(5),
        name="project",
    )(at, ordered, grad, *weights)


def backward_kernel(q, k, v, mixed_grad, out, probs_ref, message, *scratch):
    q_grad, k_grad, v_grad, staged, sems = scratch
    for j in range(PLACES):
        pairs = range(HEADS // 2)
        grads = [pair(mixed_grad, j, n) for n in pairs]
        through = [dot(pair(v, j, n), grads[n], ((1,), (1,))) for n in pairs]
        scores = []
        for n in pairs:
            probs = probs_ref[HEADS // 2 * j + n]
            probs_low = probs.astype(BF)
            put_pair(v_grad, j, n, dot(probs_low, grads[n]).astype(BF))
            inner = jnp.sum(probs_low.astype(F32) * through[n], axis=0, keepdims=True)
            scores.append((probs * (through[n] - inner)).astype(BF))
        for n in pairs:
            put_pair(k_grad, j, n, (dot(scores[n], pair(q, j, n)) * FACTOR).astype(BF))
            put_pair(q_grad, j, n, (dot(scores[n], pair(k, j, n), ((0,), (0,))) * FACTOR).astype(BF))
        pack((out, q_grad, k_grad, v_grad), j, staged.at[j])
        message_copy(staged, message, sems, j).start()
    for j in range(PLACES):
        message_copy(staged, message, sems, j).wait()


def backward_call(*arrays):
    return pl.pallas_call(
        backward_kernel,
        in_specs=[VMEM] * 6,
        out_specs=ANY,
        out_shape=message_shape,
        scratch_shapes=[rows_held] * 3 + [message_held, pltpu.SemaphoreType.DMA((PLACES,))],
        compiler_params=params(14),
        cost_estimate=cost(5),
        name="backward",
    )(*arrays)


def seq_shift(dy, dz, dc):
    seq = np.arange(SEQ).reshape(NY, NZ, 2)
    return [
        (int(seq[y, z, c]), int(seq[(y + dy) % NY, (z + dz) % NZ, c ^ dc]))
        for y in range(NY)
        for z in range(NZ)
        for c in range(2)
    ]


def seq_flip(bit):
    seq = np.arange(SEQ).reshape(NY, NZ, 2)
    return [
        (int(seq[y, z, c]), int(seq[y, z ^ bit, c])) for y in range(NY) for z in range(NZ) for c in range(2)
    ]


def add_up(parts):
    total = parts[0].astype(F32)
    for part in parts[1:]:
        total = total + part.astype(F32)
    return total


def along_x(x, shift):
    return lax.ppermute(x, "dp", [(i, (i + shift) % NX) for i in range(NX)])


def reduce_x(parts):
    return add_up([parts[0]] + [along_x(parts[d], d) for d in (2, 1, 3)]).astype(BF)


def reduce_y(chip):
    chip = chip.reshape(NY, NZ // 2 * STRIP, QUARTER)
    came = [lax.ppermute(chip[d], "seq", seq_shift(d, 0, 0)) for d in (2, 1, 3)]
    return add_up([chip[0]] + came).astype(BF).reshape(NZ // 2, STRIP, QUARTER)


def reduce_z_pairs(strips):
    at = lax.axis_index("seq") // 4 % (NZ // 2)
    pairs = strips.reshape(NZ // 2, 2, STRIP, QUARTER)
    flips = (2, 1, 3)
    picked = [lax.dynamic_index_in_dim(pairs, at ^ n, 0, keepdims=False) for n in (0,) + flips]
    own, *away = lax.optimization_barrier(picked)
    return add_up([own] + [lax.ppermute(x, "seq", seq_flip(2 * n)) for x, n in zip(away, flips)])


def reduce_z_last(pair):
    odd = lax.axis_index("seq") // 2 % 2 == 1
    came = lax.ppermute(jnp.where(odd, pair[0], pair[1]).astype(BF), "seq", seq_flip(1))
    return add_up([jnp.where(odd, pair[1], pair[0]), came])


def gather_x(own):
    came = {d: along_x(own, d) for d in (2, 1, 3)}
    place = lax.axis_index("dp")
    quarters = [lax.select_n((place - n) % NX, own, came[1], came[2], came[3]) for n in range(NX)]
    return jnp.concatenate(quarters, axis=1)


def gather_weight_even(out_weight):
    place = lax.axis_index("dp")
    own = lax.select_n(place, *[out_weight[:, QUARTER * n : QUARTER * n + QUARTER] for n in range(NX)])
    came = [lax.ppermute(own, "seq", seq_flip(n)) for n in (4, 2, 6)]
    return jnp.stack([own, came[1], came[0], came[2]])


def gather_weight_z(even, odd):
    at = lax.axis_index("seq") // 2 % NZ
    both = jnp.stack([even, odd], axis=1).reshape(NZ, STRIP, QUARTER)
    for bit in (1, 2, 4):
        halves = both.reshape(NZ // (2 * bit), 2, bit, STRIP, QUARTER)
        both = jnp.where(at & bit != 0, halves[:, ::-1], halves).reshape(NZ, STRIP, QUARTER)
    return both.reshape(NZ * STRIP, QUARTER)


def gather_weight_y(own):
    came = {d: lax.ppermute(own, "seq", seq_shift(NY - d, 0, 0)) for d in (1, 3, 2)}
    return jnp.concatenate([own, came[1], came[2], came[3]], axis=0)


def swap_cores(x):
    return lax.ppermute(x, "seq", seq_shift(0, 0, 1))


def exchange(message):
    return lax.all_to_all(message, "seq", split_axis=0, concat_axis=0, tiled=True)


def local(queries, key_field, value_field, out_grad, out_weight, frame_video):
    rank = lax.axis_index("seq")
    at = jnp.stack([rank % 2, lax.axis_index("dp"), rank // (2 * NZ), rank // 2 % NZ]).astype(jnp.int32)
    videos = jnp.concatenate([frame_video, frame_video], axis=1)

    flat = [x.reshape(ROWS, WIDTH) for x in (queries, key_field, value_field, out_grad)]
    message, even = lax.optimization_barrier((pack_call((0, 1), flat), gather_weight_even(out_weight)))
    message, even, odd = lax.optimization_barrier(
        (pack_call((2,), flat, message), even, lax.ppermute(even, "seq", seq_flip(1)))
    )
    own = gather_weight_y(gather_weight_z(even, odd))
    mid = HALF // 2
    left, right = along_x(own, 1), along_x(own, -1)
    pieces = [own, left, right, along_x(left[:mid], 1), along_x(right[mid:], -1)]
    weights = pieces + [swap_cores(piece) for piece in pieces]
    arrived, at, videos, weights = lax.optimization_barrier((exchange(message), at, videos, weights))
    q, k, v, g, probs, ordered, mine, theirs = forward_call(at, videos, arrived)
    came, came_g = swap_cores(theirs), swap_cores(g)
    out, mixed_grad = project_call(at, ordered, g, weights)
    message = backward_call(q, k, v, mixed_grad, out, probs)
    message, came, came_g = lax.optimization_barrier((message, came, came_g))
    parts = weight_call(at, mine, came, g, came_g)
    halves = [reduce_x(parts[:NX]), reduce_x(parts[NX:])]
    strips = jnp.concatenate([reduce_y(half) for half in halves], axis=0)
    came, pair = lax.optimization_barrier((exchange(message), reduce_z_pairs(strips)))
    results = unpack_call(came)
    weight_grad = gather_x(reduce_z_last(pair))
    return tuple(x.reshape(queries.shape) for x in results) + (weight_grad,)


def solution(mesh):
    placed = P("dp", "seq", None, None)
    return jax.shard_map(
        local,
        mesh=mesh,
        in_specs=(placed, placed, placed, placed, P("seq", None), P("dp", None)),
        out_specs=(placed, placed, placed, placed, P("seq", None)),
        check_vma=False,
    )
```

```python
import functools

import jax
import jax.numpy as jnp
import numpy as np
from jax import lax
from jax.experimental import pallas as pl
from jax.experimental.pallas import tpu as pltpu
from jax.sharding import PartitionSpec as P

HEAD = 128
HEADS = 12
WIDTH = HEAD * HEADS
HALF = WIDTH // 2
FRAMES = 64
PLACES = 3
ROWS = FRAMES * PLACES
NX, NY, NZ = 4, 4, 8
SEQ = NY * NZ * 2
STRIP = WIDTH // SEQ
QUARTER = WIDTH // NX
BF = jnp.bfloat16
F32 = jnp.float32
FACTOR = HEAD ** (-0.5)
MIB = 1 << 20


def params(mib):
    return pltpu.CompilerParams(vmem_limit_bytes=mib * MIB)


def cost(us):
    return pl.CostEstimate(flops=0, bytes_accessed=int(us * 3.5e6), transcendentals=0)


def dot(a, b, dims=((1,), (0,))):
    return lax.dot_general(a, b, (dims, ((), ())), preferred_element_type=F32)


def swap_matrix(to_blocks):
    a = lax.broadcasted_iota(jnp.int32, (256, 256), 0 if to_blocks else 1)
    b = lax.broadcasted_iota(jnp.int32, (256, 256), 1 if to_blocks else 0)
    return jnp.where(8 * (a % 32) + a // 32 == b, F32(1), F32(0)).astype(BF)


def pack(sources, place, out_ref):
    swap = swap_matrix(False)
    for half in range(2):
        rows = slice(FRAMES * place + 32 * half, FRAMES * place + 32 * half + 32)
        for tile in range(1):
            parts = [
                src[rows, HALF * e + 256 * tile : HALF * e + 256 * tile + HALF]
                for src in sources
                for e in range(2)
            ]
            mixed = dot(swap, jnp.concatenate(parts, axis=0))
            out_ref[256 * half : 256 * half + 256, 256 * tile : 256 * tile + HALF] = mixed.astype(BF)


def unpack(in_ref, place, sinks):
    swap = swap_matrix(True)
    for half in range(2):
        rows = slice(FRAMES * place + 32 * half, FRAMES * place + 32 * half + 32)
        for tile in range(1):
            at = HALF * place + 256 * tile
            piece = dot(swap, in_ref[256 * half : 256 * half + 256, at : at + HALF]).astype(BF)
            for n in range(8):
                col = HALF * (n % 2) + 256 * tile
                sinks[n // 2][rows, col : col + HALF] = piece[32 * n : 32 * n + 32]


def place_rows(place):
    return pl.ds(FRAMES * place, FRAMES)


def message_copy(staged, message, sems, place):
    return pltpu.make_async_copy(
        staged.at[place], message.at[:, pl.ds(HALF * place, HALF)], sems.at[place]
    )


def pack_kernel(places, a, b, c, d, *refs):
    message, *held, staged, in_sems, out_sems = refs[-8:]
    arrays = (a, b, c, d)
    came = {
        j: [
            pltpu.make_async_copy(
                src.at[place_rows(j)], dst.at[place_rows(j)], in_sems.at[4 * j + n]
            )
            for n, (src, dst) in enumerate(zip(arrays, held))
        ]
        for j in places
    }
    for j in places:
        for copy in came[j]:
            copy.start()
    for j in places:
        for copy in came[j]:
            copy.wait()
        pack(held, j, staged.at[j])
        message_copy(staged, message, out_sems, j).start()
    for j in places:
        message_copy(staged, message, out_sems, j).wait()


def unpack_kernel(in_ref, a, b, c, d, *scratch):
    held, sems = scratch[:4], scratch[4]
    arrays = (a, b, c, d)
    gone = [
        [
            pltpu.make_async_copy(src.at[place_rows(j)], dst.at[place_rows(j)], sems.at[4 * j + n])
            for n, (dst, src) in enumerate(zip(arrays, held))
        ]
        for j in range(PLACES)
    ]
    for j in range(PLACES):
        unpack(in_ref, j, held)
        for copy in gone[j]:
            copy.start()
    for copies in gone:
        for copy in copies:
            copy.wait()


VMEM = pl.BlockSpec(memory_space=pltpu.VMEM)
SMEM = pl.BlockSpec(memory_space=pltpu.SMEM)
ANY = pl.BlockSpec(memory_space=pl.ANY)
DMA = pltpu.SemaphoreType.DMA
rows_shape = jax.ShapeDtypeStruct((ROWS, WIDTH), BF)
message_shape = jax.ShapeDtypeStruct((8 * SEQ, PLACES * HALF), BF)
rows_held = pltpu.VMEM((ROWS, WIDTH), BF)
message_held = pltpu.VMEM((PLACES, 8 * SEQ, HALF), BF)
probs_shape = jax.ShapeDtypeStruct((HEADS // 2 * PLACES, 2 * FRAMES, 2 * FRAMES), F32)


def pack_call(places, arrays, message=None):
    rest = [] if message is None else [message]
    return pl.pallas_call(
        functools.partial(pack_kernel, places),
        in_specs=[ANY] * (4 + len(rest)),
        out_specs=ANY,
        out_shape=message_shape,
        input_output_aliases={4: 0} if rest else {},
        scratch_shapes=[rows_held] * 4
        + [message_held, DMA((4 * PLACES,)), DMA((PLACES,))],
        compiler_params=params(56),
        cost_estimate=cost(3),
        name="pack",
    )(*arrays, *rest)


def unpack_call(message):
    return pl.pallas_call(
        unpack_kernel,
        in_specs=[VMEM],
        out_specs=[ANY] * 4,
        out_shape=[rows_shape] * 4,
        scratch_shapes=[rows_held] * 4 + [DMA((4 * PLACES,))],
        compiler_params=params(12),
        cost_estimate=cost(3),
        name="unpack",
    )(message)


def pair(ref, place, n):
    at, rows = 2 * HEAD * n, slice(FRAMES * place, FRAMES * place + FRAMES)
    return jnp.concatenate([ref[rows, at : at + HEAD], ref[rows, at + HEAD : at + 2 * HEAD]], axis=0)


def put_pair(ref, place, n, value):
    at, rows = 2 * HEAD * n, slice(FRAMES * place, FRAMES * place + FRAMES)
    ref[rows, at : at + HEAD] = value[:FRAMES]
    ref[rows, at + HEAD : at + 2 * HEAD] = value[FRAMES:]


def strip_copies(at, copy):
    for side in range(2):
        core = at[0] if side == 0 else 1 - at[0]
        for dy in range(NY):
            for z in range(NZ):
                y = (at[2] + dy) % NY
                there = pl.multiple_of((y * NZ + z) * 2 * STRIP + core * STRIP, 8)
                copy(side, (dy * NZ + z) * STRIP, there)


PIECES = 5


def forward_place(j, allowed, q, k, v, mixed, probs_ref):
    pairs = range(HEADS // 2)
    logits = [dot(pair(k, j, n), pair(q, j, n), ((1,), (1,))) for n in pairs]
    lows = []
    for n in pairs:
        raw = jnp.where(allowed, logits[n] * FACTOR, F32(-1e30))
        shifted = jnp.exp(raw - jnp.max(raw, axis=0, keepdims=True))
        probs = shifted * (1 / jnp.sum(shifted, axis=0, keepdims=True))
        probs_ref[HEADS // 2 * j + n] = probs
        lows.append(probs.astype(BF))
    for n in pairs:
        put_pair(mixed, j, n, dot(lows[n], pair(v, j, n), ((0,), (0,))).astype(BF))


def project(at, bundle, weights, out, mixed_grad, strips, turned):
    def cols(shift, base=0):
        start = (at[1] + shift + NX) % NX * QUARTER + base
        return pl.ds(pl.multiple_of(start, QUARTER), QUARTER)

    totals = [None, None]
    for side in range(2):
        near, left, right, *far = (ref[...] for ref in weights[PIECES * side : PIECES * side + PIECES])
        pieces = (near, left, right, jnp.concatenate(far, axis=0))
        rows = bundle[:, HALF * side : HALF * side + HALF]
        turn = None
        for n, shifts in enumerate(((0, -1), (1, 2))):
            w = jnp.concatenate(pieces[2 * n : 2 * n + 2], axis=1)
            part = dot(rows, w)
            totals[n] = part if side == 0 else totals[n] + part
            g = jnp.concatenate([bundle[:, cols(shift, WIDTH)] for shift in shifts], axis=1)
            term = dot(w, g, ((1,), (1,)))
            turn = term if turn is None else turn + term
            if side == 1:
                total = totals[n].astype(BF)
                out[:, cols(shifts[0])] = total[:, :QUARTER]
                out[:, cols(shifts[1])] = total[:, QUARTER:]
        strips[side] = turn

    def copy(side, here, there):
        turned[pl.ds(there, STRIP), :] = strips[side, here : here + STRIP, :]

    strip_copies(at, copy)
    mixed_grad[...] = turned[...].T.astype(BF)


def backward_place(j, q, k, v, mixed_grad, probs_ref, q_grad, k_grad, v_grad):
    pairs = range(HEADS // 2)
    grads = [pair(mixed_grad, j, n) for n in pairs]
    through = [dot(pair(v, j, n), grads[n], ((1,), (1,))) for n in pairs]
    scores = []
    for n in pairs:
        probs = probs_ref[HEADS // 2 * j + n]
        probs_low = probs.astype(BF)
        put_pair(v_grad, j, n, dot(probs_low, grads[n]).astype(BF))
        inner = jnp.sum(probs_low.astype(F32) * through[n], axis=0, keepdims=True)
        scores.append((probs * (through[n] - inner)).astype(BF))
    for n in pairs:
        put_pair(k_grad, j, n, (dot(scores[n], pair(q, j, n)) * FACTOR).astype(BF))
        put_pair(q_grad, j, n, (dot(scores[n], pair(k, j, n), ((0,), (0,))) * FACTOR).astype(BF))


def middle_kernel(at, videos, arrived, *refs):
    pieces, (message, bundle_out), scratch = refs[: 2 * PIECES], refs[2 * PIECES : 2 * PIECES + 2], refs[2 * PIECES + 2 :]
    weights, scratch = scratch[: 2 * PIECES], scratch[2 * PIECES :]
    q, k, v, g, mixed, out, mixed_grad, q_grad, k_grad, v_grad = scratch[:10]
    in_ref, probs_ref, bundle, turned, strips, staged, in_sems, piece_sems, bundle_sem, out_sems = scratch[10:]
    parts = []
    for j in range(PLACES):
        cols = pl.ds(HALF * j, HALF)
        parts.append(pltpu.make_async_copy(arrived.at[:, cols], in_ref.at[:, cols], in_sems.at[j]))
        parts[j].start()
    came = [
        pltpu.make_async_copy(src, dst, piece_sems.at[n]) for n, (src, dst) in enumerate(zip(pieces, weights))
    ]
    for copy in came:
        copy.start()

    square = (2 * FRAMES, 2 * FRAMES)
    video = jnp.broadcast_to(videos[...], square)
    head = [lax.broadcasted_iota(jnp.int32, square, axis) // FRAMES for axis in range(2)]
    allowed = (video == video.T) & (head[0] == head[1])
    for j in range(PLACES):
        parts[j].wait()
        unpack(in_ref, j, (q, k, v, g))
        forward_place(j, allowed, q, k, v, mixed, probs_ref)

    turned[...] = mixed[...].astype(F32).T

    def take(side, here, there):
        strips[side, here : here + STRIP, :] = turned[pl.ds(there, STRIP), :]

    strip_copies(at, take)
    for side in range(2):
        bundle[:, HALF * side : HALF * side + HALF] = strips[side].T.astype(BF)
    bundle[:, WIDTH:] = g[...]
    gone = pltpu.make_async_copy(bundle, bundle_out, bundle_sem.at[0])
    gone.start()
    for copy in came:
        copy.wait()
    project(at, bundle, weights, out, mixed_grad, strips, turned)
    for j in range(PLACES):
        backward_place(j, q, k, v, mixed_grad, probs_ref, q_grad, k_grad, v_grad)
        pack((out, q_grad, k_grad, v_grad), j, staged.at[j])
        message_copy(staged, message, out_sems, j).start()
    gone.wait()
    for j in range(PLACES):
        message_copy(staged, message, out_sems, j).wait()


bundle_shape = jax.ShapeDtypeStruct((ROWS, 2 * WIDTH), BF)


def middle_call(at, videos, message, weights):
    strips_held = [pltpu.VMEM((WIDTH, ROWS), F32), pltpu.VMEM((2, HALF, ROWS), F32)]
    probs_held = pltpu.VMEM((HEADS // 2 * PLACES, 2 * FRAMES, 2 * FRAMES), F32)
    return pl.pallas_call(
        middle_kernel,
        in_specs=[SMEM, VMEM, ANY] + [ANY] * len(weights),
        out_specs=[ANY] * 2,
        out_shape=[message_shape, bundle_shape],
        scratch_shapes=[pltpu.VMEM(w.shape, BF) for w in weights]
        + [rows_held] * 10
        + [pltpu.VMEM(message_shape.shape, BF), probs_held, pltpu.VMEM(bundle_shape.shape, BF)]
        + strips_held
        + [message_held, DMA((PLACES,)), DMA((len(weights),)), DMA((1,)), DMA((PLACES,))],
        compiler_params=params(52),
        cost_estimate=cost(10),
        name="middle",
    )(at, videos, message, *weights)


def weight_kernel(at, bundle, other, *refs):
    outs, (held, other_held, low, high, in_sems, out_sems) = refs[: 2 * NX], refs[2 * NX :]
    staged, size = (low, high), NZ // 2 * STRIP
    came = [
        pltpu.make_async_copy(bundle, held, in_sems.at[0]),
        pltpu.make_async_copy(other, other_held, in_sems.at[1]),
    ]
    for copy in came:
        copy.start()
    for copy in came:
        copy.wait()
    sides = [
        (ref, ref[:, start : start + HALF].astype(F32).T.astype(BF))
        for ref, start in ((held, 0), (other_held, HALF))
    ]
    gone = []
    for d in range(0, NX, 2):
        total = None
        for ref, strips in sides:
            cols = [
                ref[:, pl.ds(pl.multiple_of((at[1] + d + i) % NX * QUARTER + WIDTH, QUARTER), QUARTER)]
                for i in range(2)
            ]
            part = dot(strips, jnp.concatenate(cols, axis=1))
            total = part if total is None else total + part
        total = total.astype(BF)
        for i in range(2):
            for half in range(2):
                n = NX * half + d + i
                for dy in range(NY):
                    row = (2 * dy + half) * size
                    piece = total[row : row + size, QUARTER * i : QUARTER * i + QUARTER]
                    staged[half][d + i, size * dy : size * dy + size, :] = piece
                gone.append(pltpu.make_async_copy(staged[half].at[d + i], outs[n], out_sems.at[n]))
                gone[-1].start()
    for copy in gone:
        copy.wait()


def weight_call(at, bundle, other):
    return pl.pallas_call(
        weight_kernel,
        in_specs=[SMEM] + [ANY] * 2,
        out_specs=[ANY] * (2 * NX),
        out_shape=[jax.ShapeDtypeStruct((HALF // 2, QUARTER), BF)] * (2 * NX),
        scratch_shapes=[pltpu.VMEM(bundle_shape.shape, BF)] * 2
        + [pltpu.VMEM((NX, HALF // 2, QUARTER), BF)] * 2
        + [DMA((2,)), DMA((2 * NX,))],
        compiler_params=params(52),
        cost_estimate=cost(4),
        name="weight",
    )(at, bundle, other)


def seq_shift(dy, dz, dc):
    seq = np.arange(SEQ).reshape(NY, NZ, 2)
    return [
        (int(seq[y, z, c]), int(seq[(y + dy) % NY, (z + dz) % NZ, c ^ dc]))
        for y in range(NY)
        for z in range(NZ)
        for c in range(2)
    ]


def seq_flip(bit):
    seq = np.arange(SEQ).reshape(NY, NZ, 2)
    return [
        (int(seq[y, z, c]), int(seq[y, z ^ bit, c])) for y in range(NY) for z in range(NZ) for c in range(2)
    ]


def add_up(parts):
    total = parts[0].astype(F32)
    for part in parts[1:]:
        total = total + part.astype(F32)
    return total


def along_x(x, shift):
    return lax.ppermute(x, "dp", [(i, (i + shift) % NX) for i in range(NX)])


def reduce_x(parts):
    return add_up([parts[0]] + [along_x(parts[d], d) for d in (2, 1, 3)]).astype(BF)


def reduce_y(chip):
    chip = chip.reshape(NY, NZ // 2 * STRIP, QUARTER)
    came = [lax.ppermute(chip[d], "seq", seq_shift(d, 0, 0)) for d in (2, 1, 3)]
    return add_up([chip[0]] + came).astype(BF).reshape(NZ // 2, STRIP, QUARTER)


def reduce_z_pairs(strips):
    at = lax.axis_index("seq") // 4 % (NZ // 2)
    pairs = strips.reshape(NZ // 2, 2, STRIP, QUARTER)
    flips = (2, 1, 3)
    picked = [lax.dynamic_index_in_dim(pairs, at ^ n, 0, keepdims=False) for n in (0,) + flips]
    own, *away = lax.optimization_barrier(picked)
    return add_up([own] + [lax.ppermute(x, "seq", seq_flip(2 * n)) for x, n in zip(away, flips)])


def reduce_z_last(pair):
    odd = lax.axis_index("seq") // 2 % 2 == 1
    came = lax.ppermute(jnp.where(odd, pair[0], pair[1]).astype(BF), "seq", seq_flip(1))
    return add_up([jnp.where(odd, pair[1], pair[0]), came])


def gather_x(own):
    came = {d: along_x(own, d) for d in (2, 1, 3)}
    place = lax.axis_index("dp")
    quarters = [lax.select_n((place - n) % NX, own, came[1], came[2], came[3]) for n in range(NX)]
    return jnp.concatenate(quarters, axis=1)


def gather_weight_even(out_weight):
    place = lax.axis_index("dp")
    own = lax.select_n(place, *[out_weight[:, QUARTER * n : QUARTER * n + QUARTER] for n in range(NX)])
    came = [lax.ppermute(own, "seq", seq_flip(n)) for n in (4, 2, 6)]
    return jnp.stack([own, came[1], came[0], came[2]])


def gather_weight_z(even, odd):
    at = lax.axis_index("seq") // 2 % NZ
    both = jnp.stack([even, odd], axis=1).reshape(NZ, STRIP, QUARTER)
    for bit in (1, 2, 4):
        halves = both.reshape(NZ // (2 * bit), 2, bit, STRIP, QUARTER)
        both = jnp.where(at & bit != 0, halves[:, ::-1], halves).reshape(NZ, STRIP, QUARTER)
    return both.reshape(NZ * STRIP, QUARTER)


def gather_weight_y(own):
    came = {d: lax.ppermute(own, "seq", seq_shift(NY - d, 0, 0)) for d in (1, 3, 2)}
    return jnp.concatenate([own, came[1], came[2], came[3]], axis=0)


def swap_cores(x):
    return lax.ppermute(x, "seq", seq_shift(0, 0, 1))


def exchange(message):
    return lax.all_to_all(message, "seq", split_axis=0, concat_axis=0, tiled=True)


def local(queries, key_field, value_field, out_grad, out_weight, frame_video):
    rank = lax.axis_index("seq")
    at = jnp.stack([rank % 2, lax.axis_index("dp"), rank // (2 * NZ), rank // 2 % NZ]).astype(jnp.int32)
    videos = jnp.concatenate([frame_video, frame_video], axis=1)

    flat = [x.reshape(ROWS, WIDTH) for x in (queries, key_field, value_field, out_grad)]
    message, even = lax.optimization_barrier((pack_call((0, 1), flat), gather_weight_even(out_weight)))
    message, even, odd = lax.optimization_barrier(
        (pack_call((2,), flat, message), even, lax.ppermute(even, "seq", seq_flip(1)))
    )
    own = gather_weight_y(gather_weight_z(even, odd))
    mid = HALF // 2
    left, right = along_x(own, 1), along_x(own, -1)
    pieces = [own, left, right, along_x(left[:mid], 1), along_x(right[mid:], -1)]
    weights = pieces + [swap_cores(piece) for piece in pieces]
    arrived, at, videos, weights = lax.optimization_barrier((exchange(message), at, videos, weights))
    message, bundle = middle_call(at, videos, arrived, weights)
    parts = weight_call(at, bundle, swap_cores(bundle))
    halves = [reduce_x(parts[:NX]), reduce_x(parts[NX:])]
    strips = jnp.concatenate([reduce_y(half) for half in halves], axis=0)
    came, pair = lax.optimization_barrier((exchange(message), reduce_z_pairs(strips)))
    results = unpack_call(came)
    weight_grad = gather_x(reduce_z_last(pair))
    return tuple(x.reshape(queries.shape) for x in results) + (weight_grad,)


def solution(mesh):
    placed = P("dp", "seq", None, None)
    return jax.shard_map(
        local,
        mesh=mesh,
        in_specs=(placed, placed, placed, placed, P("seq", None), P("dp", None)),
        out_specs=(placed, placed, placed, placed, P("seq", None)),
        check_vma=False,
    )
```

```python
import functools

import jax
import jax.numpy as jnp
import numpy as np
from jax import lax
from jax.experimental import pallas as pl
from jax.experimental.pallas import tpu as pltpu
from jax.sharding import PartitionSpec as P

HEAD = 128
HEADS = 12
WIDTH = HEAD * HEADS
HALF = WIDTH // 2
FRAMES = 64
PLACES = 3
ROWS = FRAMES * PLACES
NX, NY, NZ = 4, 4, 8
SEQ = NY * NZ * 2
STRIP = WIDTH // SEQ
QUARTER = WIDTH // NX
BF = jnp.bfloat16
F32 = jnp.float32
FACTOR = HEAD ** (-0.5)
MIB = 1 << 20


def params(mib):
    return pltpu.CompilerParams(vmem_limit_bytes=mib * MIB)


def cost(us):
    return pl.CostEstimate(flops=0, bytes_accessed=int(us * 3.5e6), transcendentals=0)


def dot(a, b, dims=((1,), (0,))):
    return lax.dot_general(a, b, (dims, ((), ())), preferred_element_type=F32)


def swap_matrix(to_blocks):
    a = lax.broadcasted_iota(jnp.int32, (256, 256), 0 if to_blocks else 1)
    b = lax.broadcasted_iota(jnp.int32, (256, 256), 1 if to_blocks else 0)
    return jnp.where(8 * (a % 32) + a // 32 == b, F32(1), F32(0)).astype(BF)


def pack(sources, place, out_ref):
    swap = swap_matrix(False)
    for half in range(2):
        rows = slice(FRAMES * place + 32 * half, FRAMES * place + 32 * half + 32)
        for tile in range(1):
            parts = [
                src[rows, HALF * e + 256 * tile : HALF * e + 256 * tile + HALF]
                for src in sources
                for e in range(2)
            ]
            mixed = dot(swap, jnp.concatenate(parts, axis=0))
            out_ref[256 * half : 256 * half + 256, 256 * tile : 256 * tile + HALF] = mixed.astype(BF)


def unpack(in_ref, place, sinks):
    swap = swap_matrix(True)
    for half in range(2):
        rows = slice(FRAMES * place + 32 * half, FRAMES * place + 32 * half + 32)
        for tile in range(1):
            at = HALF * place + 256 * tile
            piece = dot(swap, in_ref[256 * half : 256 * half + 256, at : at + HALF]).astype(BF)
            for n in range(8):
                col = HALF * (n % 2) + 256 * tile
                sinks[n // 2][rows, col : col + HALF] = piece[32 * n : 32 * n + 32]


def place_rows(place):
    return pl.ds(FRAMES * place, FRAMES)


def message_copy(staged, message, sems, place):
    return pltpu.make_async_copy(
        staged.at[place], message.at[:, pl.ds(HALF * place, HALF)], sems.at[place]
    )


def pack_kernel(places, a, b, c, d, *refs):
    message, *held, staged, in_sems, out_sems = refs[-8:]
    arrays = (a, b, c, d)
    came = {
        j: [
            pltpu.make_async_copy(
                src.at[place_rows(j)], dst.at[place_rows(j)], in_sems.at[4 * j + n]
            )
            for n, (src, dst) in enumerate(zip(arrays, held))
        ]
        for j in places
    }
    for j in places:
        for copy in came[j]:
            copy.start()
    for j in places:
        for copy in came[j]:
            copy.wait()
        pack(held, j, staged.at[j])
        message_copy(staged, message, out_sems, j).start()
    for j in places:
        message_copy(staged, message, out_sems, j).wait()


def unpack_kernel(in_ref, a, b, c, d, *scratch):
    held, sems = scratch[:4], scratch[4]
    arrays = (a, b, c, d)
    gone = [
        [
            pltpu.make_async_copy(src.at[place_rows(j)], dst.at[place_rows(j)], sems.at[4 * j + n])
            for n, (dst, src) in enumerate(zip(arrays, held))
        ]
        for j in range(PLACES)
    ]
    for j in range(PLACES):
        unpack(in_ref, j, held)
        for copy in gone[j]:
            copy.start()
    for copies in gone:
        for copy in copies:
            copy.wait()


VMEM = pl.BlockSpec(memory_space=pltpu.VMEM)
SMEM = pl.BlockSpec(memory_space=pltpu.SMEM)
ANY = pl.BlockSpec(memory_space=pl.ANY)
DMA = pltpu.SemaphoreType.DMA
rows_shape = jax.ShapeDtypeStruct((ROWS, WIDTH), BF)
message_shape = jax.ShapeDtypeStruct((8 * SEQ, PLACES * HALF), BF)
rows_held = pltpu.VMEM((ROWS, WIDTH), BF)
message_held = pltpu.VMEM((PLACES, 8 * SEQ, HALF), BF)
probs_shape = jax.ShapeDtypeStruct((HEADS // 2 * PLACES, 2 * FRAMES, 2 * FRAMES), F32)


def pack_call(places, arrays, message=None):
    rest = [] if message is None else [message]
    return pl.pallas_call(
        functools.partial(pack_kernel, places),
        in_specs=[ANY] * (4 + len(rest)),
        out_specs=ANY,
        out_shape=message_shape,
        input_output_aliases={4: 0} if rest else {},
        scratch_shapes=[rows_held] * 4
        + [message_held, DMA((4 * PLACES,)), DMA((PLACES,))],
        compiler_params=params(56),
        cost_estimate=cost(3),
        name="pack",
    )(*arrays, *rest)


def unpack_call(message):
    return pl.pallas_call(
        unpack_kernel,
        in_specs=[VMEM],
        out_specs=[ANY] * 4,
        out_shape=[rows_shape] * 4,
        scratch_shapes=[rows_held] * 4 + [DMA((4 * PLACES,))],
        compiler_params=params(12),
        cost_estimate=cost(3),
        name="unpack",
    )(message)


def pair(ref, place, n):
    at, rows = 2 * HEAD * n, slice(FRAMES * place, FRAMES * place + FRAMES)
    return jnp.concatenate([ref[rows, at : at + HEAD], ref[rows, at + HEAD : at + 2 * HEAD]], axis=0)


def put_pair(ref, place, n, value):
    at, rows = 2 * HEAD * n, slice(FRAMES * place, FRAMES * place + FRAMES)
    ref[rows, at : at + HEAD] = value[:FRAMES]
    ref[rows, at + HEAD : at + 2 * HEAD] = value[FRAMES:]


def strip_copies(at, copy):
    for side in range(2):
        core = at[0] if side == 0 else 1 - at[0]
        for dy in range(NY):
            for z in range(NZ):
                y = (at[2] + dy) % NY
                there = pl.multiple_of((y * NZ + z) * 2 * STRIP + core * STRIP, 8)
                copy(side, (dy * NZ + z) * STRIP, there)


PIECES = 5


def forward_place(j, allowed, q, k, v, mixed, probs_ref):
    pairs = range(HEADS // 2)
    logits = [dot(pair(k, j, n), pair(q, j, n), ((1,), (1,))) for n in pairs]
    lows = []
    for n in pairs:
        raw = jnp.where(allowed, logits[n] * FACTOR, F32(-1e30))
        shifted = jnp.exp(raw - jnp.max(raw, axis=0, keepdims=True))
        probs = shifted * (1 / jnp.sum(shifted, axis=0, keepdims=True))
        probs_ref[HEADS // 2 * j + n] = probs
        lows.append(probs.astype(BF))
    for n in pairs:
        put_pair(mixed, j, n, dot(lows[n], pair(v, j, n), ((0,), (0,))).astype(BF))


def project(at, bundle, weights, out, mixed_grad, strips, turned):
    def cols(shift, base=0):
        start = (at[1] + shift + NX) % NX * QUARTER + base
        return pl.ds(pl.multiple_of(start, QUARTER), QUARTER)

    totals = [None, None]
    for side in range(2):
        near, left, right, *far = (ref[...] for ref in weights[PIECES * side : PIECES * side + PIECES])
        pieces = (near, left, right, jnp.concatenate(far, axis=0))
        rows = bundle[:, HALF * side : HALF * side + HALF]
        turn = None
        for n, shifts in enumerate(((0, -1), (1, 2))):
            w = jnp.concatenate(pieces[2 * n : 2 * n + 2], axis=1)
            part = dot(rows, w)
            totals[n] = part if side == 0 else totals[n] + part
            g = jnp.concatenate([bundle[:, cols(shift, WIDTH)] for shift in shifts], axis=1)
            term = dot(w, g, ((1,), (1,)))
            turn = term if turn is None else turn + term
            if side == 1:
                total = totals[n].astype(BF)
                out[:, cols(shifts[0])] = total[:, :QUARTER]
                out[:, cols(shifts[1])] = total[:, QUARTER:]
        strips[side] = turn

    def copy(side, here, there):
        turned[pl.ds(there, STRIP), :] = strips[side, here : here + STRIP, :]

    strip_copies(at, copy)
    mixed_grad[...] = turned[...].T.astype(BF)


def backward_place(j, q, k, v, mixed_grad, probs_ref, q_grad, k_grad, v_grad):
    pairs = range(HEADS // 2)
    grads = [pair(mixed_grad, j, n) for n in pairs]
    through = [dot(pair(v, j, n), grads[n], ((1,), (1,))) for n in pairs]
    scores = []
    for n in pairs:
        probs = probs_ref[HEADS // 2 * j + n]
        probs_low = probs.astype(BF)
        put_pair(v_grad, j, n, dot(probs_low, grads[n]).astype(BF))
        inner = jnp.sum(probs_low.astype(F32) * through[n], axis=0, keepdims=True)
        scores.append((probs * (through[n] - inner)).astype(BF))
    for n in pairs:
        put_pair(k_grad, j, n, (dot(scores[n], pair(q, j, n)) * FACTOR).astype(BF))
        put_pair(q_grad, j, n, (dot(scores[n], pair(k, j, n), ((0,), (0,))) * FACTOR).astype(BF))


def middle_kernel(at, videos, arrived, *refs):
    pieces, (message, bundle_out), scratch = refs[: 2 * PIECES], refs[2 * PIECES : 2 * PIECES + 2], refs[2 * PIECES + 2 :]
    weights, scratch = scratch[: 2 * PIECES], scratch[2 * PIECES :]
    q, k, v, g, mixed, out, mixed_grad, q_grad, k_grad, v_grad = scratch[:10]
    in_ref, probs_ref, bundle, turned, strips, staged, in_sems, piece_sems, bundle_sem, out_sems = scratch[10:]
    parts = []
    for j in range(PLACES):
        cols = pl.ds(HALF * j, HALF)
        parts.append(pltpu.make_async_copy(arrived.at[:, cols], in_ref.at[:, cols], in_sems.at[j]))
        parts[j].start()
    came = [
        pltpu.make_async_copy(src, dst, piece_sems.at[n]) for n, (src, dst) in enumerate(zip(pieces, weights))
    ]
    for copy in came:
        copy.start()

    square = (2 * FRAMES, 2 * FRAMES)
    video = jnp.broadcast_to(videos[...], square)
    head = [lax.broadcasted_iota(jnp.int32, square, axis) // FRAMES for axis in range(2)]
    allowed = (video == video.T) & (head[0] == head[1])
    for j in range(PLACES):
        parts[j].wait()
        unpack(in_ref, j, (q, k, v, g))
        forward_place(j, allowed, q, k, v, mixed, probs_ref)

    turned[...] = mixed[...].astype(F32).T

    def take(side, here, there):
        strips[side, here : here + STRIP, :] = turned[pl.ds(there, STRIP), :]

    strip_copies(at, take)
    for side in range(2):
        bundle[:, HALF * side : HALF * side + HALF] = strips[side].T.astype(BF)
    bundle[:, WIDTH:] = g[...]
    gone = pltpu.make_async_copy(bundle, bundle_out, bundle_sem.at[0])
    gone.start()
    for copy in came:
        copy.wait()
    project(at, bundle, weights, out, mixed_grad, strips, turned)
    for j in range(PLACES):
        backward_place(j, q, k, v, mixed_grad, probs_ref, q_grad, k_grad, v_grad)
        pack((out, q_grad, k_grad, v_grad), j, staged.at[j])
        message_copy(staged, message, out_sems, j).start()
    gone.wait()
    for j in range(PLACES):
        message_copy(staged, message, out_sems, j).wait()


bundle_shape = jax.ShapeDtypeStruct((ROWS, 2 * WIDTH), BF)


def middle_call(at, videos, message, weights):
    strips_held = [pltpu.VMEM((WIDTH, ROWS), F32), pltpu.VMEM((2, HALF, ROWS), F32)]
    probs_held = pltpu.VMEM((HEADS // 2 * PLACES, 2 * FRAMES, 2 * FRAMES), F32)
    return pl.pallas_call(
        middle_kernel,
        in_specs=[SMEM, VMEM, ANY] + [ANY] * len(weights),
        out_specs=[ANY] * 2,
        out_shape=[message_shape, bundle_shape],
        scratch_shapes=[pltpu.VMEM(w.shape, BF) for w in weights]
        + [rows_held] * 10
        + [pltpu.VMEM(message_shape.shape, BF), probs_held, pltpu.VMEM(bundle_shape.shape, BF)]
        + strips_held
        + [message_held, DMA((PLACES,)), DMA((len(weights),)), DMA((1,)), DMA((PLACES,))],
        compiler_params=params(52),
        cost_estimate=cost(10),
        name="middle",
    )(at, videos, message, *weights)


def weight_kernel(at, bundle, other, *refs):
    outs, (held, other_held, low, high, in_sems, out_sems) = refs[: 2 * NX], refs[2 * NX :]
    staged, size = (low, high), NZ // 2 * STRIP
    first, rest, came = pl.ds(0, HALF), pl.ds(WIDTH, WIDTH), []
    for n, (src, dst, cols) in enumerate(
        ((bundle, held, first), (other, other_held, pl.ds(HALF, HALF)), (bundle, held, rest), (other, other_held, rest))
    ):
        came.append(pltpu.make_async_copy(src.at[:, cols], dst.at[:, cols], in_sems.at[n]))
        came[n].start()
    sides = []
    for n, (ref, start) in enumerate(((held, 0), (other_held, HALF))):
        came[n].wait()
        sides.append((ref, ref[:, start : start + HALF].astype(F32).T.astype(BF)))
    for copy in came[2:]:
        copy.wait()
    gone = []
    for d in range(0, NX, 2):
        total = None
        for ref, strips in sides:
            cols = [
                ref[:, pl.ds(pl.multiple_of((at[1] + d + i) % NX * QUARTER + WIDTH, QUARTER), QUARTER)]
                for i in range(2)
            ]
            part = dot(strips, jnp.concatenate(cols, axis=1))
            total = part if total is None else total + part
        total = total.astype(BF)
        for i in range(2):
            for half in range(2):
                n = NX * half + d + i
                for dy in range(NY):
                    row = (2 * dy + half) * size
                    piece = total[row : row + size, QUARTER * i : QUARTER * i + QUARTER]
                    staged[half][d + i, size * dy : size * dy + size, :] = piece
                gone.append(pltpu.make_async_copy(staged[half].at[d + i], outs[n], out_sems.at[n]))
                gone[-1].start()
    for copy in gone:
        copy.wait()


def weight_call(at, bundle, other):
    return pl.pallas_call(
        weight_kernel,
        in_specs=[SMEM] + [ANY] * 2,
        out_specs=[ANY] * (2 * NX),
        out_shape=[jax.ShapeDtypeStruct((HALF // 2, QUARTER), BF)] * (2 * NX),
        scratch_shapes=[pltpu.VMEM(bundle_shape.shape, BF)] * 2
        + [pltpu.VMEM((NX, HALF // 2, QUARTER), BF)] * 2
        + [DMA((4,)), DMA((2 * NX,))],
        compiler_params=params(52),
        cost_estimate=cost(4),
        name="weight",
    )(at, bundle, other)


def seq_shift(dy, dz, dc):
    seq = np.arange(SEQ).reshape(NY, NZ, 2)
    return [
        (int(seq[y, z, c]), int(seq[(y + dy) % NY, (z + dz) % NZ, c ^ dc]))
        for y in range(NY)
        for z in range(NZ)
        for c in range(2)
    ]


def seq_flip(bit):
    seq = np.arange(SEQ).reshape(NY, NZ, 2)
    return [
        (int(seq[y, z, c]), int(seq[y, z ^ bit, c])) for y in range(NY) for z in range(NZ) for c in range(2)
    ]


def add_up(parts):
    total = parts[0].astype(F32)
    for part in parts[1:]:
        total = total + part.astype(F32)
    return total


def along_x(x, shift):
    return lax.ppermute(x, "dp", [(i, (i + shift) % NX) for i in range(NX)])


def reduce_x(parts):
    return add_up([parts[0]] + [along_x(parts[d], d) for d in (2, 1, 3)]).astype(BF)


def reduce_y(chip):
    chip = chip.reshape(NY, NZ // 2 * STRIP, QUARTER)
    came = [lax.ppermute(chip[d], "seq", seq_shift(d, 0, 0)) for d in (2, 1, 3)]
    return add_up([chip[0]] + came).astype(BF).reshape(NZ // 2, STRIP, QUARTER)


def reduce_z_pairs(strips):
    at = lax.axis_index("seq") // 4 % (NZ // 2)
    pairs = strips.reshape(NZ // 2, 2, STRIP, QUARTER)
    flips = (2, 1, 3)
    picked = [lax.dynamic_index_in_dim(pairs, at ^ n, 0, keepdims=False) for n in (0,) + flips]
    own, *away = lax.optimization_barrier(picked)
    return add_up([own] + [lax.ppermute(x, "seq", seq_flip(2 * n)) for x, n in zip(away, flips)])


def reduce_z_last(pair):
    odd = lax.axis_index("seq") // 2 % 2 == 1
    came = lax.ppermute(jnp.where(odd, pair[0], pair[1]).astype(BF), "seq", seq_flip(1))
    return add_up([jnp.where(odd, pair[1], pair[0]), came])


def gather_x(own):
    came = {d: along_x(own, d) for d in (2, 1, 3)}
    place = lax.axis_index("dp")
    quarters = [lax.select_n((place - n) % NX, own, came[1], came[2], came[3]) for n in range(NX)]
    return jnp.concatenate(quarters, axis=1)


def gather_weight_even(out_weight):
    place = lax.axis_index("dp")
    own = lax.select_n(place, *[out_weight[:, QUARTER * n : QUARTER * n + QUARTER] for n in range(NX)])
    came = [lax.ppermute(own, "seq", seq_flip(n)) for n in (4, 2, 6)]
    return jnp.stack([own, came[1], came[0], came[2]])


def gather_weight_z(even, odd):
    at = lax.axis_index("seq") // 2 % NZ
    both = jnp.stack([even, odd], axis=1).reshape(NZ, STRIP, QUARTER)
    for bit in (1, 2, 4):
        halves = both.reshape(NZ // (2 * bit), 2, bit, STRIP, QUARTER)
        both = jnp.where(at & bit != 0, halves[:, ::-1], halves).reshape(NZ, STRIP, QUARTER)
    return both.reshape(NZ * STRIP, QUARTER)


def gather_weight_y(own):
    came = {d: lax.ppermute(own, "seq", seq_shift(NY - d, 0, 0)) for d in (1, 3, 2)}
    return jnp.concatenate([own, came[1], came[2], came[3]], axis=0)


def swap_cores(x):
    return lax.ppermute(x, "seq", seq_shift(0, 0, 1))


def exchange(message):
    return lax.all_to_all(message, "seq", split_axis=0, concat_axis=0, tiled=True)


def local(queries, key_field, value_field, out_grad, out_weight, frame_video):
    rank = lax.axis_index("seq")
    at = jnp.stack([rank % 2, lax.axis_index("dp"), rank // (2 * NZ), rank // 2 % NZ]).astype(jnp.int32)
    videos = jnp.concatenate([frame_video, frame_video], axis=1)

    flat = [x.reshape(ROWS, WIDTH) for x in (queries, key_field, value_field, out_grad)]
    message, even = lax.optimization_barrier((pack_call((0, 1), flat), gather_weight_even(out_weight)))
    message, even, odd = lax.optimization_barrier(
        (pack_call((2,), flat, message), even, lax.ppermute(even, "seq", seq_flip(1)))
    )
    own = gather_weight_y(gather_weight_z(even, odd))
    mid = HALF // 2
    left, right = along_x(own, 1), along_x(own, -1)
    pieces = [own, left, right, along_x(left[:mid], 1), along_x(right[mid:], -1)]
    weights = pieces + [swap_cores(piece) for piece in pieces]
    arrived, at, videos, weights = lax.optimization_barrier((exchange(message), at, videos, weights))
    message, bundle = middle_call(at, videos, arrived, weights)
    parts = weight_call(at, bundle, swap_cores(bundle))
    halves = [reduce_x(parts[:NX]), reduce_x(parts[NX:])]
    strips = jnp.concatenate([reduce_y(half) for half in halves], axis=0)
    came, pair = lax.optimization_barrier((exchange(message), reduce_z_pairs(strips)))
    results, strip = lax.optimization_barrier((unpack_call(came), reduce_z_last(pair)))
    weight_grad = gather_x(strip)
    return tuple(x.reshape(queries.shape) for x in results) + (weight_grad,)


def solution(mesh):
    placed = P("dp", "seq", None, None)
    return jax.shard_map(
        local,
        mesh=mesh,
        in_specs=(placed, placed, placed, placed, P("seq", None), P("dp", None)),
        out_specs=(placed, placed, placed, placed, P("seq", None)),
        check_vma=False,
    )
```

```python
import functools

import jax
import jax.numpy as jnp
import numpy as np
from jax import lax
from jax.experimental import pallas as pl
from jax.experimental.pallas import tpu as pltpu
from jax.sharding import PartitionSpec as P

HEAD = 128
HEADS = 12
WIDTH = HEAD * HEADS
HALF = WIDTH // 2
FRAMES = 64
PLACES = 3
ROWS = FRAMES * PLACES
NX, NY, NZ = 4, 4, 8
SEQ = NY * NZ * 2
STRIP = WIDTH // SEQ
QUARTER = WIDTH // NX
BF = jnp.bfloat16
F32 = jnp.float32
FACTOR = HEAD ** (-0.5)
MIB = 1 << 20


def params(mib):
    return pltpu.CompilerParams(vmem_limit_bytes=mib * MIB)


def cost(us):
    return pl.CostEstimate(flops=0, bytes_accessed=int(us * 3.5e6), transcendentals=0)


def dot(a, b, dims=((1,), (0,))):
    return lax.dot_general(a, b, (dims, ((), ())), preferred_element_type=F32)


def swap_matrix(to_blocks):
    a = lax.broadcasted_iota(jnp.int32, (256, 256), 0 if to_blocks else 1)
    b = lax.broadcasted_iota(jnp.int32, (256, 256), 1 if to_blocks else 0)
    return jnp.where(8 * (a % 32) + a // 32 == b, F32(1), F32(0)).astype(BF)


def pack(sources, place, out_ref):
    swap = swap_matrix(False)
    for half in range(2):
        rows = slice(FRAMES * place + 32 * half, FRAMES * place + 32 * half + 32)
        for tile in range(1):
            parts = [
                src[rows, HALF * e + 256 * tile : HALF * e + 256 * tile + HALF]
                for src in sources
                for e in range(2)
            ]
            mixed = dot(swap, jnp.concatenate(parts, axis=0))
            out_ref[256 * half : 256 * half + 256, 256 * tile : 256 * tile + HALF] = mixed.astype(BF)


def unpack(in_ref, place, sinks):
    swap = swap_matrix(True)
    for half in range(2):
        rows = slice(FRAMES * place + 32 * half, FRAMES * place + 32 * half + 32)
        for tile in range(1):
            at = HALF * place + 256 * tile
            piece = dot(swap, in_ref[256 * half : 256 * half + 256, at : at + HALF]).astype(BF)
            for n in range(8):
                col = HALF * (n % 2) + 256 * tile
                sinks[n // 2][rows, col : col + HALF] = piece[32 * n : 32 * n + 32]


def place_rows(place):
    return pl.ds(FRAMES * place, FRAMES)


def message_copy(staged, message, sems, place):
    return pltpu.make_async_copy(
        staged.at[place], message.at[:, pl.ds(HALF * place, HALF)], sems.at[place]
    )


def pack_kernel(places, a, b, c, d, *refs):
    message, *held, staged, in_sems, out_sems = refs[-8:]
    arrays = (a, b, c, d)
    came = {
        j: [
            pltpu.make_async_copy(
                src.at[place_rows(j)], dst.at[place_rows(j)], in_sems.at[4 * j + n]
            )
            for n, (src, dst) in enumerate(zip(arrays, held))
        ]
        for j in places
    }
    for j in places:
        for copy in came[j]:
            copy.start()
    for j in places:
        for copy in came[j]:
            copy.wait()
        pack(held, j, staged.at[j])
        message_copy(staged, message, out_sems, j).start()
    for j in places:
        message_copy(staged, message, out_sems, j).wait()


def unpack_kernel(message, a, b, c, d, *scratch):
    held, (in_ref, in_sems, sems) = scratch[:4], scratch[4:]
    came = []
    for j in range(PLACES):
        cols = pl.ds(HALF * j, HALF)
        came.append(pltpu.make_async_copy(message.at[:, cols], in_ref.at[:, cols], in_sems.at[j]))
        came[j].start()
    arrays = (a, b, c, d)
    gone = [
        [
            pltpu.make_async_copy(src.at[place_rows(j)], dst.at[place_rows(j)], sems.at[4 * j + n])
            for n, (dst, src) in enumerate(zip(arrays, held))
        ]
        for j in range(PLACES)
    ]
    for j in range(PLACES):
        came[j].wait()
        unpack(in_ref, j, held)
        for copy in gone[j]:
            copy.start()
    for copies in gone:
        for copy in copies:
            copy.wait()


VMEM = pl.BlockSpec(memory_space=pltpu.VMEM)
SMEM = pl.BlockSpec(memory_space=pltpu.SMEM)
ANY = pl.BlockSpec(memory_space=pl.ANY)
DMA = pltpu.SemaphoreType.DMA
rows_shape = jax.ShapeDtypeStruct((ROWS, WIDTH), BF)
message_shape = jax.ShapeDtypeStruct((8 * SEQ, PLACES * HALF), BF)
rows_held = pltpu.VMEM((ROWS, WIDTH), BF)
message_held = pltpu.VMEM((PLACES, 8 * SEQ, HALF), BF)
probs_shape = jax.ShapeDtypeStruct((HEADS // 2 * PLACES, 2 * FRAMES, 2 * FRAMES), F32)


def pack_call(places, arrays, message=None):
    rest = [] if message is None else [message]
    return pl.pallas_call(
        functools.partial(pack_kernel, places),
        in_specs=[ANY] * (4 + len(rest)),
        out_specs=ANY,
        out_shape=message_shape,
        input_output_aliases={4: 0} if rest else {},
        scratch_shapes=[rows_held] * 4
        + [message_held, DMA((4 * PLACES,)), DMA((PLACES,))],
        compiler_params=params(56),
        cost_estimate=cost(3),
        name="pack",
    )(*arrays, *rest)


def unpack_call(message):
    return pl.pallas_call(
        unpack_kernel,
        in_specs=[ANY],
        out_specs=[ANY] * 4,
        out_shape=[rows_shape] * 4,
        scratch_shapes=[rows_held] * 4
        + [pltpu.VMEM(message_shape.shape, BF), DMA((PLACES,)), DMA((4 * PLACES,))],
        compiler_params=params(58),
        cost_estimate=cost(3),
        name="unpack",
    )(message)


def pair(ref, place, n):
    at, rows = 2 * HEAD * n, slice(FRAMES * place, FRAMES * place + FRAMES)
    return jnp.concatenate([ref[rows, at : at + HEAD], ref[rows, at + HEAD : at + 2 * HEAD]], axis=0)


def put_pair(ref, place, n, value):
    at, rows = 2 * HEAD * n, slice(FRAMES * place, FRAMES * place + FRAMES)
    ref[rows, at : at + HEAD] = value[:FRAMES]
    ref[rows, at + HEAD : at + 2 * HEAD] = value[FRAMES:]


def strip_copies(at, copy):
    for side in range(2):
        core = at[0] if side == 0 else 1 - at[0]
        for dy in range(NY):
            for z in range(NZ):
                y = (at[2] + dy) % NY
                there = pl.multiple_of((y * NZ + z) * 2 * STRIP + core * STRIP, 8)
                copy(side, (dy * NZ + z) * STRIP, there)


PIECES = 5


def forward_place(j, allowed, q, k, v, mixed, probs_ref):
    pairs = range(HEADS // 2)
    logits = [dot(pair(k, j, n), pair(q, j, n), ((1,), (1,))) for n in pairs]
    lows = []
    for n in pairs:
        raw = jnp.where(allowed, logits[n] * FACTOR, F32(-1e30))
        shifted = jnp.exp(raw - jnp.max(raw, axis=0, keepdims=True))
        probs = shifted * (1 / jnp.sum(shifted, axis=0, keepdims=True))
        probs_ref[HEADS // 2 * j + n] = probs
        lows.append(probs.astype(BF))
    for n in pairs:
        put_pair(mixed, j, n, dot(lows[n], pair(v, j, n), ((0,), (0,))).astype(BF))


def project(at, bundle, weights, out, mixed_grad, strips, turned):
    def cols(shift, base=0):
        start = (at[1] + shift + NX) % NX * QUARTER + base
        return pl.ds(pl.multiple_of(start, QUARTER), QUARTER)

    totals = [None, None]
    for side in range(2):
        near, left, right, *far = (ref[...] for ref in weights[PIECES * side : PIECES * side + PIECES])
        pieces = (near, left, right, jnp.concatenate(far, axis=0))
        rows = bundle[:, HALF * side : HALF * side + HALF]
        turn = None
        for n, shifts in enumerate(((0, -1), (1, 2))):
            w = jnp.concatenate(pieces[2 * n : 2 * n + 2], axis=1)
            part = dot(rows, w)
            totals[n] = part if side == 0 else totals[n] + part
            g = jnp.concatenate([bundle[:, cols(shift, WIDTH)] for shift in shifts], axis=1)
            term = dot(w, g, ((1,), (1,)))
            turn = term if turn is None else turn + term
            if side == 1:
                total = totals[n].astype(BF)
                out[:, cols(shifts[0])] = total[:, :QUARTER]
                out[:, cols(shifts[1])] = total[:, QUARTER:]
        strips[side] = turn

    def copy(side, here, there):
        turned[pl.ds(there, STRIP), :] = strips[side, here : here + STRIP, :]

    strip_copies(at, copy)
    mixed_grad[...] = turned[...].T.astype(BF)


def backward_place(j, q, k, v, mixed_grad, probs_ref, q_grad, k_grad, v_grad):
    pairs = range(HEADS // 2)
    grads = [pair(mixed_grad, j, n) for n in pairs]
    through = [dot(pair(v, j, n), grads[n], ((1,), (1,))) for n in pairs]
    scores = []
    for n in pairs:
        probs = probs_ref[HEADS // 2 * j + n]
        probs_low = probs.astype(BF)
        put_pair(v_grad, j, n, dot(probs_low, grads[n]).astype(BF))
        inner = jnp.sum(probs_low.astype(F32) * through[n], axis=0, keepdims=True)
        scores.append((probs * (through[n] - inner)).astype(BF))
    for n in pairs:
        put_pair(k_grad, j, n, (dot(scores[n], pair(q, j, n)) * FACTOR).astype(BF))
        put_pair(q_grad, j, n, (dot(scores[n], pair(k, j, n), ((0,), (0,))) * FACTOR).astype(BF))


def middle_kernel(at, videos, arrived, *refs):
    pieces, (message, bundle_out), scratch = refs[: 2 * PIECES], refs[2 * PIECES : 2 * PIECES + 2], refs[2 * PIECES + 2 :]
    weights, scratch = scratch[: 2 * PIECES], scratch[2 * PIECES :]
    q, k, v, g, mixed, out, mixed_grad, q_grad, k_grad, v_grad = scratch[:10]
    in_ref, probs_ref, bundle, turned, strips, staged, in_sems, piece_sems, bundle_sem, out_sems = scratch[10:]
    parts = []
    for j in range(PLACES):
        cols = pl.ds(HALF * j, HALF)
        parts.append(pltpu.make_async_copy(arrived.at[:, cols], in_ref.at[:, cols], in_sems.at[j]))
        parts[j].start()
    came = [
        pltpu.make_async_copy(src, dst, piece_sems.at[n]) for n, (src, dst) in enumerate(zip(pieces, weights))
    ]
    for copy in came:
        copy.start()

    square = (2 * FRAMES, 2 * FRAMES)
    video = jnp.broadcast_to(videos[...], square)
    head = [lax.broadcasted_iota(jnp.int32, square, axis) // FRAMES for axis in range(2)]
    allowed = (video == video.T) & (head[0] == head[1])
    for j in range(PLACES):
        parts[j].wait()
        unpack(in_ref, j, (q, k, v, g))
        forward_place(j, allowed, q, k, v, mixed, probs_ref)

    turned[...] = mixed[...].astype(F32).T

    def take(side, here, there):
        strips[side, here : here + STRIP, :] = turned[pl.ds(there, STRIP), :]

    strip_copies(at, take)
    for side in range(2):
        bundle[:, HALF * side : HALF * side + HALF] = strips[side].T.astype(BF)
    bundle[:, WIDTH:] = g[...]
    gone = pltpu.make_async_copy(bundle, bundle_out, bundle_sem.at[0])
    gone.start()
    for copy in came:
        copy.wait()
    project(at, bundle, weights, out, mixed_grad, strips, turned)
    for j in range(PLACES):
        backward_place(j, q, k, v, mixed_grad, probs_ref, q_grad, k_grad, v_grad)
        pack((out, q_grad, k_grad, v_grad), j, staged.at[j])
        message_copy(staged, message, out_sems, j).start()
    gone.wait()
    for j in range(PLACES):
        message_copy(staged, message, out_sems, j).wait()


bundle_shape = jax.ShapeDtypeStruct((ROWS, 2 * WIDTH), BF)


def middle_call(at, videos, message, weights):
    strips_held = [pltpu.VMEM((WIDTH, ROWS), F32), pltpu.VMEM((2, HALF, ROWS), F32)]
    probs_held = pltpu.VMEM((HEADS // 2 * PLACES, 2 * FRAMES, 2 * FRAMES), F32)
    return pl.pallas_call(
        middle_kernel,
        in_specs=[SMEM, VMEM, ANY] + [ANY] * len(weights),
        out_specs=[ANY] * 2,
        out_shape=[message_shape, bundle_shape],
        scratch_shapes=[pltpu.VMEM(w.shape, BF) for w in weights]
        + [rows_held] * 10
        + [pltpu.VMEM(message_shape.shape, BF), probs_held, pltpu.VMEM(bundle_shape.shape, BF)]
        + strips_held
        + [message_held, DMA((PLACES,)), DMA((len(weights),)), DMA((1,)), DMA((PLACES,))],
        compiler_params=params(52),
        cost_estimate=cost(10),
        name="middle",
    )(at, videos, message, *weights)


def weight_kernel(at, bundle, other, *outs):
    size = NZ // 2 * STRIP
    sides = [
        (ref, ref[:, start : start + HALF].astype(F32).T.astype(BF)) for ref, start in ((bundle, 0), (other, HALF))
    ]
    for d in range(0, NX, 2):
        total = None
        for ref, strips in sides:
            cols = [
                ref[:, pl.ds(pl.multiple_of((at[1] + d + i) % NX * QUARTER + WIDTH, QUARTER), QUARTER)]
                for i in range(2)
            ]
            part = dot(strips, jnp.concatenate(cols, axis=1))
            total = part if total is None else total + part
        total = total.astype(BF)
        for i in range(2):
            for half in range(2):
                for dy in range(NY):
                    row = (2 * dy + half) * size
                    piece = total[row : row + size, QUARTER * i : QUARTER * i + QUARTER]
                    outs[NX * half + d + i][size * dy : size * dy + size, :] = piece


def weight_call(at, bundle, other):
    return pl.pallas_call(
        weight_kernel,
        in_specs=[SMEM] + [VMEM] * 2,
        out_specs=[VMEM] * (2 * NX),
        out_shape=[jax.ShapeDtypeStruct((HALF // 2, QUARTER), BF)] * (2 * NX),
        compiler_params=params(12),
        cost_estimate=cost(3),
        name="weight",
    )(at, bundle, other)


def seq_shift(dy, dz, dc):
    seq = np.arange(SEQ).reshape(NY, NZ, 2)
    return [
        (int(seq[y, z, c]), int(seq[(y + dy) % NY, (z + dz) % NZ, c ^ dc]))
        for y in range(NY)
        for z in range(NZ)
        for c in range(2)
    ]


def seq_flip(bit):
    seq = np.arange(SEQ).reshape(NY, NZ, 2)
    return [
        (int(seq[y, z, c]), int(seq[y, z ^ bit, c])) for y in range(NY) for z in range(NZ) for c in range(2)
    ]


def add_up(parts):
    total = parts[0].astype(F32)
    for part in parts[1:]:
        total = total + part.astype(F32)
    return total


def along_x(x, shift):
    return lax.ppermute(x, "dp", [(i, (i + shift) % NX) for i in range(NX)])


def reduce_x(parts):
    return add_up([parts[0]] + [along_x(parts[d], d) for d in (2, 1, 3)]).astype(BF)


def reduce_y(chip):
    chip = chip.reshape(NY, NZ // 2 * STRIP, QUARTER)
    came = [lax.ppermute(chip[d], "seq", seq_shift(d, 0, 0)) for d in (2, 1, 3)]
    return add_up([chip[0]] + came).astype(BF).reshape(NZ // 2, STRIP, QUARTER)


def reduce_z_pairs(strips):
    at = lax.axis_index("seq") // 4 % (NZ // 2)
    pairs = strips.reshape(NZ // 2, 2, STRIP, QUARTER)
    flips = (2, 1, 3)
    picked = [lax.dynamic_index_in_dim(pairs, at ^ n, 0, keepdims=False) for n in (0,) + flips]
    own, *away = lax.optimization_barrier(picked)
    return add_up([own] + [lax.ppermute(x, "seq", seq_flip(2 * n)) for x, n in zip(away, flips)])


def reduce_z_last(pair):
    odd = lax.axis_index("seq") // 2 % 2 == 1
    came = lax.ppermute(jnp.where(odd, pair[0], pair[1]).astype(BF), "seq", seq_flip(1))
    return add_up([jnp.where(odd, pair[1], pair[0]), came])


def gather_x(own):
    came = {d: along_x(own, d) for d in (2, 1, 3)}
    place = lax.axis_index("dp")
    quarters = [lax.select_n((place - n) % NX, own, came[1], came[2], came[3]) for n in range(NX)]
    return jnp.concatenate(quarters, axis=1)


def gather_weight_even(out_weight):
    place = lax.axis_index("dp")
    own = lax.select_n(place, *[out_weight[:, QUARTER * n : QUARTER * n + QUARTER] for n in range(NX)])
    came = [lax.ppermute(own, "seq", seq_flip(n)) for n in (4, 2, 6)]
    return jnp.stack([own, came[1], came[0], came[2]])


def gather_weight_z(even, odd):
    at = lax.axis_index("seq") // 2 % NZ
    both = jnp.stack([even, odd], axis=1).reshape(NZ, STRIP, QUARTER)
    for bit in (1, 2, 4):
        halves = both.reshape(NZ // (2 * bit), 2, bit, STRIP, QUARTER)
        both = jnp.where(at & bit != 0, halves[:, ::-1], halves).reshape(NZ, STRIP, QUARTER)
    return both.reshape(NZ * STRIP, QUARTER)


def gather_weight_y(own):
    came = {d: lax.ppermute(own, "seq", seq_shift(NY - d, 0, 0)) for d in (1, 3, 2)}
    return jnp.concatenate([own, came[1], came[2], came[3]], axis=0)


def swap_cores(x):
    return lax.ppermute(x, "seq", seq_shift(0, 0, 1))


def exchange(message):
    return lax.all_to_all(message, "seq", split_axis=0, concat_axis=0, tiled=True)


def local(queries, key_field, value_field, out_grad, out_weight, frame_video):
    rank = lax.axis_index("seq")
    at = jnp.stack([rank % 2, lax.axis_index("dp"), rank // (2 * NZ), rank // 2 % NZ]).astype(jnp.int32)
    videos = jnp.concatenate([frame_video, frame_video], axis=1)

    flat = [x.reshape(ROWS, WIDTH) for x in (queries, key_field, value_field, out_grad)]
    message, even = lax.optimization_barrier((pack_call((0, 1), flat), gather_weight_even(out_weight)))
    message, even, odd = lax.optimization_barrier(
        (pack_call((2,), flat, message), even, lax.ppermute(even, "seq", seq_flip(1)))
    )
    own = gather_weight_y(gather_weight_z(even, odd))
    mid = HALF // 2
    left, right = along_x(own, 1), along_x(own, -1)
    pieces = [own, left, right, along_x(left[:mid], 1), along_x(right[mid:], -1)]
    weights = pieces + [swap_cores(piece) for piece in pieces]
    arrived, at, videos, weights = lax.optimization_barrier((exchange(message), at, videos, weights))
    message, bundle = middle_call(at, videos, arrived, weights)
    parts = weight_call(at, bundle, swap_cores(bundle))
    halves = [reduce_x(parts[:NX]), reduce_x(parts[NX:])]
    strips = jnp.concatenate([reduce_y(half) for half in halves], axis=0)
    came, pair = lax.optimization_barrier((exchange(message), reduce_z_pairs(strips)))
    results, strip = lax.optimization_barrier((unpack_call(came), reduce_z_last(pair)))
    weight_grad = gather_x(strip)
    return tuple(x.reshape(queries.shape) for x in results) + (weight_grad,)


def solution(mesh):
    placed = P("dp", "seq", None, None)
    return jax.shard_map(
        local,
        mesh=mesh,
        in_specs=(placed, placed, placed, placed, P("seq", None), P("dp", None)),
        out_specs=(placed, placed, placed, placed, P("seq", None)),
        check_vma=False,
    )
```

```python
import functools

import jax
import jax.numpy as jnp
import numpy as np
from jax import lax
from jax.experimental import pallas as pl
from jax.experimental.pallas import tpu as pltpu
from jax.sharding import PartitionSpec as P

HEAD = 128
HEADS = 12
WIDTH = HEAD * HEADS
HALF = WIDTH // 2
FRAMES = 64
PLACES = 3
ROWS = FRAMES * PLACES
NX, NY, NZ = 4, 4, 8
SEQ = NY * NZ * 2
STRIP = WIDTH // SEQ
QUARTER = WIDTH // NX
BF = jnp.bfloat16
F32 = jnp.float32
FACTOR = HEAD ** (-0.5)
MIB = 1 << 20


def params(mib):
    return pltpu.CompilerParams(vmem_limit_bytes=mib * MIB)


def cost(us):
    return pl.CostEstimate(flops=0, bytes_accessed=int(us * 3.5e6), transcendentals=0)


def dot(a, b, dims=((1,), (0,))):
    return lax.dot_general(a, b, (dims, ((), ())), preferred_element_type=F32)


def swap_matrix(to_blocks):
    a = lax.broadcasted_iota(jnp.int32, (256, 256), 0 if to_blocks else 1)
    b = lax.broadcasted_iota(jnp.int32, (256, 256), 1 if to_blocks else 0)
    return jnp.where(8 * (a % 32) + a // 32 == b, F32(1), F32(0)).astype(BF)


def pack(sources, place, out_ref, after):
    swap = swap_matrix(False)
    for half in range(2):
        rows = slice(FRAMES * place + 32 * half, FRAMES * place + 32 * half + 32)
        for tile in range(1):
            parts = [
                src[rows, HALF * e + 256 * tile : HALF * e + 256 * tile + HALF]
                for src in sources
                for e in range(2)
            ]
            mixed = dot(swap, jnp.concatenate(parts, axis=0))
            out_ref[256 * half : 256 * half + 256, 256 * tile : 256 * tile + HALF] = mixed.astype(BF)
        after(half)


def unpack(in_ref, place, sinks, before):
    swap = swap_matrix(True)
    for half in range(2):
        before(half)
        rows = slice(FRAMES * place + 32 * half, FRAMES * place + 32 * half + 32)
        for tile in range(1):
            at = HALF * place + 256 * tile
            piece = dot(swap, in_ref[256 * half : 256 * half + 256, at : at + HALF]).astype(BF)
            for n in range(8):
                col = HALF * (n % 2) + 256 * tile
                sinks[n // 2][rows, col : col + HALF] = piece[32 * n : 32 * n + 32]


def place_rows(place):
    return pl.ds(FRAMES * place, FRAMES)


def message_copy(staged, message, sems, place, half):
    rows = pl.ds(256 * half, 256)
    return pltpu.make_async_copy(
        staged.at[place, rows], message.at[rows, pl.ds(HALF * place, HALF)], sems.at[2 * place + half]
    )


def message_read(message, held, sems, place, half):
    part = (pl.ds(256 * half, 256), pl.ds(HALF * place, HALF))
    return pltpu.make_async_copy(message.at[part], held.at[part], sems.at[2 * place + half])


PARTS = [(place, half) for place in range(PLACES) for half in range(2)]


def pack_kernel(places, a, b, c, d, *refs):
    message, *held, staged, in_sems, out_sems = refs[-8:]
    arrays = (a, b, c, d)
    came = {
        j: [
            pltpu.make_async_copy(
                src.at[place_rows(j)], dst.at[place_rows(j)], in_sems.at[4 * j + n]
            )
            for n, (src, dst) in enumerate(zip(arrays, held))
        ]
        for j in places
    }
    for j in places:
        for copy in came[j]:
            copy.start()
    for j in places:
        for copy in came[j]:
            copy.wait()
        pack(held, j, staged.at[j], lambda half, j=j: message_copy(staged, message, out_sems, j, half).start())
    for j in places:
        for half in range(2):
            message_copy(staged, message, out_sems, j, half).wait()


def unpack_kernel(message, a, b, c, d, *scratch):
    held, (in_ref, in_sems, sems) = scratch[:4], scratch[4:]
    came = [message_read(message, in_ref, in_sems, *part) for part in PARTS]
    for copy in came:
        copy.start()
    arrays = (a, b, c, d)
    gone = [
        [
            pltpu.make_async_copy(src.at[place_rows(j)], dst.at[place_rows(j)], sems.at[4 * j + n])
            for n, (dst, src) in enumerate(zip(arrays, held))
        ]
        for j in range(PLACES)
    ]
    for j in range(PLACES):
        unpack(in_ref, j, held, lambda half, j=j: came[2 * j + half].wait())
        for copy in gone[j]:
            copy.start()
    for copies in gone:
        for copy in copies:
            copy.wait()


VMEM = pl.BlockSpec(memory_space=pltpu.VMEM)
SMEM = pl.BlockSpec(memory_space=pltpu.SMEM)
ANY = pl.BlockSpec(memory_space=pl.ANY)
DMA = pltpu.SemaphoreType.DMA
rows_shape = jax.ShapeDtypeStruct((ROWS, WIDTH), BF)
message_shape = jax.ShapeDtypeStruct((8 * SEQ, PLACES * HALF), BF)
rows_held = pltpu.VMEM((ROWS, WIDTH), BF)
message_held = pltpu.VMEM((PLACES, 8 * SEQ, HALF), BF)
probs_shape = jax.ShapeDtypeStruct((HEADS // 2 * PLACES, 2 * FRAMES, 2 * FRAMES), F32)


def pack_call(places, arrays, message=None):
    rest = [] if message is None else [message]
    return pl.pallas_call(
        functools.partial(pack_kernel, places),
        in_specs=[ANY] * (4 + len(rest)),
        out_specs=ANY,
        out_shape=message_shape,
        input_output_aliases={4: 0} if rest else {},
        scratch_shapes=[rows_held] * 4
        + [message_held, DMA((4 * PLACES,)), DMA((2 * PLACES,))],
        compiler_params=params(56),
        cost_estimate=cost(3),
        name="pack",
    )(*arrays, *rest)


def unpack_call(message):
    return pl.pallas_call(
        unpack_kernel,
        in_specs=[ANY],
        out_specs=[ANY] * 4,
        out_shape=[rows_shape] * 4,
        scratch_shapes=[rows_held] * 4
        + [pltpu.VMEM(message_shape.shape, BF), DMA((2 * PLACES,)), DMA((4 * PLACES,))],
        compiler_params=params(58),
        cost_estimate=cost(3),
        name="unpack",
    )(message)


def pair(ref, place, n):
    at, rows = 2 * HEAD * n, slice(FRAMES * place, FRAMES * place + FRAMES)
    return jnp.concatenate([ref[rows, at : at + HEAD], ref[rows, at + HEAD : at + 2 * HEAD]], axis=0)


def put_pair(ref, place, n, value):
    at, rows = 2 * HEAD * n, slice(FRAMES * place, FRAMES * place + FRAMES)
    ref[rows, at : at + HEAD] = value[:FRAMES]
    ref[rows, at + HEAD : at + 2 * HEAD] = value[FRAMES:]


def strip_copies(at, copy):
    for side in range(2):
        core = at[0] if side == 0 else 1 - at[0]
        for dy in range(NY):
            for z in range(NZ):
                y = (at[2] + dy) % NY
                there = pl.multiple_of((y * NZ + z) * 2 * STRIP + core * STRIP, 8)
                copy(side, (dy * NZ + z) * STRIP, there)


PIECES = 5


def forward_place(j, allowed, q, k, v, mixed, probs_ref):
    pairs = range(HEADS // 2)
    logits = [dot(pair(k, j, n), pair(q, j, n), ((1,), (1,))) for n in pairs]
    lows = []
    for n in pairs:
        raw = jnp.where(allowed, logits[n] * FACTOR, F32(-1e30))
        shifted = jnp.exp(raw - jnp.max(raw, axis=0, keepdims=True))
        probs = shifted * (1 / jnp.sum(shifted, axis=0, keepdims=True))
        probs_ref[HEADS // 2 * j + n] = probs
        lows.append(probs.astype(BF))
    for n in pairs:
        put_pair(mixed, j, n, dot(lows[n], pair(v, j, n), ((0,), (0,))).astype(BF))


def project(at, bundle, weights, out, mixed_grad, strips, turned):
    def cols(shift, base=0):
        start = (at[1] + shift + NX) % NX * QUARTER + base
        return pl.ds(pl.multiple_of(start, QUARTER), QUARTER)

    totals = [None, None]
    for side in range(2):
        near, left, right, *far = (ref[...] for ref in weights[PIECES * side : PIECES * side + PIECES])
        pieces = (near, left, right, jnp.concatenate(far, axis=0))
        rows = bundle[:, HALF * side : HALF * side + HALF]
        turn = None
        for n, shifts in enumerate(((0, -1), (1, 2))):
            w = jnp.concatenate(pieces[2 * n : 2 * n + 2], axis=1)
            part = dot(rows, w)
            totals[n] = part if side == 0 else totals[n] + part
            g = jnp.concatenate([bundle[:, cols(shift, WIDTH)] for shift in shifts], axis=1)
            term = dot(w, g, ((1,), (1,)))
            turn = term if turn is None else turn + term
            if side == 1:
                total = totals[n].astype(BF)
                out[:, cols(shifts[0])] = total[:, :QUARTER]
                out[:, cols(shifts[1])] = total[:, QUARTER:]
        strips[side] = turn

    def copy(side, here, there):
        turned[pl.ds(there, STRIP), :] = strips[side, here : here + STRIP, :]

    strip_copies(at, copy)
    mixed_grad[...] = turned[...].T.astype(BF)


def backward_place(j, q, k, v, mixed_grad, probs_ref, q_grad, k_grad, v_grad):
    pairs = range(HEADS // 2)
    grads = [pair(mixed_grad, j, n) for n in pairs]
    through = [dot(pair(v, j, n), grads[n], ((1,), (1,))) for n in pairs]
    scores = []
    for n in pairs:
        probs = probs_ref[HEADS // 2 * j + n]
        probs_low = probs.astype(BF)
        put_pair(v_grad, j, n, dot(probs_low, grads[n]).astype(BF))
        inner = jnp.sum(probs_low.astype(F32) * through[n], axis=0, keepdims=True)
        scores.append((probs * (through[n] - inner)).astype(BF))
    for n in pairs:
        put_pair(k_grad, j, n, (dot(scores[n], pair(q, j, n)) * FACTOR).astype(BF))
        put_pair(q_grad, j, n, (dot(scores[n], pair(k, j, n), ((0,), (0,))) * FACTOR).astype(BF))


def middle_kernel(at, videos, arrived, *refs):
    pieces, (message, bundle_out), scratch = refs[: 2 * PIECES], refs[2 * PIECES : 2 * PIECES + 2], refs[2 * PIECES + 2 :]
    weights, scratch = scratch[: 2 * PIECES], scratch[2 * PIECES :]
    q, k, v, g, mixed, out, mixed_grad, q_grad, k_grad, v_grad = scratch[:10]
    in_ref, probs_ref, bundle, turned, strips, staged, in_sems, piece_sems, bundle_sem, out_sems = scratch[10:]
    parts = [message_read(arrived, in_ref, in_sems, *part) for part in PARTS]
    for copy in parts:
        copy.start()
    came = [
        pltpu.make_async_copy(src, dst, piece_sems.at[n]) for n, (src, dst) in enumerate(zip(pieces, weights))
    ]
    for copy in came:
        copy.start()

    square = (2 * FRAMES, 2 * FRAMES)
    video = jnp.broadcast_to(videos[...], square)
    head = [lax.broadcasted_iota(jnp.int32, square, axis) // FRAMES for axis in range(2)]
    allowed = (video == video.T) & (head[0] == head[1])
    for j in range(PLACES):
        unpack(in_ref, j, (q, k, v, g), lambda half, j=j: parts[2 * j + half].wait())
        forward_place(j, allowed, q, k, v, mixed, probs_ref)

    turned[...] = mixed[...].astype(F32).T

    def take(side, here, there):
        strips[side, here : here + STRIP, :] = turned[pl.ds(there, STRIP), :]

    strip_copies(at, take)
    for side in range(2):
        bundle[:, HALF * side : HALF * side + HALF] = strips[side].T.astype(BF)
    bundle[:, WIDTH:] = g[...]
    gone = pltpu.make_async_copy(bundle, bundle_out, bundle_sem.at[0])
    gone.start()
    for copy in came:
        copy.wait()
    project(at, bundle, weights, out, mixed_grad, strips, turned)
    for j in range(PLACES):
        backward_place(j, q, k, v, mixed_grad, probs_ref, q_grad, k_grad, v_grad)
        sources = (out, q_grad, k_grad, v_grad)
        pack(sources, j, staged.at[j], lambda half, j=j: message_copy(staged, message, out_sems, j, half).start())
    gone.wait()
    for part in PARTS:
        message_copy(staged, message, out_sems, *part).wait()


bundle_shape = jax.ShapeDtypeStruct((ROWS, 2 * WIDTH), BF)


def middle_call(at, videos, message, weights):
    strips_held = [pltpu.VMEM((WIDTH, ROWS), F32), pltpu.VMEM((2, HALF, ROWS), F32)]
    probs_held = pltpu.VMEM((HEADS // 2 * PLACES, 2 * FRAMES, 2 * FRAMES), F32)
    return pl.pallas_call(
        middle_kernel,
        in_specs=[SMEM, VMEM, ANY] + [ANY] * len(weights),
        out_specs=[ANY] * 2,
        out_shape=[message_shape, bundle_shape],
        scratch_shapes=[pltpu.VMEM(w.shape, BF) for w in weights]
        + [rows_held] * 10
        + [pltpu.VMEM(message_shape.shape, BF), probs_held, pltpu.VMEM(bundle_shape.shape, BF)]
        + strips_held
        + [message_held, DMA((2 * PLACES,)), DMA((len(weights),)), DMA((1,)), DMA((2 * PLACES,))],
        compiler_params=params(52),
        cost_estimate=cost(10),
        name="middle",
    )(at, videos, message, *weights)


def weight_kernel(at, bundle, other, *outs):
    size = NZ // 2 * STRIP
    sides = [
        (ref, ref[:, start : start + HALF].astype(F32).T.astype(BF)) for ref, start in ((bundle, 0), (other, HALF))
    ]
    for d in range(0, NX, 2):
        total = None
        for ref, strips in sides:
            cols = [
                ref[:, pl.ds(pl.multiple_of((at[1] + d + i) % NX * QUARTER + WIDTH, QUARTER), QUARTER)]
                for i in range(2)
            ]
            part = dot(strips, jnp.concatenate(cols, axis=1))
            total = part if total is None else total + part
        total = total.astype(BF)
        for i in range(2):
            for half in range(2):
                for dy in range(NY):
                    row = (2 * dy + half) * size
                    piece = total[row : row + size, QUARTER * i : QUARTER * i + QUARTER]
                    outs[NX * half + d + i][size * dy : size * dy + size, :] = piece


def weight_call(at, bundle, other):
    return pl.pallas_call(
        weight_kernel,
        in_specs=[SMEM] + [VMEM] * 2,
        out_specs=[VMEM] * (2 * NX),
        out_shape=[jax.ShapeDtypeStruct((HALF // 2, QUARTER), BF)] * (2 * NX),
        compiler_params=params(12),
        cost_estimate=cost(3),
        name="weight",
    )(at, bundle, other)


def seq_shift(dy, dz, dc):
    seq = np.arange(SEQ).reshape(NY, NZ, 2)
    return [
        (int(seq[y, z, c]), int(seq[(y + dy) % NY, (z + dz) % NZ, c ^ dc]))
        for y in range(NY)
        for z in range(NZ)
        for c in range(2)
    ]


def seq_flip(bit):
    seq = np.arange(SEQ).reshape(NY, NZ, 2)
    return [
        (int(seq[y, z, c]), int(seq[y, z ^ bit, c])) for y in range(NY) for z in range(NZ) for c in range(2)
    ]


def add_up(parts):
    total = parts[0].astype(F32)
    for part in parts[1:]:
        total = total + part.astype(F32)
    return total


def along_x(x, shift):
    return lax.ppermute(x, "dp", [(i, (i + shift) % NX) for i in range(NX)])


def reduce_x(parts):
    return add_up([parts[0]] + [along_x(parts[d], d) for d in (2, 1, 3)]).astype(BF)


def reduce_y(chip):
    chip = chip.reshape(NY, NZ // 2 * STRIP, QUARTER)
    came = [lax.ppermute(chip[d], "seq", seq_shift(d, 0, 0)) for d in (2, 1, 3)]
    return add_up([chip[0]] + came).astype(BF).reshape(NZ // 2, STRIP, QUARTER)


def reduce_z_pairs(strips):
    at = lax.axis_index("seq") // 4 % (NZ // 2)
    pairs = strips.reshape(NZ // 2, 2, STRIP, QUARTER)
    flips = (2, 1, 3)
    picked = [lax.dynamic_index_in_dim(pairs, at ^ n, 0, keepdims=False) for n in (0,) + flips]
    own, *away = lax.optimization_barrier(picked)
    return add_up([own] + [lax.ppermute(x, "seq", seq_flip(2 * n)) for x, n in zip(away, flips)])


def reduce_z_last(pair):
    odd = lax.axis_index("seq") // 2 % 2 == 1
    came = lax.ppermute(jnp.where(odd, pair[0], pair[1]).astype(BF), "seq", seq_flip(1))
    return add_up([jnp.where(odd, pair[1], pair[0]), came])


def gather_x(own):
    came = {d: along_x(own, d) for d in (2, 1, 3)}
    place = lax.axis_index("dp")
    quarters = [lax.select_n((place - n) % NX, own, came[1], came[2], came[3]) for n in range(NX)]
    return jnp.concatenate(quarters, axis=1)


def gather_weight_even(out_weight):
    place = lax.axis_index("dp")
    columns = [out_weight[None, :, QUARTER * n : QUARTER * n + QUARTER] for n in range(NX)]
    own = lax.optimization_barrier(lax.select_n(place, *columns))
    came = [lax.ppermute(own, "seq", seq_flip(n)) for n in (4, 2, 6)]
    return jnp.concatenate([own, came[1], came[0], came[2]], axis=0)


def gather_weight_z(even, odd):
    at = lax.axis_index("seq") // 2 % NZ
    both = jnp.stack([even, odd], axis=1).reshape(NZ, STRIP, QUARTER)
    for bit in (1, 2, 4):
        halves = both.reshape(NZ // (2 * bit), 2, bit, STRIP, QUARTER)
        both = jnp.where(at & bit != 0, halves[:, ::-1], halves).reshape(NZ, STRIP, QUARTER)
    return both.reshape(NZ * STRIP, QUARTER)


def gather_weight_y(own):
    came = {d: lax.ppermute(own, "seq", seq_shift(NY - d, 0, 0)) for d in (1, 3, 2)}
    return jnp.concatenate([own, came[1], came[2], came[3]], axis=0)


def swap_cores(x):
    return lax.ppermute(x, "seq", seq_shift(0, 0, 1))


def exchange(message):
    return lax.all_to_all(message, "seq", split_axis=0, concat_axis=0, tiled=True)


def local(queries, key_field, value_field, out_grad, out_weight, frame_video):
    rank = lax.axis_index("seq")
    at = jnp.stack([rank % 2, lax.axis_index("dp"), rank // (2 * NZ), rank // 2 % NZ]).astype(jnp.int32)
    videos = jnp.concatenate([frame_video, frame_video], axis=1)

    flat = [x.reshape(ROWS, WIDTH) for x in (queries, key_field, value_field, out_grad)]
    message, even = lax.optimization_barrier((pack_call((0,), flat), gather_weight_even(out_weight)))
    message, even, odd = lax.optimization_barrier(
        (pack_call((1, 2), flat, message), even, lax.ppermute(even, "seq", seq_flip(1)))
    )
    own = gather_weight_y(gather_weight_z(even, odd))
    mid = HALF // 2
    left, right = along_x(own, 1), along_x(own, -1)
    pieces = [own, left, right, along_x(left[:mid], 1), along_x(right[mid:], -1)]
    weights = pieces + [swap_cores(piece) for piece in pieces]
    arrived, at, videos, weights = lax.optimization_barrier((exchange(message), at, videos, weights))
    message, bundle = middle_call(at, videos, arrived, weights)
    parts = weight_call(at, bundle, swap_cores(bundle))
    halves = [reduce_x(parts[:NX]), reduce_x(parts[NX:])]
    strips = jnp.concatenate([reduce_y(half) for half in halves], axis=0)
    came, pair = lax.optimization_barrier((exchange(message), reduce_z_pairs(strips)))
    results, strip = lax.optimization_barrier((unpack_call(came), reduce_z_last(pair)))
    weight_grad = gather_x(strip)
    return tuple(x.reshape(queries.shape) for x in results) + (weight_grad,)


def solution(mesh):
    placed = P("dp", "seq", None, None)
    return jax.shard_map(
        local,
        mesh=mesh,
        in_specs=(placed, placed, placed, placed, P("seq", None), P("dp", None)),
        out_specs=(placed, placed, placed, placed, P("seq", None)),
        check_vma=False,
    )
```

```python
import functools

import jax
import jax.numpy as jnp
import numpy as np
from jax import lax
from jax.experimental import pallas as pl
from jax.experimental.pallas import tpu as pltpu
from jax.sharding import PartitionSpec as P

HEAD = 128
HEADS = 12
WIDTH = HEAD * HEADS
HALF = WIDTH // 2
FRAMES = 64
PLACES = 3
ROWS = FRAMES * PLACES
NX, NY, NZ = 4, 4, 8
SEQ = NY * NZ * 2
STRIP = WIDTH // SEQ
QUARTER = WIDTH // NX
BF = jnp.bfloat16
F32 = jnp.float32
FACTOR = HEAD ** (-0.5)
MIB = 1 << 20


def params(mib):
    return pltpu.CompilerParams(vmem_limit_bytes=mib * MIB)


def cost(us):
    return pl.CostEstimate(flops=0, bytes_accessed=int(us * 3.5e6), transcendentals=0)


def dot(a, b, dims=((1,), (0,))):
    return lax.dot_general(a, b, (dims, ((), ())), preferred_element_type=F32)


def swap_matrix(to_blocks):
    a = lax.broadcasted_iota(jnp.int32, (256, 256), 0 if to_blocks else 1)
    b = lax.broadcasted_iota(jnp.int32, (256, 256), 1 if to_blocks else 0)
    return jnp.where(8 * (a % 32) + a // 32 == b, F32(1), F32(0)).astype(BF)


def pack(sources, place, out_ref):
    swap = swap_matrix(False)
    for half in range(2):
        rows = slice(FRAMES * place + 32 * half, FRAMES * place + 32 * half + 32)
        for tile in range(1):
            parts = [
                src[rows, HALF * e + 256 * tile : HALF * e + 256 * tile + HALF]
                for src in sources
                for e in range(2)
            ]
            mixed = dot(swap, jnp.concatenate(parts, axis=0))
            out_ref[256 * half : 256 * half + 256, 256 * tile : 256 * tile + HALF] = mixed.astype(BF)


def unpack(in_ref, place, sinks):
    swap = swap_matrix(True)
    for half in range(2):
        rows = slice(FRAMES * place + 32 * half, FRAMES * place + 32 * half + 32)
        for tile in range(1):
            at = HALF * place + 256 * tile
            piece = dot(swap, in_ref[256 * half : 256 * half + 256, at : at + HALF]).astype(BF)
            for n in range(8):
                col = HALF * (n % 2) + 256 * tile
                sinks[n // 2][rows, col : col + HALF] = piece[32 * n : 32 * n + 32]


def place_rows(place):
    return pl.ds(FRAMES * place, FRAMES)


def message_copy(staged, message, sems, place):
    return pltpu.make_async_copy(
        staged.at[place], message.at[:, pl.ds(HALF * place, HALF)], sems.at[place]
    )


def pack_kernel(places, a, b, c, d, *refs):
    message, *held, staged, in_sems, out_sems = refs[-8:]
    arrays = (a, b, c, d)
    came = {
        j: [
            pltpu.make_async_copy(
                src.at[place_rows(j)], dst.at[place_rows(j)], in_sems.at[4 * j + n]
            )
            for n, (src, dst) in enumerate(zip(arrays, held))
        ]
        for j in places
    }
    for j in places:
        for copy in came[j]:
            copy.start()
    for j in places:
        for copy in came[j]:
            copy.wait()
        pack(held, j, staged.at[j])
        message_copy(staged, message, out_sems, j).start()
    for j in places:
        message_copy(staged, message, out_sems, j).wait()


def unpack_kernel(message, a, b, c, d, *scratch):
    held, (in_ref, in_sems, sems) = scratch[:4], scratch[4:]
    came = []
    for j in range(PLACES):
        cols = pl.ds(HALF * j, HALF)
        came.append(pltpu.make_async_copy(message.at[:, cols], in_ref.at[:, cols], in_sems.at[j]))
        came[j].start()
    arrays = (a, b, c, d)
    gone = [
        [
            pltpu.make_async_copy(src.at[place_rows(j)], dst.at[place_rows(j)], sems.at[4 * j + n])
            for n, (dst, src) in enumerate(zip(arrays, held))
        ]
        for j in range(PLACES)
    ]
    for j in range(PLACES):
        came[j].wait()
        unpack(in_ref, j, held)
        for copy in gone[j]:
            copy.start()
    for copies in gone:
        for copy in copies:
            copy.wait()


VMEM = pl.BlockSpec(memory_space=pltpu.VMEM)
SMEM = pl.BlockSpec(memory_space=pltpu.SMEM)
ANY = pl.BlockSpec(memory_space=pl.ANY)
DMA = pltpu.SemaphoreType.DMA
rows_shape = jax.ShapeDtypeStruct((ROWS, WIDTH), BF)
message_shape = jax.ShapeDtypeStruct((8 * SEQ, PLACES * HALF), BF)
rows_held = pltpu.VMEM((ROWS, WIDTH), BF)
message_held = pltpu.VMEM((PLACES, 8 * SEQ, HALF), BF)
probs_shape = jax.ShapeDtypeStruct((HEADS // 2 * PLACES, 2 * FRAMES, 2 * FRAMES), F32)


def pack_call(places, arrays, message=None):
    rest = [] if message is None else [message]
    return pl.pallas_call(
        functools.partial(pack_kernel, places),
        in_specs=[ANY] * (4 + len(rest)),
        out_specs=ANY,
        out_shape=message_shape,
        input_output_aliases={4: 0} if rest else {},
        scratch_shapes=[rows_held] * 4
        + [message_held, DMA((4 * PLACES,)), DMA((PLACES,))],
        compiler_params=params(56),
        cost_estimate=cost(3),
        name="pack",
    )(*arrays, *rest)


def unpack_call(message):
    return pl.pallas_call(
        unpack_kernel,
        in_specs=[ANY],
        out_specs=[ANY] * 4,
        out_shape=[rows_shape] * 4,
        scratch_shapes=[rows_held] * 4
        + [pltpu.VMEM(message_shape.shape, BF), DMA((PLACES,)), DMA((4 * PLACES,))],
        compiler_params=params(58),
        cost_estimate=cost(3),
        name="unpack",
    )(message)


def pair(ref, place, n):
    at, rows = 2 * HEAD * n, slice(FRAMES * place, FRAMES * place + FRAMES)
    return jnp.concatenate([ref[rows, at : at + HEAD], ref[rows, at + HEAD : at + 2 * HEAD]], axis=0)


def put_pair(ref, place, n, value):
    at, rows = 2 * HEAD * n, slice(FRAMES * place, FRAMES * place + FRAMES)
    ref[rows, at : at + HEAD] = value[:FRAMES]
    ref[rows, at + HEAD : at + 2 * HEAD] = value[FRAMES:]


def strip_copies(at, copy):
    for side in range(2):
        core = at[0] if side == 0 else 1 - at[0]
        for dy in range(NY):
            for z in range(NZ):
                y = (at[2] + dy) % NY
                there = pl.multiple_of((y * NZ + z) * 2 * STRIP + core * STRIP, 8)
                copy(side, (dy * NZ + z) * STRIP, there)


PIECES = 5


def forward_place(j, allowed, q, k, v, mixed, probs_ref):
    pairs = range(HEADS // 2)
    logits = [dot(pair(k, j, n), pair(q, j, n), ((1,), (1,))) for n in pairs]
    lows = []
    for n in pairs:
        raw = jnp.where(allowed, logits[n] * FACTOR, F32(-1e30))
        shifted = jnp.exp(raw - jnp.max(raw, axis=0, keepdims=True))
        probs = shifted * (1 / jnp.sum(shifted, axis=0, keepdims=True))
        probs_ref[HEADS // 2 * j + n] = probs
        lows.append(probs.astype(BF))
    for n in pairs:
        put_pair(mixed, j, n, dot(lows[n], pair(v, j, n), ((0,), (0,))).astype(BF))


def project(at, bundle, weights, out, mixed_grad, strips, turned):
    def cols(shift, base=0):
        start = (at[1] + shift + NX) % NX * QUARTER + base
        return pl.ds(pl.multiple_of(start, QUARTER), QUARTER)

    totals = [None, None]
    for side in range(2):
        near, left, right, *far = (ref[...] for ref in weights[PIECES * side : PIECES * side + PIECES])
        pieces = (near, left, right, jnp.concatenate(far, axis=0))
        rows = bundle[:, HALF * side : HALF * side + HALF]
        turn = None
        for n, shifts in enumerate(((0, -1), (1, 2))):
            w = jnp.concatenate(pieces[2 * n : 2 * n + 2], axis=1)
            part = dot(rows, w)
            totals[n] = part if side == 0 else totals[n] + part
            g = jnp.concatenate([bundle[:, cols(shift, WIDTH)] for shift in shifts], axis=1)
            term = dot(w, g, ((1,), (1,)))
            turn = term if turn is None else turn + term
            if side == 1:
                total = totals[n].astype(BF)
                out[:, cols(shifts[0])] = total[:, :QUARTER]
                out[:, cols(shifts[1])] = total[:, QUARTER:]
        strips[side] = turn

    def copy(side, here, there):
        turned[pl.ds(there, STRIP), :] = strips[side, here : here + STRIP, :]

    strip_copies(at, copy)
    mixed_grad[...] = turned[...].T.astype(BF)


def backward_place(j, q, k, v, mixed_grad, probs_ref, q_grad, k_grad, v_grad):
    pairs = range(HEADS // 2)
    grads = [pair(mixed_grad, j, n) for n in pairs]
    through = [dot(pair(v, j, n), grads[n], ((1,), (1,))) for n in pairs]
    scores = []
    for n in pairs:
        probs = probs_ref[HEADS // 2 * j + n]
        probs_low = probs.astype(BF)
        put_pair(v_grad, j, n, dot(probs_low, grads[n]).astype(BF))
        inner = jnp.sum(probs_low.astype(F32) * through[n], axis=0, keepdims=True)
        scores.append((probs * (through[n] - inner)).astype(BF))
    for n in pairs:
        put_pair(k_grad, j, n, (dot(scores[n], pair(q, j, n)) * FACTOR).astype(BF))
        put_pair(q_grad, j, n, (dot(scores[n], pair(k, j, n), ((0,), (0,))) * FACTOR).astype(BF))


def middle_kernel(at, videos, arrived, *refs):
    pieces, (message, bundle_out), scratch = refs[: 2 * PIECES], refs[2 * PIECES : 2 * PIECES + 2], refs[2 * PIECES + 2 :]
    weights, scratch = scratch[: 2 * PIECES], scratch[2 * PIECES :]
    q, k, v, g, mixed, out, mixed_grad, q_grad, k_grad, v_grad = scratch[:10]
    in_ref, probs_ref, bundle, turned, strips, staged, in_sems, piece_sems, bundle_sem, out_sems = scratch[10:]
    parts = []
    for j in range(PLACES):
        cols = pl.ds(HALF * j, HALF)
        parts.append(pltpu.make_async_copy(arrived.at[:, cols], in_ref.at[:, cols], in_sems.at[j]))
        parts[j].start()
    came = [
        pltpu.make_async_copy(src, dst, piece_sems.at[n]) for n, (src, dst) in enumerate(zip(pieces, weights))
    ]
    for copy in came:
        copy.start()

    square = (2 * FRAMES, 2 * FRAMES)
    video = jnp.broadcast_to(videos[...], square)
    head = [lax.broadcasted_iota(jnp.int32, square, axis) // FRAMES for axis in range(2)]
    allowed = (video == video.T) & (head[0] == head[1])
    for j in range(PLACES):
        parts[j].wait()
        unpack(in_ref, j, (q, k, v, g))
        forward_place(j, allowed, q, k, v, mixed, probs_ref)

    turned[...] = mixed[...].astype(F32).T

    def take(side, here, there):
        strips[side, here : here + STRIP, :] = turned[pl.ds(there, STRIP), :]

    strip_copies(at, take)
    for side in range(2):
        bundle[:, HALF * side : HALF * side + HALF] = strips[side].T.astype(BF)
    bundle[:, WIDTH:] = g[...]
    gone = pltpu.make_async_copy(bundle, bundle_out, bundle_sem.at[0])
    gone.start()
    for copy in came:
        copy.wait()
    project(at, bundle, weights, out, mixed_grad, strips, turned)
    for j in range(PLACES):
        backward_place(j, q, k, v, mixed_grad, probs_ref, q_grad, k_grad, v_grad)
        pack((out, q_grad, k_grad, v_grad), j, staged.at[j])
        message_copy(staged, message, out_sems, j).start()
    gone.wait()
    for j in range(PLACES):
        message_copy(staged, message, out_sems, j).wait()


bundle_shape = jax.ShapeDtypeStruct((ROWS, 2 * WIDTH), BF)


def middle_call(at, videos, message, weights):
    strips_held = [pltpu.VMEM((WIDTH, ROWS), F32), pltpu.VMEM((2, HALF, ROWS), F32)]
    probs_held = pltpu.VMEM((HEADS // 2 * PLACES, 2 * FRAMES, 2 * FRAMES), F32)
    return pl.pallas_call(
        middle_kernel,
        in_specs=[SMEM, VMEM, ANY] + [ANY] * len(weights),
        out_specs=[ANY] * 2,
        out_shape=[message_shape, bundle_shape],
        scratch_shapes=[pltpu.VMEM(w.shape, BF) for w in weights]
        + [rows_held] * 10
        + [pltpu.VMEM(message_shape.shape, BF), probs_held, pltpu.VMEM(bundle_shape.shape, BF)]
        + strips_held
        + [message_held, DMA((PLACES,)), DMA((len(weights),)), DMA((1,)), DMA((PLACES,))],
        compiler_params=params(52),
        cost_estimate=cost(10),
        name="middle",
    )(at, videos, message, *weights)


def weight_kernel(at, bundle, other, *outs):
    size = NZ // 2 * STRIP
    sides = [
        (ref, ref[:, start : start + HALF].astype(F32).T.astype(BF)) for ref, start in ((bundle, 0), (other, HALF))
    ]
    for d in range(0, NX, 2):
        total = None
        for ref, strips in sides:
            cols = [
                ref[:, pl.ds(pl.multiple_of((at[1] + d + i) % NX * QUARTER + WIDTH, QUARTER), QUARTER)]
                for i in range(2)
            ]
            part = dot(strips, jnp.concatenate(cols, axis=1))
            total = part if total is None else total + part
        total = total.astype(BF)
        for i in range(2):
            for half in range(2):
                for dy in range(NY):
                    row = (2 * dy + half) * size
                    piece = total[row : row + size, QUARTER * i : QUARTER * i + QUARTER]
                    outs[NX * half + d + i][size * dy : size * dy + size, :] = piece


def weight_call(at, bundle, other):
    return pl.pallas_call(
        weight_kernel,
        in_specs=[SMEM] + [VMEM] * 2,
        out_specs=[VMEM] * (2 * NX),
        out_shape=[jax.ShapeDtypeStruct((HALF // 2, QUARTER), BF)] * (2 * NX),
        compiler_params=params(12),
        cost_estimate=cost(3),
        name="weight",
    )(at, bundle, other)


def seq_shift(dy, dz, dc):
    seq = np.arange(SEQ).reshape(NY, NZ, 2)
    return [
        (int(seq[y, z, c]), int(seq[(y + dy) % NY, (z + dz) % NZ, c ^ dc]))
        for y in range(NY)
        for z in range(NZ)
        for c in range(2)
    ]


def seq_flip(bit):
    seq = np.arange(SEQ).reshape(NY, NZ, 2)
    return [
        (int(seq[y, z, c]), int(seq[y, z ^ bit, c])) for y in range(NY) for z in range(NZ) for c in range(2)
    ]


def add_up(parts):
    total = parts[0].astype(F32)
    for part in parts[1:]:
        total = total + part.astype(F32)
    return total


def along_x(x, shift):
    return lax.ppermute(x, "dp", [(i, (i + shift) % NX) for i in range(NX)])


def reduce_x(parts):
    return add_up([parts[0]] + [along_x(parts[d], d) for d in (2, 1, 3)]).astype(BF)


def reduce_y(chip):
    chip = chip.reshape(NY, NZ // 2 * STRIP, QUARTER)
    came = [lax.ppermute(chip[d], "seq", seq_shift(d, 0, 0)) for d in (2, 1, 3)]
    return add_up([chip[0]] + came).astype(BF).reshape(NZ // 2, STRIP, QUARTER)


def reduce_z_pairs(strips):
    at = lax.axis_index("seq") // 4 % (NZ // 2)
    pairs = strips.reshape(NZ // 2, 2, STRIP, QUARTER)
    flips = (2, 1, 3)
    picked = [lax.dynamic_index_in_dim(pairs, at ^ n, 0, keepdims=False) for n in (0,) + flips]
    own, *away = lax.optimization_barrier(picked)
    return add_up([own] + [lax.ppermute(x, "seq", seq_flip(2 * n)) for x, n in zip(away, flips)])


def reduce_z_last(pair):
    odd = lax.axis_index("seq") // 2 % 2 == 1
    came = lax.ppermute(jnp.where(odd, pair[0], pair[1]).astype(BF), "seq", seq_flip(1))
    return add_up([jnp.where(odd, pair[1], pair[0]), came])


def gather_x(own):
    came = {d: along_x(own, d) for d in (2, 1, 3)}
    place = lax.axis_index("dp")
    quarters = [lax.select_n((place - n) % NX, own, came[1], came[2], came[3]) for n in range(NX)]
    return jnp.concatenate(quarters, axis=1)


def gather_weight_even(out_weight):
    place = lax.axis_index("dp")
    columns = [out_weight[None, :, QUARTER * n : QUARTER * n + QUARTER] for n in range(NX)]
    own = lax.optimization_barrier(lax.select_n(place, *columns))
    came = [lax.ppermute(own, "seq", seq_flip(n)) for n in (4, 2, 6)]
    return jnp.concatenate([own, came[1], came[0], came[2]], axis=0)


def gather_weight_z(even, odd):
    at = lax.axis_index("seq") // 2 % NZ
    both = jnp.stack([even, odd], axis=1).reshape(NZ, STRIP, QUARTER)
    for bit in (1, 2, 4):
        halves = both.reshape(NZ // (2 * bit), 2, bit, STRIP, QUARTER)
        both = jnp.where(at & bit != 0, halves[:, ::-1], halves).reshape(NZ, STRIP, QUARTER)
    return both.reshape(NZ * STRIP, QUARTER)


def gather_weight_y(own):
    came = {d: lax.ppermute(own, "seq", seq_shift(NY - d, 0, 0)) for d in (1, 3, 2)}
    return jnp.concatenate([own, came[1], came[2], came[3]], axis=0)


def swap_cores(x):
    return lax.ppermute(x, "seq", seq_shift(0, 0, 1))


def exchange(message):
    return lax.all_to_all(message, "seq", split_axis=0, concat_axis=0, tiled=True)


def local(queries, key_field, value_field, out_grad, out_weight, frame_video):
    rank = lax.axis_index("seq")
    at = jnp.stack([rank % 2, lax.axis_index("dp"), rank // (2 * NZ), rank // 2 % NZ]).astype(jnp.int32)
    videos = jnp.concatenate([frame_video, frame_video], axis=1)

    flat = [x.reshape(ROWS, WIDTH) for x in (queries, key_field, value_field, out_grad)]
    message, even = lax.optimization_barrier((pack_call((0,), flat), gather_weight_even(out_weight)))
    message, even, odd = lax.optimization_barrier(
        (pack_call((1, 2), flat, message), even, lax.ppermute(even, "seq", seq_flip(1)))
    )
    own = gather_weight_y(gather_weight_z(even, odd))
    mid = HALF // 2
    left, right = along_x(own, 1), along_x(own, -1)
    pieces = [own, left, right, along_x(left[:mid], 1), along_x(right[mid:], -1)]
    weights = pieces + [swap_cores(piece) for piece in pieces]
    arrived, at, videos, weights = lax.optimization_barrier((exchange(message), at, videos, weights))
    message, bundle = middle_call(at, videos, arrived, weights)
    parts = weight_call(at, bundle, swap_cores(bundle))
    halves = [reduce_x(parts[:NX]), reduce_x(parts[NX:])]
    strips = jnp.concatenate([reduce_y(half) for half in halves], axis=0)
    came, pair = lax.optimization_barrier((exchange(message), reduce_z_pairs(strips)))
    results, strip = lax.optimization_barrier((unpack_call(came), reduce_z_last(pair)))
    weight_grad = gather_x(strip)
    return tuple(x.reshape(queries.shape) for x in results) + (weight_grad,)


def solution(mesh):
    placed = P("dp", "seq", None, None)
    return jax.shard_map(
        local,
        mesh=mesh,
        in_specs=(placed, placed, placed, placed, P("seq", None), P("dp", None)),
        out_specs=(placed, placed, placed, placed, P("seq", None)),
        check_vma=False,
    )
```
